32 devices in a mesh: section: 2 (over y), tensor: 4 (over x, core), dp: 4 (over z).
Axes of the slice: x: 2, y: 2, z: 4, core: 2. Of those that a mesh axis runs over, the one named last changes fastest.
Arguments:
- block_input: bfloat16 [8, 256, 768], P('dp', 'tensor'), may hold values from -6 to 6
- segments: int32 [8, 256], P('dp'), may hold values from 0 to 2, as said below
- out_grad: bfloat16 [8, 256, 768], P('dp', 'tensor'), may hold values from -6 to 6
- query_key_value_weight: bfloat16 [2, 768, 3, 768], P('section', None, None, 'tensor'), may hold values from -0.21875 to 0.21875
- b_qv: bfloat16 [2, 2, 768], P('section', None, 'tensor'), may hold values from -3 to 3
- attention_output_weight: bfloat16 [2, 768, 768], P('section', 'tensor'), may hold values from -0.625 to 0.625
- attention_out_bias: bfloat16 [2, 768], P('section'), may hold values from -2 to 2
- ln_gain: bfloat16 [2, 2, 768], P('section'), may hold values from 0.5 to 1.5
- ln_bias: bfloat16 [2, 2, 768], P('section'), may hold values from -2 to 2
- up_projection_weight: bfloat16 [2, 768, 3072], P('section', None, 'tensor'), may hold values from -0.21875 to 0.21875
- up_proj_bias: bfloat16 [2, 3072], P('section', 'tensor'), may hold values from -3 to 3
- down_projection_weight: bfloat16 [2, 3072, 768], P('section', 'tensor'), may hold values from -0.15625 to 0.15625
- down_proj_bias: bfloat16 [2, 768], P('section'), may hold values from -2 to 2
Outputs:
- layer_outputs: bfloat16 [2, 8, 256, 768], P('section', 'dp', 'tensor')
- input_grads: bfloat16 [2, 8, 256, 768], P('section', 'dp', 'tensor')
- grad_w_qkv: float32 [2, 768, 3, 768], P('section', None, None, 'tensor')
- grad_b_qv: float32 [2, 2, 768], P('section', None, 'tensor')
- grad_w_out: float32 [2, 768, 768], P('section', 'tensor')
- grad_b_out: float32 [2, 768], P('section')
- grad_ln_gain: float32 [2, 2, 768], P('section')
- grad_ln_bias: float32 [2, 2, 768], P('section')
- grad_w_up: float32 [2, 768, 3072], P('section', None, 'tensor')
- grad_b_up: float32 [2, 3072], P('section', 'tensor')
- grad_w_down: float32 [2, 3072, 768], P('section', 'tensor')
- grad_b_down: float32 [2, 768], P('section')
The draws below stay inside these ranges and needn't reach their ends.
Inputs may be any that keep to these rules, and one draw needn't show every extreme that they name: `segments`: along each sequence the document numbers never fall; document 1 begins at a position below 64 and ends at or after position 192; documents 0 and 2 are the pieces before and after it.
All inputs are finite; a program needn't handle non-finite values.
Results may differ from the reference program's by a relative error of at most 0.022.
Values may be sent and summed in bfloat16 or wider, within the bound.
No kernel may reach another device: no remote copies, remote signals or barrier semaphores. Data moves between devices by JAX's collectives and lax.ppermute only.
A program may use at most 128 MiB of HBM per device.

```python
import jax
import jax.numpy as jnp
from jax import lax

D = 768
H = 12
HEAD_DIM = 64
FF = 3072
L = 256
SEQS = 8


def draw_segments(key, part):
    key = jax.random.fold_in(key, 7)
    key_start, key_end = jax.random.split(key)
    start = jax.random.randint(key_start, (SEQS, 1), 1, L // 4)
    finish = jax.random.randint(key_end, (SEQS, 1), 3 * L // 4 + 1, L)
    places = jnp.arange(L, dtype=jnp.int32)[None, :]
    return (places >= start).astype(jnp.int32) + (places >= finish).astype(jnp.int32)


def shard_levels(stream_key, dims, cuts, smallest, largest):
    def one(position, shards_of):
        draws = jax.random.uniform(jax.random.fold_in(jax.random.fold_in(stream_key, 6), position), (shards_of,), jnp.float32, smallest / len(cuts), largest / len(cuts))
        return jnp.repeat(jnp.exp(draws), dims[position] // shards_of).reshape((-1,) + (1,) * (len(dims) - position - 1))

    factor_of = one(*cuts[0])
    for cut in cuts[1:]:
        factor_of = factor_of * one(*cut)
    return factor_of


def bell_draw(key, extent, deviation, bound, cuts=(), held_as=jnp.bfloat16):
    values = jax.random.normal(key, extent, jnp.float32) * deviation
    if len(cuts) > 0:
        values = shard_levels(key, extent, cuts, -0.22, 0.18) * values
    return jnp.clip(values, min=-bound, max=bound).astype(held_as)


def setup_inputs(seed: int = 0) -> dict:
    seeds = jax.random.split(jax.random.key(seed), 14)
    block_input = bell_draw(seeds[0], (SEQS, L, D), 1.0, 6.0, ((0, 4), (1, 4)))
    segments = draw_segments(jax.random.fold_in(seeds[13], 71), 0)
    out_grad = bell_draw(seeds[2], (SEQS, L, D), 1.0, 6.0, ((0, 4), (1, 4)))
    query_key_value_weight = bell_draw(seeds[3], (2, D, 3, D), D ** -0.5, 0.21875, ((0, 2), (3, 4)))
    b_qv = bell_draw(seeds[4], (2, 2, D), 0.5, 3.0, ((0, 2), (2, 4)))
    attention_output_weight = bell_draw(seeds[5], (2, D, D), (D // 8) ** -0.5, 0.625, ((0, 2), (1, 4)))
    attention_out_bias = bell_draw(seeds[6], (2, D), 0.3, 2.0, ((0, 2),))
    ln_gain = jnp.clip(1.0 + 0.1 * jax.random.normal(seeds[7], (2, 2, D), jnp.float32), 0.5, 1.5).astype(jnp.bfloat16)
    ln_bias = bell_draw(seeds[8], (2, 2, D), 0.3, 2.0, ((0, 2),))
    up_projection_weight = bell_draw(seeds[9], (2, D, FF), D ** -0.5, 0.21875, ((0, 2), (2, 4)))
    up_proj_bias = bell_draw(seeds[10], (2, FF), 0.5, 3.0, ((0, 2), (1, 4)))
    down_projection_weight = bell_draw(seeds[11], (2, FF, D), (FF // 2) ** -0.5, 0.15625, ((0, 2), (1, 4)))
    down_proj_bias = bell_draw(seeds[12], (2, D), 0.3, 2.0, ((0, 2),))
    return {"block_input": block_input, "segments": segments, "out_grad": out_grad, "query_key_value_weight": query_key_value_weight, "b_qv": b_qv, "attention_output_weight": attention_output_weight, "attention_out_bias": attention_out_bias, "ln_gain": ln_gain, "ln_bias": ln_bias, "up_projection_weight": up_projection_weight, "up_proj_bias": up_proj_bias, "down_projection_weight": down_projection_weight, "down_proj_bias": down_proj_bias}


EPSILON = 1e-06
HIGH_ACCURACY = lax.Precision.HIGHEST

@jax.custom_vjp
def low(v):
    return lax.optimization_barrier(v.astype(jnp.bfloat16)).astype(jnp.float32)

@jax.custom_vjp
def low_back(v):
    return v

def low_keep(v):
    return (low(v), None)

def low_pass(kept, grad):
    return (grad,)

def back_keep(v):
    return (v, None)

def back_low(kept, grad):
    return (low(grad),)
low.defvjp(low_keep, low_pass)
low_back.defvjp(back_keep, back_low)

def normalize(values, gain, shift):
    centred = values - lax.optimization_barrier(jnp.mean(values, -1, keepdims=True))
    spread = lax.optimization_barrier(jnp.mean(centred * centred, -1, keepdims=True))
    return centred * lax.rsqrt(spread + EPSILON) * gain + shift

def attend(query, key_rows, value, seg_rows):
    scores = low_back(jnp.einsum('sqhe,skhe->shqk', query, key_rows, precision=HIGH_ACCURACY) * HEAD_DIM ** (-0.5))
    same = (seg_rows[:, :, None] == seg_rows[:, None, :])[:, None]
    scores = jnp.where(same, scores, -1e+30)
    peak = lax.optimization_barrier(jnp.max(scores, -1, keepdims=True))
    weights = jnp.exp(scores - peak)
    probs = low(weights / lax.optimization_barrier(jnp.sum(weights, -1, keepdims=True)))
    return jnp.einsum('shqk,skhe->sqhe', probs, value, precision=HIGH_ACCURACY)

def layer(inputs, query_key_value_weight, b_qv, attention_output_weight, attention_out_bias, gain, shift, up_projection_weight, up_proj_bias, down_projection_weight, down_proj_bias, seg_rows):
    layer_entry = low_back(inputs)
    count = inputs.shape[0]
    length = inputs.shape[1]
    heads_shape = (count, length, H, HEAD_DIM)
    projected = jnp.einsum('qhj,jpv->qhpv', low(layer_entry), query_key_value_weight, precision=HIGH_ACCURACY)
    query = low(low_back(projected[:, :, 0] + b_qv[0])).reshape(heads_shape)
    key_rows = low(low_back(projected[:, :, 1])).reshape(heads_shape)
    value = low(low_back(projected[:, :, 2] + b_qv[1])).reshape(heads_shape)
    mixed_heads = low(low_back(attend(query, key_rows, value, seg_rows).reshape(count, length, D)))
    branch_output = low_back(jnp.einsum('hmy,yv->hmv', mixed_heads, attention_output_weight, precision=HIGH_ACCURACY) + attention_out_bias)
    first_layer = normalize(layer_entry + branch_output, gain[0], shift[0])
    hidden_units = low_back(jnp.einsum('xjg,gq->xjq', low(first_layer), up_projection_weight, precision=HIGH_ACCURACY) + up_proj_bias)
    activation_values = low(jax.nn.gelu(hidden_units, approximate=False))
    second_layer = low_back(jnp.einsum('bxz,zp->bxp', activation_values, down_projection_weight, precision=HIGH_ACCURACY) + down_proj_bias)
    return low(normalize(first_layer + second_layer, gain[1], shift[1]))

def widen(array):
    return array.astype(jnp.float32)

def reference(block_input, segments, out_grad, query_key_value_weight, b_qv, attention_output_weight, attention_out_bias, ln_gain, ln_bias, up_projection_weight, up_proj_bias, down_projection_weight, down_proj_bias):
    stacks = (query_key_value_weight, b_qv, attention_output_weight, attention_out_bias, ln_gain, ln_bias, up_projection_weight, up_proj_bias, down_projection_weight, down_proj_bias)
    params_first = tuple((widen(item[0]) for item in stacks))
    params_second = tuple((widen(item[1]) for item in stacks))
    group = 8
    blocks = SEQS // group
    inputs = widen(block_input).reshape(blocks, group, L, D)
    cotangents = widen(out_grad).reshape(blocks, group, L, D)
    seg_blocks = segments.reshape(blocks, group, L)
    zero_first = jax.tree.map(jnp.zeros_like, params_first)
    zero_second = jax.tree.map(jnp.zeros_like, params_second)

    def step(totals, pieces):
        rows_in, seg_rows, cot_rows = pieces

        def run_layer(values, *weights):
            return layer(values, *weights, seg_rows)
        middle, pull_first = jax.vjp(run_layer, rows_in, *params_first)
        final, pull_second = jax.vjp(run_layer, middle, *params_second)
        back_second = pull_second(cot_rows)
        back_first = pull_first(back_second[0])
        new_first = jax.tree.map(jnp.add, totals[0], tuple(back_first[1:]))
        new_second = jax.tree.map(jnp.add, totals[1], tuple(back_second[1:]))
        return ((new_first, new_second), (middle, final, back_first[0], back_second[0]))
    totals, results = lax.scan(step, (zero_first, zero_second), (inputs, seg_blocks, cotangents))
    middle, final, grad_entry, grad_middle = results
    layer_outputs = jnp.stack([middle.reshape(SEQS, L, D), final.reshape(SEQS, L, D)]).astype(jnp.bfloat16)
    input_grads = jnp.stack([grad_entry.reshape(SEQS, L, D), grad_middle.reshape(SEQS, L, D)]).astype(jnp.bfloat16)
    grads = tuple((jnp.stack([totals[0][index], totals[1][index]]) for index in range(10)))
    return (layer_outputs, input_grads, grads[0], grads[1], grads[2], grads[3], grads[4], grads[5], grads[6], grads[7], grads[8], grads[9])
```

```python
import functools

import jax
import jax.numpy as jnp
from jax import lax
from jax.experimental import pallas as pl
from jax.experimental.pallas import tpu as pltpu
from jax.sharding import PartitionSpec as P

HEAD_DIM = 64
EPSILON = 1e-06
BIG_NEGATIVE = -1e30
VMEM_BYTES = 40 * 1024 * 1024
EXTRA_ROWS = 16
SQRT_HALF = 0.7071067811865476
INV_SQRT_TAU = 0.3989422804014327

f32 = jnp.float32
bf16 = jnp.bfloat16


def dot_nn(left, right):
    return lax.dot_general(left, right, (((1,), (0,)), ((), ())), preferred_element_type=f32)


def dot_nt(left, right):
    return lax.dot_general(left, right, (((1,), (1,)), ((), ())), preferred_element_type=f32)


def dot_tn(left, right):
    return lax.dot_general(left, right, (((0,), (0,)), ((), ())), preferred_element_type=f32)


def shape(dims, kind):
    return jax.ShapeDtypeStruct(dims, kind)


def run(kernel, outs, args, flops, name, **grid):
    moved = sum(item.size * item.dtype.itemsize for item in (*args, *outs))
    return pl.pallas_call(
        kernel,
        out_shape=outs,
        name=name,
        compiler_params=pltpu.CompilerParams(vmem_limit_bytes=VMEM_BYTES),
        cost_estimate=pl.CostEstimate(flops=flops, bytes_accessed=moved, transcendentals=0),
        **grid,
    )(*args)


def heads_forward(rows, w, bias, same):
    query = ((dot_nn(rows, w[0]) + bias[0:1]).astype(bf16) * HEAD_DIM**-0.5).astype(bf16)
    key = dot_nn(rows, w[1]).astype(bf16)
    value = (dot_nn(rows, w[2]) + bias[1:2]).astype(bf16)
    probs, mixed = [], []
    for start in range(0, query.shape[1], HEAD_DIM):
        head = slice(start, start + HEAD_DIM)
        scores = jnp.where(same, dot_nt(query[:, head], key[:, head]), BIG_NEGATIVE)
        weights = jnp.exp(scores - jnp.max(scores, -1, keepdims=True))
        total = jnp.sum(weights, -1, keepdims=True)
        low = (weights * (1.0 / total)).astype(bf16)
        probs.append(low)
        mixed.append(dot_nn(low, value[:, head]).astype(bf16))
    return query, key, value, probs, jnp.concatenate(mixed, 1)


def heads_backward(query, key, value, probs, grad_mixed):
    parts = [], [], []
    for number, low in enumerate(probs):
        head = slice(number * HEAD_DIM, (number + 1) * HEAD_DIM)
        upstream = grad_mixed[:, head]
        wide = low.astype(f32)
        product = wide * dot_nt(upstream, value[:, head])
        scores = (product - wide * jnp.sum(product, -1, keepdims=True)).astype(bf16)
        parts[0].append((dot_nn(scores, key[:, head]) * HEAD_DIM**-0.5).astype(bf16))
        parts[1].append(dot_tn(scores, query[:, head]).astype(bf16))
        parts[2].append(dot_tn(low, upstream).astype(bf16))
    return [jnp.concatenate(part, 1) for part in parts]


def attend_kernel(own, other, w_own, w_far, b_own, b_far, o_own, o_far, seg_row, seg_col, *outs):
    keep, send = outs[:2]
    rows = jnp.concatenate([own[...], other[...]], 0)
    same = seg_col[...] == seg_row[...]
    total = None
    for group, (w, bias, out) in enumerate(((w_own, b_own, o_own), (w_far, b_far, o_far))):
        query, key, value, probs, mixed = heads_forward(rows, w, bias, same)
        if len(outs) > 2:
            qkv, kept = outs[2:]
            qkv[group, 0], qkv[group, 1], qkv[group, 2] = query, key, value
            for number, low in enumerate(probs):
                kept[group, number] = low
        term = dot_nn(mixed, out[...])
        total = term if total is None else total + term
    half = own.shape[0]
    keep[...] = total[:half]
    send[...] = total[half:].astype(bf16)


def attend_back_kernel(own, other, w_own, w_far, o_own, o_far, qkv, kept, keep, send):
    rows = jnp.concatenate([own[...], other[...]], 0)
    total = None
    for group, (w, out) in enumerate(((w_own, o_own), (w_far, o_far))):
        grad_mixed = dot_nt(rows, out[...]).astype(bf16)
        probs = [kept[group, number] for number in range(kept.shape[1])]
        parts = heads_backward(qkv[group, 0], qkv[group, 1], qkv[group, 2], probs, grad_mixed)
        for number, part in enumerate(parts):
            term = dot_nt(part, w[number])
            total = term if total is None else total + term
    half = own.shape[0]
    keep[...] = total[:half]
    send[...] = total[half:].astype(bf16)


def standard(values):
    centred = values - jnp.mean(values, -1, keepdims=True)
    spread = lax.rsqrt(jnp.mean(centred * centred, -1, keepdims=True) + EPSILON)
    return centred * spread, spread


def norm_kernel(arrived, kept, residual, bias, gain, shift, *outs):
    summed = residual[...].astype(f32) + (arrived[...].astype(f32) + kept[...] + bias[...])
    result = standard(summed)[0] * gain[...] + shift[...]
    outs[0][...] = result.astype(bf16)
    if len(outs) > 1:
        outs[1][...] = result
    if len(outs) > 2:
        outs[2][...] = summed


def norm_grads(values, gain, upstream):
    normal, spread = standard(values)
    scaled = upstream * gain
    along = jnp.mean(scaled * normal, -1, keepdims=True)
    grad = (scaled - jnp.mean(scaled, -1, keepdims=True) - normal * along) * spread
    return grad, jnp.sum(upstream * normal, 0, keepdims=True), jnp.sum(upstream, 0, keepdims=True)


def norm_back_kernel(upstream, values, gain, grad, low, gain_bias):
    result, grad_gain, grad_shift = norm_grads(values[...], gain[...], upstream[...].astype(f32))
    grad[...] = result
    low[...] = result.astype(bf16)
    gain_bias[0:1] = grad_gain
    gain_bias[1:2] = grad_shift


def norm_back_sum_kernel(arrived, kept, residual, values, gain, others, grad, low):
    upstream = residual[...] + (arrived[...].astype(f32) + kept[...])
    result, grad_gain, grad_shift = norm_grads(values[...], gain[...], upstream)
    rows = result.shape[0]
    grad[...] = result
    low[0:rows] = result.astype(bf16)
    small = jnp.concatenate([grad_gain, grad_shift, others[0:2]], 0)
    high = small.astype(bf16)
    rest = (small - high.astype(f32)).astype(bf16)
    blank = jnp.zeros((EXTRA_ROWS - 8, result.shape[1]), bf16)
    low[rows : rows + EXTRA_ROWS] = jnp.concatenate([high, rest, blank], 0)


def feed_kernel(one, two, three, four, up, up_bias, down, keep, send, *saved):
    part = one.shape[0]
    rows = jnp.concatenate([one[...], two[...], three[...], four[...]], 0)
    hidden = dot_nn(rows, up[...]) + up_bias[...]
    phi = 0.5 * (1.0 + lax.erf(hidden * SQRT_HALF))
    if saved:
        slope = phi + hidden * (jnp.exp(-0.5 * hidden * hidden) * INV_SQRT_TAU)
        saved[0][...] = slope.astype(bf16)
    total = dot_nn((hidden * phi).astype(bf16), down[...])
    keep[...] = total[: 2 * part]
    send[...] = total[2 * part :].astype(bf16)


def feed_back_kernel(one, two, three, four, slope, up, down, keep, send):
    part = one.shape[0]
    rows = jnp.concatenate([one[...], two[...], three[...], four[...]], 0)
    hidden = (dot_nt(rows, down[...]) * slope[...].astype(f32)).astype(bf16)
    total = dot_nt(hidden, up[...])
    keep[...] = total[: 2 * part]
    send[...] = total[2 * part :].astype(bf16)


def halves_kernel(arrived, kept, keep, send):
    part = keep.shape[0]
    total = arrived[...].astype(f32) + kept[...]
    keep[...] = total[:part]
    send[...] = total[part:].astype(bf16)


def entry_grad_kernel(arrived, kept, residual, low):
    low[...] = (residual[...] + (arrived[...].astype(f32) + kept[...])).astype(bf16)


def attend_all_kernel(rows, w, bias, seg_row, seg_col, qkv, kept, mixed):
    part = rows.shape[1] - EXTRA_ROWS
    whole = jnp.concatenate([rows[0, :part], rows[1, :part]], 0)
    same = seg_col[0] == seg_row[0]
    query, key, value, probs, heads = heads_forward(whole, w, bias, same)
    qkv[0, 0], qkv[0, 1], qkv[0, 2] = query, key, value
    for number, low in enumerate(probs):
        kept[0, number] = low
    mixed[0] = heads


def attend_grads_kernel(rows, grads, out, qkv, kept, mixed, g_w, g_b, g_out, g_out_b):
    @pl.when(pl.program_id(0) == 0)
    def _():
        g_w[...] = jnp.zeros_like(g_w)
        g_b[...] = jnp.zeros_like(g_b)
        g_out[...] = jnp.zeros_like(g_out)
        g_out_b[...] = jnp.zeros_like(g_out_b)

    part = rows.shape[1] - EXTRA_ROWS
    entry = jnp.concatenate([rows[0, :part], rows[1, :part]], 0)
    branch = jnp.concatenate([grads[0, :part], grads[1, :part]], 0)
    grad_mixed = dot_nt(branch, out[...]).astype(bf16)
    probs = [kept[0, number] for number in range(kept.shape[1])]
    parts = heads_backward(qkv[0, 0], qkv[0, 1], qkv[0, 2], probs, grad_mixed)
    for number, item in enumerate(parts):
        g_w[number] += dot_tn(entry, item)
    g_b[0:1] += jnp.sum(parts[0].astype(f32), 0, keepdims=True)
    g_b[1:2] += jnp.sum(parts[2].astype(f32), 0, keepdims=True)
    g_out[...] += dot_tn(mixed[0], branch)
    g_out_b[...] += jnp.sum(branch.astype(f32), 0, keepdims=True)


def feed_grads_kernel(rows, grads, up, up_bias, down, g_up, g_up_b, g_down, g_down_b):
    @pl.when(pl.program_id(0) == 0)
    def _():
        g_up[...] = jnp.zeros_like(g_up)
        g_up_b[...] = jnp.zeros_like(g_up_b)
        g_down[...] = jnp.zeros_like(g_down)
        g_down_b[...] = jnp.zeros_like(g_down_b)

    first, grad = rows[...], grads[...]
    hidden = dot_nn(first, up[...]) + up_bias[...]
    phi = 0.5 * (1.0 + lax.erf(hidden * SQRT_HALF))
    slope = phi + hidden * (jnp.exp(-0.5 * hidden * hidden) * INV_SQRT_TAU)
    act = (hidden * phi).astype(bf16)
    grad_hidden = (dot_nt(grad, down[...]) * slope).astype(bf16)
    g_down[...] += dot_tn(act, grad)
    g_up[...] += dot_tn(first, grad_hidden)
    g_up_b[...] += jnp.sum(grad_hidden.astype(f32), 0, keepdims=True)
    g_down_b[...] += jnp.sum(grad.astype(f32), 0, keepdims=True)


def whole(item):
    return pl.BlockSpec(item.shape, lambda step: (0,) * len(item.shape))


def leading(item, count):
    rest = len(item.shape) - 1
    return pl.BlockSpec((count,) + item.shape[1:], lambda step: (step,) + (0,) * rest)


def shards(
    block_input,
    segments,
    out_grad,
    query_key_value_weight,
    b_qv,
    attention_output_weight,
    attention_out_bias,
    ln_gain,
    ln_bias,
    up_projection_weight,
    up_proj_bias,
    down_projection_weight,
    down_proj_bias,
):
    assert lax.axis_size("tensor") == 4 and block_input.shape[0] == 2
    groups = lax.axis_size("dp")
    section = lax.axis_index("section")
    place = lax.axis_index("tensor")
    a, b = place // 2, place % 2
    seqs, quarter, width = block_input.shape
    length = segments.shape[1]
    part = length // 2
    local = query_key_value_weight.shape[3]
    hidden_local = up_projection_weight.shape[2]
    heads = local // HEAD_DIM

    beside = [(i, i ^ 1) for i in range(4)]
    across = [(i, i ^ 2) for i in range(4)]
    turn = [(2 * s + c, 2 * c + s) for s in range(2) for c in range(2)]
    twist = [(2 * s + c, 2 * c + 1 - s) for s in range(2) for c in range(2)]
    untwist = [(target, source) for source, target in twist]

    def swap(value, pairs):
        return lax.ppermute(value, "tensor", pairs)

    def pieces_of(block):
        one = swap(jnp.where(b == 0, block[0], block[1]), turn)
        two = swap(jnp.where(b == 0, block[1], block[0]), untwist)
        return jnp.where(a == 0, jnp.concatenate([one, two]), jnp.concatenate([two, one]))

    def blocks_of(piece):
        one = swap(jnp.where(a == 0, piece[:quarter], piece[quarter:]), turn)
        two = swap(jnp.where(a == 0, piece[quarter:], piece[:quarter]), twist)
        return jnp.where(b == 0, jnp.stack([one, two]), jnp.stack([two, one]))

    w_own = jnp.transpose(query_key_value_weight[0], (1, 0, 2))
    o_own = attention_output_weight[0]
    b_own = b_qv[0].astype(f32)
    entry_input = pieces_of(block_input)
    w_far = swap(w_own, across)
    o_far = swap(o_own, across)
    b_far = swap(b_own, across)
    cotangent = pieces_of(out_grad)
    out_bias = attention_out_bias.astype(f32)
    gain = ln_gain[0].astype(f32)
    shift = ln_bias[0].astype(f32)
    up, down = up_projection_weight[0], down_projection_weight[0]
    up_bias = up_proj_bias.astype(f32)
    down_bias = down_proj_bias.astype(f32)

    seg_own = segments[0] if seqs == 1 else jnp.where(a == 0, segments[0], segments[1])
    seg_own = seg_own.astype(f32)
    seg_turned = jnp.where(b == 0, seg_own, jnp.roll(seg_own, part))
    seg_row, seg_col = seg_turned[None, :], seg_turned[:, None]

    piece_f, piece_h = shape((part, width), f32), shape((part, width), bf16)
    pair_f, pair_h = shape((2 * part, width), f32), shape((2 * part, width), bf16)
    weights_macs = length * width * 4 * local * 2
    scores_macs = 2 * heads * length * length * HEAD_DIM
    feed_macs = 4 * part * width * hidden_local * 2

    def forward(entry, save):
        outs = [piece_f, piece_h]
        if save:
            outs += [
                shape((2, 3, length, local), bf16),
                shape((2, heads, length, length), bf16),
            ]
        args = (entry, swap(entry, beside), w_own, w_far, b_own, b_far, o_own, o_far, seg_row, seg_col)
        flops = 2 * weights_macs + 4 * scores_macs
        keep, send, *kept = run(attend_kernel, outs, args, flops, "attend")
        args = (swap(send, beside), keep, entry, out_bias, gain[0:1], shift[0:1])
        first_low, first, *first_res = run(
            norm_kernel, [piece_h, piece_f] + [piece_f] * save, args, 0, "first_norm"
        )
        far = swap(first_low, across)
        near, far_near = swap(first_low, beside), None
        far_near = swap(far, beside)
        outs = [pair_f, pair_h] + [shape((4 * part, hidden_local), bf16)] * save
        args = (first_low, far, near, far_near, up, up_bias, down)
        keep, send, *slope = run(feed_kernel, outs, args, 2 * feed_macs, "feed")
        keep, send = run(halves_kernel, [piece_f, piece_h], (swap(send, beside), keep), 0, "halves")
        args = (swap(send, across), keep, first, down_bias, gain[1:2], shift[1:2])
        output, *second = run(
            norm_kernel, [piece_h] + [piece_f, piece_f] * save, args, 0, "second_norm"
        )
        if not save:
            return output
        return output, kept, first_low, first_res[0], slope[0], second[1]

    def backward(upstream, saved):
        kept, first_res, slope, second_res = saved
        grad_second, grad_y, gain_bias = run(
            norm_back_kernel,
            [piece_f, piece_h, shape((2, width), f32)],
            (upstream, second_res, gain[1:2]),
            0,
            "second_norm_back",
        )
        far = swap(grad_y, across)
        near = swap(grad_y, beside)
        far_near = swap(far, beside)
        args = (grad_y, far, near, far_near, slope, up, down)
        keep, send = run(feed_back_kernel, [pair_f, pair_h], args, 2 * feed_macs, "feed_back")
        keep, send = run(halves_kernel, [piece_f, piece_h], (swap(send, beside), keep), 0, "halves")
        args = (swap(send, across), keep, grad_second, first_res, gain[0:1], gain_bias)
        grad_first, grad_branch = run(
            norm_back_sum_kernel,
            [piece_f, shape((part + EXTRA_ROWS, width), bf16)],
            args,
            0,
            "first_norm_back",
        )
        branch = grad_branch[:part]
        args = (branch, swap(branch, beside), w_own, w_far, o_own, o_far, *kept)
        flops = 2 * weights_macs + 10 * scores_macs
        keep, send = run(attend_back_kernel, [piece_f, piece_h], args, flops, "attend_back")
        args = (swap(send, beside), keep, grad_first)
        grad_entry = run(entry_grad_kernel, [piece_h], args, 0, "entry_grad")[0]
        return grad_entry, grad_y, grad_branch

    middle = lax.ppermute(forward(entry_input, False), "section", [(0, 1)])
    entry = jnp.where(section == 0, entry_input, middle)
    output, kept, first_low, first_res, slope, second_res = forward(entry, True)
    saved = (kept, first_res, slope, second_res)
    middle = lax.ppermute(backward(cotangent, saved)[0], "section", [(1, 0)])
    grad_entry, grad_y, grad_branch = backward(jnp.where(section == 1, cotangent, middle), saved)

    wide = groups <= 4
    axes = ("dp", "tensor") if wide else ("tensor",)
    seg_line = jnp.where(b == 0, seg_own[:part], seg_own[part:]).astype(bf16)
    seg_line = jnp.pad(seg_line[None], ((0, EXTRA_ROWS - 1), (0, width - part)))
    entry_all = lax.all_gather(jnp.concatenate([entry, seg_line]), axes)
    first_all = lax.all_gather(first_low, axes)
    grad_y_all = lax.all_gather(grad_y, axes)
    grad_branch_all = lax.all_gather(grad_branch, axes)
    count = entry_all.shape[0] // 2

    seg_all = entry_all[:, part, :part].astype(f32).reshape(count, length)
    args = (entry_all, w_own, b_own, seg_all[:, None, :], seg_all[:, :, None])
    outs = [
        shape((count, 3, length, local), bf16),
        shape((count, heads, length, length), bf16),
        shape((count, length, local), bf16),
    ]
    qkv_all, kept_all, mixed_all = run(
        attend_all_kernel,
        outs,
        args,
        count * (weights_macs + 2 * scores_macs),
        "attend_all",
        grid=(count,),
        in_specs=[leading(args[0], 2), whole(w_own), whole(b_own), leading(args[3], 1), leading(args[4], 1)],
        out_specs=[leading(item, 1) for item in outs],
    )

    args = (
        first_all.reshape(-1, width),
        grad_y_all.reshape(-1, width),
        up,
        up_bias,
        down,
    )
    outs = [
        shape((width, hidden_local), f32),
        shape((1, hidden_local), f32),
        shape((hidden_local, width), f32),
        shape((1, width), f32),
    ]
    block = 2 * length
    g_up, g_up_b, g_down, g_down_b = run(
        feed_grads_kernel,
        outs,
        args,
        count * feed_macs * 2,
        "feed_grads",
        grid=(args[0].shape[0] // block,),
        in_specs=[leading(args[0], block), leading(args[1], block), whole(up), whole(up_bias), whole(down)],
        out_specs=[whole(item) for item in outs],
    )

    args = (entry_all, grad_branch_all, o_own, qkv_all, kept_all, mixed_all)
    outs = [
        shape((3, width, local), f32),
        shape((2, local), f32),
        shape((local, width), f32),
        shape((1, width), f32),
    ]
    g_w, g_b, g_out, g_out_b = run(
        attend_grads_kernel,
        outs,
        args,
        count * (weights_macs + 5 * scores_macs),
        "attend_grads",
        grid=(count,),
        in_specs=[leading(args[0], 2), leading(args[1], 2), whole(o_own)]
        + [leading(item, 1) for item in args[3:]],
        out_specs=[whole(item) for item in outs],
    )
    small = jnp.sum(grad_branch_all[:, part : part + 8].astype(f32), 0)
    small = small[:4] + small[4:]
    totals = (g_w, g_b, g_out, g_up, g_up_b, g_down)
    if not wide:
        totals = [lax.psum(item.astype(bf16), "dp").astype(f32) for item in totals]
        g_out_b, g_down_b, small = lax.psum((g_out_b, g_down_b, small), "dp")
    g_w, g_b, g_out, g_up, g_up_b, g_down = totals
    return (
        blocks_of(output)[None],
        blocks_of(grad_entry)[None],
        jnp.transpose(g_w, (1, 0, 2))[None],
        g_b[None],
        g_out[None],
        g_out_b,
        jnp.stack([small[0], small[2]])[None],
        jnp.stack([small[1], small[3]])[None],
        g_up[None],
        g_up_b,
        g_down[None],
        g_down_b,
    )


def solution(mesh):
    return jax.shard_map(
        shards,
        mesh=mesh,
        in_specs=(
            P("dp", "tensor", None),
            P("dp", None),
            P("dp", "tensor", None),
            P("section", None, None, "tensor"),
            P("section", None, "tensor"),
            P("section", "tensor", None),
            P("section", None),
            P("section", None, None),
            P("section", None, None),
            P("section", None, "tensor"),
            P("section", "tensor"),
            P("section", "tensor", None),
            P("section", None),
        ),
        out_specs=(
            P("section", "dp", "tensor", None),
            P("section", "dp", "tensor", None),
            P("section", None, None, "tensor"),
            P("section", None, "tensor"),
            P("section", "tensor", None),
            P("section", None),
            P("section", None, None),
            P("section", None, None),
            P("section", None, "tensor"),
            P("section", "tensor"),
            P("section", "tensor", None),
            P("section", None),
        ),
        check_vma=False,
    )
```

```python
import functools

import jax
import jax.numpy as jnp
from jax import lax
from jax.experimental import pallas as pl
from jax.experimental.pallas import tpu as pltpu
from jax.sharding import PartitionSpec as P

HEAD_DIM = 64
EPSILON = 1e-06
BIG_NEGATIVE = -1e30
MIB = 1024 * 1024
EXTRA_ROWS = 16
SQRT_HALF = 0.7071067811865476
INV_SQRT_TAU = 0.3989422804014327

f32 = jnp.float32
bf16 = jnp.bfloat16


def dot_nn(left, right):
    return lax.dot_general(left, right, (((1,), (0,)), ((), ())), preferred_element_type=f32)


def dot_nt(left, right):
    return lax.dot_general(left, right, (((1,), (1,)), ((), ())), preferred_element_type=f32)


def dot_tn(left, right):
    return lax.dot_general(left, right, (((0,), (0,)), ((), ())), preferred_element_type=f32)


def shape(dims, kind):
    return jax.ShapeDtypeStruct(dims, kind)


def run(kernel, outs, args, flops, name, mib=16, **grid):
    moved = sum(item.size * item.dtype.itemsize for item in (*args, *outs))
    return pl.pallas_call(
        kernel,
        out_shape=outs,
        name=name,
        compiler_params=pltpu.CompilerParams(vmem_limit_bytes=mib * MIB),
        cost_estimate=pl.CostEstimate(flops=flops, bytes_accessed=moved, transcendentals=0),
        **grid,
    )(*args)


def heads_forward(rows, w, bias, same):
    query = ((dot_nn(rows, w[0]) + bias[0:1]).astype(bf16) * HEAD_DIM**-0.5).astype(bf16)
    key = dot_nn(rows, w[1]).astype(bf16)
    value = (dot_nn(rows, w[2]) + bias[1:2]).astype(bf16)
    probs, mixed = [], []
    for start in range(0, query.shape[1], HEAD_DIM):
        head = slice(start, start + HEAD_DIM)
        scores = jnp.where(same, dot_nt(query[:, head], key[:, head]), BIG_NEGATIVE)
        weights = jnp.exp(scores - jnp.max(scores, -1, keepdims=True))
        total = jnp.sum(weights, -1, keepdims=True)
        low = (weights * (1.0 / total)).astype(bf16)
        probs.append(low)
        mixed.append(dot_nn(low, value[:, head]).astype(bf16))
    return query, key, value, probs, jnp.concatenate(mixed, 1)


def heads_backward(query, key, value, probs, grad_mixed):
    parts = [], [], []
    for number, low in enumerate(probs):
        head = slice(number * HEAD_DIM, (number + 1) * HEAD_DIM)
        upstream = grad_mixed[:, head]
        wide = low.astype(f32)
        product = wide * dot_nt(upstream, value[:, head])
        scores = (product - wide * jnp.sum(product, -1, keepdims=True)).astype(bf16)
        parts[0].append((dot_nn(scores, key[:, head]) * HEAD_DIM**-0.5).astype(bf16))
        parts[1].append(dot_tn(scores, query[:, head]).astype(bf16))
        parts[2].append(dot_tn(low, upstream).astype(bf16))
    return [jnp.concatenate(part, 1) for part in parts]


def attend_kernel(own, other, w_own, w_far, b_own, b_far, o_own, o_far, seg_row, seg_col, *outs):
    keep, send = outs[:2]
    rows = jnp.concatenate([own[...], other[...]], 0)
    same = seg_col[...] == seg_row[...]
    total = None
    for group, (w, bias, out) in enumerate(((w_own, b_own, o_own), (w_far, b_far, o_far))):
        query, key, value, probs, mixed = heads_forward(rows, w, bias, same)
        if len(outs) > 2:
            qkv, kept = outs[2:]
            qkv[group, 0], qkv[group, 1], qkv[group, 2] = query, key, value
            for number, low in enumerate(probs):
                kept[group, number] = low
        term = dot_nn(mixed, out[...])
        total = term if total is None else total + term
    half = own.shape[0]
    keep[...] = total[:half]
    send[...] = total[half:].astype(bf16)


def attend_back_kernel(own, other, w_own, w_far, o_own, o_far, qkv, kept, keep, send):
    rows = jnp.concatenate([own[...], other[...]], 0)
    total = None
    for group, (w, out) in enumerate(((w_own, o_own), (w_far, o_far))):
        grad_mixed = dot_nt(rows, out[...]).astype(bf16)
        probs = [kept[group, number] for number in range(kept.shape[1])]
        parts = heads_backward(qkv[group, 0], qkv[group, 1], qkv[group, 2], probs, grad_mixed)
        for number, part in enumerate(parts):
            term = dot_nt(part, w[number])
            total = term if total is None else total + term
    half = own.shape[0]
    keep[...] = total[:half]
    send[...] = total[half:].astype(bf16)


def standard(values):
    centred = values - jnp.mean(values, -1, keepdims=True)
    spread = lax.rsqrt(jnp.mean(centred * centred, -1, keepdims=True) + EPSILON)
    return centred * spread, spread


def norm_kernel(arrived, kept, residual, bias, gain, shift, *outs):
    summed = residual[...].astype(f32) + (arrived[...].astype(f32) + kept[...] + bias[...])
    result = standard(summed)[0] * gain[...] + shift[...]
    outs[0][...] = result.astype(bf16)
    if len(outs) > 1:
        outs[1][...] = result
    if len(outs) > 2:
        outs[2][...] = summed


def norm_grads(values, gain, upstream):
    normal, spread = standard(values)
    scaled = upstream * gain
    along = jnp.mean(scaled * normal, -1, keepdims=True)
    grad = (scaled - jnp.mean(scaled, -1, keepdims=True) - normal * along) * spread
    return grad, jnp.sum(upstream * normal, 0, keepdims=True), jnp.sum(upstream, 0, keepdims=True)


def norm_back_kernel(upstream, values, gain, grad, low, gain_bias):
    result, grad_gain, grad_shift = norm_grads(values[...], gain[...], upstream[...].astype(f32))
    grad[...] = result
    low[...] = result.astype(bf16)
    gain_bias[0:1] = grad_gain
    gain_bias[1:2] = grad_shift


def norm_back_sum_kernel(arrived, kept, residual, values, gain, others, grad, low):
    upstream = residual[...] + (arrived[...].astype(f32) + kept[...])
    result, grad_gain, grad_shift = norm_grads(values[...], gain[...], upstream)
    rows = result.shape[0]
    grad[...] = result
    low[0:rows] = result.astype(bf16)
    small = jnp.concatenate([grad_gain, grad_shift, others[0:2]], 0)
    high = small.astype(bf16)
    rest = (small - high.astype(f32)).astype(bf16)
    blank = jnp.zeros((EXTRA_ROWS - 8, result.shape[1]), bf16)
    low[rows : rows + EXTRA_ROWS] = jnp.concatenate([high, rest, blank], 0)


def feed_kernel(one, two, three, four, up, up_bias, down, keep, send, *saved):
    part = one.shape[0]
    rows = jnp.concatenate([one[...], two[...], three[...], four[...]], 0)
    hidden = dot_nn(rows, up[...]) + up_bias[...]
    phi = 0.5 * (1.0 + lax.erf(hidden * SQRT_HALF))
    if saved:
        slope = phi + hidden * (jnp.exp(-0.5 * hidden * hidden) * INV_SQRT_TAU)
        saved[0][...] = slope.astype(bf16)
    total = dot_nn((hidden * phi).astype(bf16), down[...])
    keep[...] = total[: 2 * part]
    send[...] = total[2 * part :].astype(bf16)


def feed_back_kernel(one, two, three, four, slope, up, down, keep, send):
    part = one.shape[0]
    rows = jnp.concatenate([one[...], two[...], three[...], four[...]], 0)
    hidden = (dot_nt(rows, down[...]) * slope[...].astype(f32)).astype(bf16)
    total = dot_nt(hidden, up[...])
    keep[...] = total[: 2 * part]
    send[...] = total[2 * part :].astype(bf16)


def halves_kernel(arrived, kept, keep, send):
    part = keep.shape[0]
    total = arrived[...].astype(f32) + kept[...]
    keep[...] = total[:part]
    send[...] = total[part:].astype(bf16)


def entry_grad_kernel(arrived, kept, residual, low):
    low[...] = (residual[...] + (arrived[...].astype(f32) + kept[...])).astype(bf16)


def attend_all_kernel(mine, other, w, bias, seg_row, seg_col, qkv, kept, mixed):
    part = mine.shape[1] - EXTRA_ROWS
    rows = jnp.concatenate([mine[0, :part], other[0, :part]], 0)
    same = seg_col[0] == seg_row[0]
    query, key, value, probs, heads = heads_forward(rows, w, bias, same)
    qkv[0, 0], qkv[0, 1], qkv[0, 2] = query, key, value
    for number, low in enumerate(probs):
        kept[0, number] = low
    mixed[0] = heads


def attend_grads_kernel(group, mine, other, one, two, three, four, out, qkv, kept, mixed, *refs):
    g_w, g_b, g_out, g_out_b, g_small = refs[-5:]
    part = mine.shape[1] - EXTRA_ROWS
    sums = None
    for seq, (low_half, high_half) in enumerate(((one, two), (three, four))):
        entry = jnp.concatenate([mine[seq, :part], other[seq, :part]], 0)
        branch = jnp.concatenate([low_half[:part], high_half[:part]], 0)
        grad_mixed = dot_nt(branch, out[...]).astype(bf16)
        probs = [kept[seq, number] for number in range(kept.shape[1])]
        parts = heads_backward(qkv[seq, 0], qkv[seq, 1], qkv[seq, 2], probs, grad_mixed)
        small = low_half[part:].astype(f32) + high_half[part:].astype(f32)
        terms = [dot_tn(entry, item) for item in parts]
        terms += [jnp.sum(parts[0].astype(f32), 0, keepdims=True)]
        terms += [jnp.sum(parts[2].astype(f32), 0, keepdims=True)]
        terms += [dot_tn(mixed[seq], branch), jnp.sum(branch.astype(f32), 0, keepdims=True)]
        terms += [small[:4] + small[4:8]]
        sums = terms if sums is None else [old + new for old, new in zip(sums, terms)]
    before = refs[:-5]
    for number, item in enumerate(sums):
        name = (0, 0, 0, 1, 1, 2, 3, 4)[number]
        spot = ((0,), (1,), (2,), (slice(0, 1),), (slice(1, 2),), (), (), ())[number]
        spot = spot if spot else (...,)
        refs[name - 5][spot] = item + before[name][spot] if before else item


def feed_all_kernel(rows, up, up_bias, act, slope):
    hidden = dot_nn(rows[...], up[...]) + up_bias[...]
    phi = 0.5 * (1.0 + lax.erf(hidden * SQRT_HALF))
    act[...] = (hidden * phi).astype(bf16)
    slope[...] = (phi + hidden * (jnp.exp(-0.5 * hidden * hidden) * INV_SQRT_TAU)).astype(bf16)


def feed_grads_kernel(*refs):
    down, g_up, g_up_b, g_down, g_down_b = refs[8:]

    @pl.when(pl.program_id(0) == 0)
    def _():
        g_up[...] = jnp.zeros_like(g_up)
        g_up_b[...] = jnp.zeros_like(g_up_b)
        g_down[...] = jnp.zeros_like(g_down)
        g_down_b[...] = jnp.zeros_like(g_down_b)

    first, grad, act, slope = (
        jnp.concatenate([refs[i][...], refs[i + 4][...]], 0) for i in range(4)
    )
    grad_hidden = (dot_nt(grad, down[...]) * slope.astype(f32)).astype(bf16)
    g_down[...] += dot_tn(act, grad)
    g_up[...] += dot_tn(first, grad_hidden)
    g_up_b[...] += jnp.sum(grad_hidden.astype(f32), 0, keepdims=True)
    g_down_b[...] += jnp.sum(grad.astype(f32), 0, keepdims=True)


def whole(item):
    return pl.BlockSpec(item.shape, lambda step: (0,) * len(item.shape))


def leading(item, count):
    rest = len(item.shape) - 1
    return pl.BlockSpec((count,) + item.shape[1:], lambda step: (step,) + (0,) * rest)


def shards(
    block_input,
    segments,
    out_grad,
    query_key_value_weight,
    b_qv,
    attention_output_weight,
    attention_out_bias,
    ln_gain,
    ln_bias,
    up_projection_weight,
    up_proj_bias,
    down_projection_weight,
    down_proj_bias,
):
    assert lax.axis_size("tensor") == 4 and block_input.shape[0] == 2
    groups = lax.axis_size("dp")
    section = lax.axis_index("section")
    place = lax.axis_index("tensor")
    a, b = place // 2, place % 2
    seqs, quarter, width = block_input.shape
    length = segments.shape[1]
    part = length // 2
    local = query_key_value_weight.shape[3]
    hidden_local = up_projection_weight.shape[2]
    heads = local // HEAD_DIM

    beside = [(i, i ^ 1) for i in range(4)]
    across = [(i, i ^ 2) for i in range(4)]
    turn = [(2 * s + c, 2 * c + s) for s in range(2) for c in range(2)]
    twist = [(2 * s + c, 2 * c + 1 - s) for s in range(2) for c in range(2)]
    untwist = [(target, source) for source, target in twist]

    def swap(value, pairs):
        return lax.ppermute(value, "tensor", pairs)

    def pieces_of(block):
        one = swap(jnp.where(b == 0, block[0], block[1]), turn)
        two = swap(jnp.where(b == 0, block[1], block[0]), untwist)
        return jnp.where(a == 0, jnp.concatenate([one, two]), jnp.concatenate([two, one]))

    def blocks_of(piece):
        one = swap(jnp.where(a == 0, piece[:quarter], piece[quarter:]), turn)
        two = swap(jnp.where(a == 0, piece[quarter:], piece[:quarter]), twist)
        return jnp.where(b == 0, jnp.stack([one, two]), jnp.stack([two, one]))

    w_own = jnp.transpose(query_key_value_weight[0], (1, 0, 2))
    o_own = attention_output_weight[0]
    b_own = b_qv[0].astype(f32)
    entry_input = pieces_of(block_input)
    w_far = swap(w_own, across)
    o_far = swap(o_own, across)
    b_far = swap(b_own, across)
    cotangent = pieces_of(out_grad)
    out_bias = attention_out_bias.astype(f32)
    gain = ln_gain[0].astype(f32)
    shift = ln_bias[0].astype(f32)
    up, down = up_projection_weight[0], down_projection_weight[0]
    up_bias = up_proj_bias.astype(f32)
    down_bias = down_proj_bias.astype(f32)

    seg_own = segments[0] if seqs == 1 else jnp.where(a == 0, segments[0], segments[1])
    seg_own = seg_own.astype(f32)
    seg_turned = jnp.where(b == 0, seg_own, jnp.roll(seg_own, part))
    seg_row, seg_col = seg_turned[None, :], seg_turned[:, None]

    piece_f, piece_h = shape((part, width), f32), shape((part, width), bf16)
    pair_f, pair_h = shape((2 * part, width), f32), shape((2 * part, width), bf16)
    weights_macs = length * width * 4 * local * 2
    scores_macs = 2 * heads * length * length * HEAD_DIM
    feed_macs = 4 * part * width * hidden_local * 2

    def forward(entry, save):
        outs = [piece_f, piece_h]
        if save:
            outs += [
                shape((2, 3, length, local), bf16),
                shape((2, heads, length, length), bf16),
            ]
        args = (entry, swap(entry, beside), w_own, w_far, b_own, b_far, o_own, o_far, seg_row, seg_col)
        flops = 2 * weights_macs + 4 * scores_macs
        keep, send, *kept = run(attend_kernel, outs, args, flops, "attend")
        args = (swap(send, beside), keep, entry, out_bias, gain[0:1], shift[0:1])
        first_low, first, *first_res = run(
            norm_kernel, [piece_h, piece_f] + [piece_f] * save, args, 0, "first_norm"
        )
        far = swap(first_low, across)
        near, far_near = swap(first_low, beside), None
        far_near = swap(far, beside)
        outs = [pair_f, pair_h] + [shape((4 * part, hidden_local), bf16)] * save
        args = (first_low, far, near, far_near, up, up_bias, down)
        keep, send, *slope = run(feed_kernel, outs, args, 2 * feed_macs, "feed")
        keep, send = run(halves_kernel, [piece_f, piece_h], (swap(send, beside), keep), 0, "halves")
        args = (swap(send, across), keep, first, down_bias, gain[1:2], shift[1:2])
        output, *second = run(
            norm_kernel, [piece_h] + [piece_f, piece_f] * save, args, 0, "second_norm"
        )
        if not save:
            return output
        return output, kept, (first_low, far), first_res[0], slope[0], second[1]

    def backward(upstream, saved):
        kept, first_res, slope, second_res = saved
        grad_second, grad_y, gain_bias = run(
            norm_back_kernel,
            [piece_f, piece_h, shape((2, width), f32)],
            (upstream, second_res, gain[1:2]),
            0,
            "second_norm_back",
        )
        far = swap(grad_y, across)
        near = swap(grad_y, beside)
        far_near = swap(far, beside)
        args = (grad_y, far, near, far_near, slope, up, down)
        keep, send = run(feed_back_kernel, [pair_f, pair_h], args, 2 * feed_macs, "feed_back")
        keep, send = run(halves_kernel, [piece_f, piece_h], (swap(send, beside), keep), 0, "halves")
        args = (swap(send, across), keep, grad_second, first_res, gain[0:1], gain_bias)
        grad_first, grad_branch = run(
            norm_back_sum_kernel,
            [piece_f, shape((part + EXTRA_ROWS, width), bf16)],
            args,
            0,
            "first_norm_back",
        )
        branch = grad_branch[:part]
        args = (branch, swap(branch, beside), w_own, w_far, o_own, o_far, *kept)
        flops = 2 * weights_macs + 10 * scores_macs
        keep, send = run(attend_back_kernel, [piece_f, piece_h], args, flops, "attend_back")
        args = (swap(send, beside), keep, grad_first)
        grad_entry = run(entry_grad_kernel, [piece_h], args, 0, "entry_grad")[0]
        return grad_entry, (grad_y, far), grad_branch

    sections = [(0, 1), (1, 0)]
    middle = lax.ppermute(forward(entry_input, False), "section", sections)
    entry = jnp.where(section == 0, entry_input, middle)
    output, kept, first, first_res, slope, second_res = forward(entry, True)
    saved = (kept, first_res, slope, second_res)
    middle = lax.ppermute(backward(cotangent, saved)[0], "section", sections)
    grad_entry, grad_y, branch = backward(jnp.where(section == 1, cotangent, middle), saved)

    wide = groups in (2, 4)
    count = groups if wide else 1

    def gather(pair):
        pair = jnp.stack(pair)
        mine = lax.all_gather(pair, "dp") if wide else pair[None]
        return mine, swap(mine, beside)

    seg_line = jnp.where(b == 0, seg_own[:part], seg_own[part:]).astype(bf16)
    seg_line = jnp.pad(seg_line[None], ((0, EXTRA_ROWS - 1), (0, width - part)))
    entry_long = jnp.concatenate([entry, seg_line])
    entries = [
        item.reshape(2 * count, part + EXTRA_ROWS, width)
        for item in gather((entry_long, swap(entry_long, across)))
    ]
    firsts = [item.reshape(-1, width) for item in gather(first)]
    grads_y = [item.reshape(-1, width) for item in gather(grad_y)]

    seg_all = jnp.concatenate([item[:, part, :part] for item in entries], 1).astype(f32)
    args = (*entries, w_own, b_own, seg_all[:, None, :], seg_all[:, :, None])
    outs = [
        shape((2 * count, 3, length, local), bf16),
        shape((2 * count, heads, length, length), bf16),
        shape((2 * count, length, local), bf16),
    ]
    attended = run(
        attend_all_kernel,
        outs,
        args,
        2 * count * (weights_macs + 2 * scores_macs),
        "attend_all",
        grid=(2 * count,),
        in_specs=[leading(args[0], 1)] * 2
        + [whole(w_own), whole(b_own), leading(args[4], 1), leading(args[5], 1)],
        out_specs=[leading(item, 1) for item in outs],
    )

    block = 2 * part
    tall = firsts[0].shape[0]
    units = shape((tall, hidden_local), bf16)
    acts = [
        run(
            feed_all_kernel,
            [units, units],
            (item, up, up_bias),
            tall * width * hidden_local * 2,
            "feed_all",
            grid=(tall // block,),
            in_specs=[leading(item, block), whole(up), whole(up_bias)],
            out_specs=[leading(units, block)] * 2,
        )
        for item in firsts
    ]
    args = (firsts[0], grads_y[0], *acts[0], firsts[1], grads_y[1], *acts[1], down)
    outs = [
        shape((width, hidden_local), f32),
        shape((1, hidden_local), f32),
        shape((hidden_local, width), f32),
        shape((1, width), f32),
    ]
    g_up, g_up_b, g_down, g_down_b = run(
        feed_grads_kernel,
        outs,
        args,
        2 * tall * width * hidden_local * 6,
        "feed_grads",
        mib=28,
        grid=(tall // block,),
        in_specs=[leading(item, block) for item in args[:8]] + [whole(down)],
        out_specs=[whole(item) for item in outs],
    )

    outs = [
        shape((3, width, local), f32),
        shape((2, local), f32),
        shape((local, width), f32),
        shape((1, width), f32),
        shape((4, width), f32),
    ]
    sums = []
    for step in range(count):
        if step == 0:
            piece = branch
        else:
            piece = lax.ppermute(branch, "dp", [(i, i ^ step) for i in range(groups)])
        far = swap(piece, across)
        args = (*entries, piece, swap(piece, beside), far, swap(far, beside), o_own, *attended, *sums)
        args = ((lax.axis_index("dp") ^ step if wide else jnp.int32(0)).reshape(1), *args)

        def picked(item):
            rest = len(item.shape) - 1
            return pl.BlockSpec((2,) + item.shape[1:], lambda i, group: (group[0],) + (0,) * rest)

        def fixed(item):
            rest = len(item.shape)
            return pl.BlockSpec(item.shape, lambda i, group: (0,) * rest)

        specs = [picked(item) for item in args[1:3]] + [fixed(item) for item in args[3:8]]
        specs += [picked(item) for item in args[8:11]] + [fixed(item) for item in args[11:]]
        sums = run(
            attend_grads_kernel,
            outs,
            args,
            2 * (weights_macs + 5 * scores_macs),
            "attend_grads",
            grid_spec=pltpu.PrefetchScalarGridSpec(
                num_scalar_prefetch=1,
                grid=(1,),
                in_specs=specs,
                out_specs=[fixed(item) for item in outs],
            ),
            input_output_aliases={11 + i: i for i in range(len(sums))},
        )
    g_w, g_b, g_out, g_out_b, small = sums
    totals = (g_w, g_b, g_out, g_up, g_up_b, g_down)
    if not wide:
        totals = [lax.psum(item.astype(bf16), "dp").astype(f32) for item in totals]
        g_out_b, g_down_b, small = lax.psum((g_out_b, g_down_b, small), "dp")
    g_w, g_b, g_out, g_up, g_up_b, g_down = totals
    return (
        blocks_of(output)[None],
        blocks_of(grad_entry)[None],
        jnp.transpose(g_w, (1, 0, 2))[None],
        g_b[None],
        g_out[None],
        g_out_b,
        jnp.stack([small[0], small[2]])[None],
        jnp.stack([small[1], small[3]])[None],
        g_up[None],
        g_up_b,
        g_down[None],
        g_down_b,
    )


def solution(mesh):
    return jax.shard_map(
        shards,
        mesh=mesh,
        in_specs=(
            P("dp", "tensor", None),
            P("dp", None),
            P("dp", "tensor", None),
            P("section", None, None, "tensor"),
            P("section", None, "tensor"),
            P("section", "tensor", None),
            P("section", None),
            P("section", None, None),
            P("section", None, None),
            P("section", None, "tensor"),
            P("section", "tensor"),
            P("section", "tensor", None),
            P("section", None),
        ),
        out_specs=(
            P("section", "dp", "tensor", None),
            P("section", "dp", "tensor", None),
            P("section", None, None, "tensor"),
            P("section", None, "tensor"),
            P("section", "tensor", None),
            P("section", None),
            P("section", None, None),
            P("section", None, None),
            P("section", None, "tensor"),
            P("section", "tensor"),
            P("section", "tensor", None),
            P("section", None),
        ),
        check_vma=False,
    )
```

```python
import functools

import jax
import jax.numpy as jnp
from jax import lax
from jax.experimental import pallas as pl
from jax.experimental.pallas import tpu as pltpu
from jax.sharding import PartitionSpec as P

HEAD_DIM = 64
EPSILON = 1e-06
BIG_NEGATIVE = -1e30
MIB = 1024 * 1024
EXTRA_ROWS = 16
GAIN, SHIFT, OUT_BIAS, UP_BIAS, DOWN_BIAS, QV_OWN, QV_FAR, TABLE_ROWS = 0, 2, 4, 5, 6, 7, 9, 16
SQRT_HALF = 0.7071067811865476
INV_SQRT_TAU = 0.3989422804014327

f32 = jnp.float32
bf16 = jnp.bfloat16


def dot_nn(left, right):
    return lax.dot_general(left, right, (((1,), (0,)), ((), ())), preferred_element_type=f32)


def dot_nt(left, right):
    return lax.dot_general(left, right, (((1,), (1,)), ((), ())), preferred_element_type=f32)


def dot_tn(left, right):
    return lax.dot_general(left, right, (((0,), (0,)), ((), ())), preferred_element_type=f32)


def shape(dims, kind):
    return jax.ShapeDtypeStruct(dims, kind)


def run(kernel, outs, args, us, name, mib=16, after=(), grid=None, in_specs=None, out_specs=None,
        scalars=0, aliases=None):
    count = len(args)
    if in_specs is None:
        in_specs = [pl.BlockSpec(memory_space=pltpu.VMEM)] * count
    if out_specs is None:
        out_specs = [pl.BlockSpec(memory_space=pltpu.VMEM)] * len(outs)
    waits = [pl.BlockSpec(memory_space=pl.ANY)] * len(after)

    def body(*refs):
        kernel(*refs[:count], *refs[count + len(after) :])

    moved = sum(item.size * item.dtype.itemsize for item in (*args, *outs))
    return pl.pallas_call(
        body,
        out_shape=outs,
        grid_spec=pltpu.PrefetchScalarGridSpec(
            num_scalar_prefetch=scalars,
            grid=grid or (),
            in_specs=[*in_specs, *waits],
            out_specs=out_specs,
        ),
        name=name,
        input_output_aliases=aliases or {},
        compiler_params=pltpu.CompilerParams(vmem_limit_bytes=mib * MIB),
        cost_estimate=pl.CostEstimate(
            flops=int(us * 1.15e9), bytes_accessed=moved, transcendentals=0
        ),
    )(*args, *after)


def heads_forward(rows, w, table, line, same):
    local = w.shape[-1]
    query = dot_nn(rows, w[0]) + table[line : line + 1, :local]
    query = (query.astype(bf16) * HEAD_DIM**-0.5).astype(bf16)
    key = dot_nn(rows, w[1]).astype(bf16)
    value = (dot_nn(rows, w[2]) + table[line + 1 : line + 2, :local]).astype(bf16)
    probs, mixed = [], []
    for start in range(0, query.shape[1], HEAD_DIM):
        head = slice(start, start + HEAD_DIM)
        scores = jnp.where(same, dot_nt(query[:, head], key[:, head]), BIG_NEGATIVE)
        weights = jnp.exp(scores - jnp.max(scores, -1, keepdims=True))
        total = jnp.sum(weights, -1, keepdims=True)
        low = (weights * (1.0 / total)).astype(bf16)
        probs.append(low)
        mixed.append(dot_nn(low, value[:, head]).astype(bf16))
    return query, key, value, probs, jnp.concatenate(mixed, 1)


def heads_backward(query, key, value, probs, grad_mixed):
    parts = [], [], []
    for number, low in enumerate(probs):
        head = slice(number * HEAD_DIM, (number + 1) * HEAD_DIM)
        upstream = grad_mixed[:, head]
        wide = low.astype(f32)
        product = wide * dot_nt(upstream, value[:, head])
        scores = (product - wide * jnp.sum(product, -1, keepdims=True)).astype(bf16)
        parts[0].append((dot_nn(scores, key[:, head]) * HEAD_DIM**-0.5).astype(bf16))
        parts[1].append(dot_tn(scores, query[:, head]).astype(bf16))
        parts[2].append(dot_tn(low, upstream).astype(bf16))
    return [jnp.concatenate(part, 1) for part in parts]


def attend_kernel(
    own, other, w_own, w_far, o_own, o_far, table, seg_row, seg_col, *outs
):
    keep, send = outs[:2]
    rows = jnp.concatenate([own[...], other[...]], 0)
    same = seg_col[...] == seg_row[...]
    total = None
    for group, (w, out) in enumerate(((w_own, o_own), (w_far, o_far))):
        query, key, value, probs, mixed = heads_forward(rows, w, table, QV_OWN + 2 * group, same)
        if len(outs) > 2:
            qkv, kept = outs[2:]
            qkv[group, 0], qkv[group, 1], qkv[group, 2] = query, key, value
            for number, low in enumerate(probs):
                kept[group, number] = low
        term = dot_nn(mixed, out[...])
        total = term if total is None else total + term
    half = own.shape[0]
    keep[...] = own[...].astype(f32) + (total[:half] + table[OUT_BIAS : OUT_BIAS + 1])
    send[...] = total[half:].astype(bf16)


def attend_back_kernel(own, other, w_own, w_far, o_own, o_far, qkv, kept, residual, keep, send):
    half = own.shape[0] - EXTRA_ROWS
    rows = jnp.concatenate([own[:half], other[:half]], 0)
    total = None
    for group, (w, out) in enumerate(((w_own, o_own), (w_far, o_far))):
        grad_mixed = dot_nt(rows, out[...]).astype(bf16)
        probs = [kept[group, number] for number in range(kept.shape[1])]
        parts = heads_backward(qkv[group, 0], qkv[group, 1], qkv[group, 2], probs, grad_mixed)
        for number, part in enumerate(parts):
            term = dot_nt(part, w[number])
            total = term if total is None else total + term
    keep[...] = total[:half] + residual[...]
    send[...] = total[half:].astype(bf16)


def standard(values):
    centred = values - jnp.mean(values, -1, keepdims=True)
    spread = lax.rsqrt(jnp.mean(centred * centred, -1, keepdims=True) + EPSILON)
    return centred * spread, spread


def norm_kernel(which, arrived, kept, table, *outs):
    summed = arrived[...].astype(f32) + kept[...]
    gain, shift = table[GAIN + which : GAIN + which + 1], table[SHIFT + which : SHIFT + which + 1]
    outs[0][...] = (standard(summed)[0] * gain + shift).astype(bf16)
    if len(outs) > 1:
        outs[1][...] = summed


def norm_grads(values, gain, upstream):
    normal, spread = standard(values)
    scaled = upstream * gain
    along = jnp.mean(scaled * normal, -1, keepdims=True)
    grad = (scaled - jnp.mean(scaled, -1, keepdims=True) - normal * along) * spread
    return grad, jnp.sum(upstream * normal, 0, keepdims=True), jnp.sum(upstream, 0, keepdims=True)


def norm_back_kernel(upstream, values, table, grad, low, gain_bias):
    result, grad_gain, grad_shift = norm_grads(
        values[...], table[GAIN + 1 : GAIN + 2], upstream[...].astype(f32)
    )
    grad[...] = result
    low[...] = result.astype(bf16)
    gain_bias[0:1] = grad_gain
    gain_bias[1:2] = grad_shift


def norm_back_sum_kernel(arrived, kept, values, table, others, grad, low):
    upstream = arrived[...].astype(f32) + kept[...]
    result, grad_gain, grad_shift = norm_grads(values[...], table[GAIN : GAIN + 1], upstream)
    rows = result.shape[0]
    grad[...] = result
    low[0:rows] = result.astype(bf16)
    small = jnp.concatenate([grad_gain, grad_shift, others[0:2]], 0)
    high = small.astype(bf16)
    rest = (small - high.astype(f32)).astype(bf16)
    blank = jnp.zeros((EXTRA_ROWS - 8, result.shape[1]), bf16)
    low[rows : rows + EXTRA_ROWS] = jnp.concatenate([high, rest, blank], 0)


def feed_kernel(one, two, three, four, up, down, table, keep, send, *saved):
    part = one.shape[0]
    rows = jnp.concatenate([one[...], two[...], three[...], four[...]], 0)
    hidden = dot_nn(rows, up[...]) + table[UP_BIAS : UP_BIAS + 1]
    phi = 0.5 * (1.0 + lax.erf(hidden * SQRT_HALF))
    if saved:
        slope = phi + hidden * (jnp.exp(-0.5 * hidden * hidden) * INV_SQRT_TAU)
        saved[0][...] = slope.astype(bf16)
    total = dot_nn((hidden * phi).astype(bf16), down[...])
    keep[:part] = one[...].astype(f32) + (total[:part] + table[DOWN_BIAS : DOWN_BIAS + 1])
    keep[part:] = total[part : 2 * part]
    send[...] = total[2 * part :].astype(bf16)


def feed_back_kernel(one, two, three, four, slope, up, down, residual, keep, send):
    part = one.shape[0]
    rows = jnp.concatenate([one[...], two[...], three[...], four[...]], 0)
    hidden = (dot_nt(rows, down[...]) * slope[...].astype(f32)).astype(bf16)
    total = dot_nt(hidden, up[...])
    keep[:part] = total[:part] + residual[...]
    keep[part:] = total[part : 2 * part]
    send[...] = total[2 * part :].astype(bf16)


def halves_kernel(arrived, kept, keep, send):
    part = keep.shape[0]
    total = arrived[...].astype(f32) + kept[...]
    keep[...] = total[:part]
    send[...] = total[part:].astype(bf16)


def entry_grad_kernel(arrived, kept, low):
    low[...] = (arrived[...].astype(f32) + kept[...]).astype(bf16)


def copy_kernel(source, target):
    target[...] = source[...]


def pair_kernel(*refs):
    for number, ref in enumerate(refs[:-1]):
        refs[-1][number] = ref[...]


def group_forward(entry, w, table, seg_row, seg_col):
    local, length = w.shape[1], entry.shape[0] // 2
    bias = jnp.transpose(table[QV_OWN : QV_OWN + 2, :local])
    query = ((dot_nt(w[0], entry) + bias[:, 0:1]).astype(bf16) * HEAD_DIM**-0.5).astype(bf16)
    key = dot_nt(w[1], entry).astype(bf16)
    value = (dot_nt(w[2], entry) + bias[:, 1:2]).astype(bf16)
    probs, mixed = [], []
    for seq in range(2):
        span = slice(length * seq, length * (seq + 1))
        same = seg_col[seq] == seg_row[seq]
        for start in range(0, local, HEAD_DIM):
            head = slice(start, start + HEAD_DIM)
            scores = jnp.where(same, dot_tn(key[head, span], query[head, span]), BIG_NEGATIVE)
            weights = jnp.exp(scores - jnp.max(scores, 0, keepdims=True))
            weights = weights * (1.0 / jnp.sum(weights, 0, keepdims=True))
            probs.append(weights.astype(bf16))
            mixed.append(dot_nn(value[head, span], probs[-1]).astype(bf16))
    heads = len(probs) // 2
    columns = [jnp.concatenate(mixed[heads * seq : heads * (seq + 1)], 0) for seq in range(2)]
    return query, key, value, probs, jnp.concatenate(columns, 1)


def attend_group_kernel(one, two, three, four, w, table, seg_row, seg_col, lines, kept):
    entry = jnp.concatenate([one[...], two[...], three[...], four[...]], 0)
    *parts, probs, mixed = group_forward(entry, w, table, seg_row, seg_col)
    for number, item in enumerate((*parts, mixed)):
        lines[number] = item
    for number, item in enumerate(probs):
        kept[number] = item


def unpack_kernel(total, g_w, g_out, small):
    local = g_out.shape[0]
    for number in range(3):
        g_w[number] = total[local * number : local * (number + 1)].astype(f32)
    g_out[...] = total[3 * local : 4 * local].astype(f32)
    rest = total[4 * local :].astype(f32)
    small[...] = rest + jnp.concatenate([rest[7:], rest[:7]], 0)


def attend_grads_kernel(*refs):
    lines, kept, out, total = refs[8:]
    entry = jnp.concatenate([item[...] for item in refs[:4]], 0)
    pieces = [item[...] for item in refs[4:8]]
    part = refs[0].shape[0]
    local = out.shape[0]
    query, key, value, mixed = (lines[number] for number in range(4))
    probs = [kept[number] for number in range(kept.shape[0])]
    branch = jnp.concatenate([item[:part] for item in pieces], 0)
    grad_mixed = dot_nt(out[...], branch).astype(bf16)
    columns = []
    heads = len(probs) // 2
    for seq in range(2):
        span = slice(2 * part * seq, 2 * part * (seq + 1))
        rows = [], [], []
        for number in range(heads):
            head = slice(HEAD_DIM * number, HEAD_DIM * (number + 1))
            low = probs[heads * seq + number]
            q, k, v, upstream = (item[head, span] for item in (query, key, value, grad_mixed))
            wide = low.astype(f32)
            grads = wide * dot_tn(v, upstream)
            grads = (grads - wide * jnp.sum(grads, 0, keepdims=True)).astype(bf16)
            rows[0].append((dot_nn(k, grads) * HEAD_DIM**-0.5).astype(bf16))
            rows[1].append(dot_nt(q, grads).astype(bf16))
            rows[2].append(dot_nt(upstream, low).astype(bf16))
        columns.append([jnp.concatenate(item, 0) for item in rows])
    parts = [jnp.concatenate(pair, 1) for pair in zip(*columns)]
    for number, item in enumerate(parts):
        total[local * number : local * (number + 1)] = dot_nn(item, entry).astype(bf16)
    total[3 * local : 4 * local] = dot_nn(mixed, branch).astype(bf16)
    ones = jnp.ones((8, entry.shape[0]), bf16)
    blank = jnp.zeros((2, entry.shape[1] - local), f32)
    sums = jnp.concatenate([dot_nt(ones, parts[0])[:1], dot_nt(ones, parts[2])[:1]], 0)
    small = sum(item[part:].astype(f32) for item in pieces)
    sums = [jnp.concatenate([sums, blank], 1), dot_nn(ones, branch)[:1], small[:4] + small[4:8]]
    sums = jnp.concatenate(sums, 0)
    high = sums.astype(bf16)
    rest = (sums - high.astype(f32)).astype(bf16)
    blank = jnp.zeros((EXTRA_ROWS - 14, sums.shape[1]), bf16)
    total[4 * local : 4 * local + EXTRA_ROWS] = jnp.concatenate([high, rest, blank], 0)


def feed_grads_kernel(*refs):
    up, down, table, g_up, g_up_b, g_down, g_down_b = refs[4:]

    @pl.when(pl.program_id(0) == 0)
    def _():
        g_up[...] = jnp.zeros_like(g_up)
        g_up_b[...] = jnp.zeros_like(g_up_b)
        g_down[...] = jnp.zeros_like(g_down)
        g_down_b[...] = jnp.zeros_like(g_down_b)

    first, grad = (jnp.concatenate([refs[i][...], refs[i + 2][...]], 0) for i in range(2))
    hidden = dot_nn(first, up[...]) + table[UP_BIAS : UP_BIAS + 1]
    phi = 0.5 * (1.0 + lax.erf(hidden * SQRT_HALF))
    slope = phi + hidden * (jnp.exp(-0.5 * hidden * hidden) * INV_SQRT_TAU)
    act = (hidden * phi).astype(bf16)
    grad_hidden = (dot_nt(grad, down[...]) * slope).astype(bf16)
    g_down[...] += dot_tn(act, grad)
    g_up[...] += dot_tn(first, grad_hidden)
    g_up_b[...] += jnp.sum(grad_hidden.astype(f32), 0, keepdims=True)
    g_down_b[...] += jnp.sum(grad.astype(f32), 0, keepdims=True)


def whole(item):
    return pl.BlockSpec(item.shape, lambda step: (0,) * len(item.shape))


def leading(item, count):
    rest = len(item.shape) - 1
    return pl.BlockSpec((count,) + item.shape[1:], lambda step: (step,) + (0,) * rest)


def shards(
    block_input,
    segments,
    out_grad,
    query_key_value_weight,
    b_qv,
    attention_output_weight,
    attention_out_bias,
    ln_gain,
    ln_bias,
    up_projection_weight,
    up_proj_bias,
    down_projection_weight,
    down_proj_bias,
):
    assert lax.axis_size("tensor") == 4 and block_input.shape[0] == 2
    groups = lax.axis_size("dp")
    section = lax.axis_index("section")
    place = lax.axis_index("tensor")
    a, b = place // 2, place % 2
    seqs, quarter, width = block_input.shape
    length = segments.shape[1]
    part = length // 2
    local = query_key_value_weight.shape[3]
    hidden_local = up_projection_weight.shape[2]
    heads = local // HEAD_DIM

    beside = [(i, i ^ 1) for i in range(4)]
    across = [(i, i ^ 2) for i in range(4)]
    turn = [(2 * s + c, 2 * c + s) for s in range(2) for c in range(2)]
    twist = [(2 * s + c, 2 * c + 1 - s) for s in range(2) for c in range(2)]
    untwist = [(target, source) for source, target in twist]

    def swap(value, pairs):
        return lax.ppermute(value, "tensor", pairs)

    def pieces_of(block):
        one = swap(jnp.where(b == 0, block[0], block[1]), turn)
        two = swap(jnp.where(b == 0, block[1], block[0]), untwist)
        return jnp.where(a == 0, jnp.concatenate([one, two]), jnp.concatenate([two, one]))

    def blocks_of(piece):
        one = swap(jnp.where(a == 0, piece[:quarter], piece[quarter:]), turn)
        two = swap(jnp.where(a == 0, piece[quarter:], piece[:quarter]), twist)
        return jnp.where(b == 0, jnp.stack([one, two]), jnp.stack([two, one]))

    w_own = jnp.transpose(query_key_value_weight[0], (1, 0, 2))
    w_turned = jnp.transpose(query_key_value_weight[0], (1, 2, 0))
    o_own = attention_output_weight[0]
    b_own = b_qv[0].astype(f32)
    entry_input = pieces_of(block_input)
    w_far = swap(w_own, across)
    o_far = swap(o_own, across)
    cotangent = pieces_of(out_grad)
    up, down = up_projection_weight[0], down_projection_weight[0]

    def lines(item):
        return jnp.pad(item, ((0, 0), (0, width - item.shape[1])))

    b_own = lines(b_qv[0])
    table = [ln_gain[0], ln_bias[0], attention_out_bias, lines(up_proj_bias), down_proj_bias]
    table += [b_own, swap(b_own, across)]
    table = jnp.concatenate(table).astype(f32)
    table = jnp.pad(table, ((0, TABLE_ROWS - table.shape[0]), (0, 0)))

    seg_own = segments[0] if seqs == 1 else jnp.where(a == 0, segments[0], segments[1])
    seg_own = seg_own.astype(f32)
    seg_turned = jnp.where(b == 0, seg_own, jnp.roll(seg_own, part))
    seg_row, seg_col = seg_turned[None, :], seg_turned[:, None]
    seg_far = jnp.where(a == 0, segments[1], segments[0]).astype(f32)
    seg_far = jnp.where(b == 0, seg_far, jnp.roll(seg_far, part))
    seg_both = jnp.stack([seg_turned, seg_far])

    piece_f, piece_h = shape((part, width), f32), shape((part, width), bf16)
    pair_f, pair_h = shape((2 * part, width), f32), shape((2 * part, width), bf16)

    def forward(entry, save, after=()):
        outs = [piece_f, piece_h]
        if save:
            outs += [
                shape((2, 3, length, local), bf16),
                shape((2, heads, length, length), bf16),
            ]
        args = (entry, swap(entry, beside), w_own, w_far, o_own, o_far, table, seg_row, seg_col)
        keep, branch, *kept = run(attend_kernel, outs, args, 3.0, "attend")
        args = (swap(branch, beside), keep, table)
        first, *first_res = run(
            functools.partial(norm_kernel, 0), [piece_h] + [piece_f] * save, args, 0, "first_norm"
        )
        far = swap(first, across)
        near, far_near = swap(first, beside), swap(far, beside)
        outs = [pair_f, pair_h] + [shape((4 * part, hidden_local), bf16)] * save
        args = (first, far, near, far_near, up, down, table)
        keep, send, *slope = run(feed_kernel, outs, args, 1.6, "feed")
        keep, send = run(halves_kernel, [piece_f, piece_h], (swap(send, beside), keep), 0, "halves")
        args = (swap(send, across), keep, table)
        output, *second_res = run(
            functools.partial(norm_kernel, 1),
            [piece_h] + [piece_f] * save,
            args,
            0,
            "second_norm",
            after=after,
        )
        if not save:
            return output
        return output, (kept, first_res[0], slope[0], second_res[0]), (first, far), branch

    def backward(upstream, saved, after=(), later=()):
        kept, first_res, slope, second_res = saved
        grad_second, grad_y, gain_bias = run(
            norm_back_kernel,
            [piece_f, piece_h, shape((2, width), f32)],
            (upstream, second_res, table),
            0,
            "second_norm_back",
            after=after,
        )
        far = swap(grad_y, across)
        near, far_near = swap(grad_y, beside), swap(far, beside)
        args = (grad_y, far, near, far_near, slope, up, down, grad_second)
        keep, gate = run(feed_back_kernel, [pair_f, pair_h], args, 1.5, "feed_back")
        keep, send = run(halves_kernel, [piece_f, piece_h], (swap(gate, beside), keep), 0, "halves")
        args = (swap(send, across), keep, first_res, table, gain_bias)
        outs = [piece_f, shape((part + EXTRA_ROWS, width), bf16)]
        grad_first, branch = run(norm_back_sum_kernel, outs, args, 0, "first_norm_back", after=later)
        near = swap(branch, beside)

        args = (branch, near, w_own, w_far, o_own, o_far, *kept, grad_first)
        keep, send = run(attend_back_kernel, [piece_f, piece_h], args, 3.2, "attend_back")
        args = (swap(send, beside), keep)
        grad_entry = run(entry_grad_kernel, [piece_h], args, 0, "entry_grad")[0]
        return grad_entry, (grad_y, far), branch, near, send

    wide = groups in (2, 4)
    count = groups if wide else 1

    def gather(pair):
        mine = lax.all_gather(pair, "dp") if wide else pair[None]
        return mine, swap(mine, beside)

    sections = [(0, 1), (1, 0)]
    middle = lax.ppermute(forward(entry_input, False, (cotangent,)), "section", sections)
    entry = jnp.where(section == 0, entry_input, middle)
    output, saved, first_pair, token = forward(entry, True)

    entry_far = swap(entry, across)
    entries = (entry, swap(entry, beside), entry_far, swap(entry_far, beside))

    grad = backward(cotangent, saved)[0]
    firsts = [item.reshape(-1, width) for item in gather(jnp.stack(first_pair))]
    layer_output = blocks_of(output)
    args = (*entries, w_turned, table, seg_both[:, None, :], seg_both[:, :, None])
    outs = [shape((4, local, 2 * length), bf16), shape((2 * heads, length, length), bf16)]
    attended = run(attend_group_kernel, outs, args, 4.0, "attend_group", mib=24)
    middle = lax.ppermute(grad, "section", sections)
    grad_entry, grad_y, branch, near, token = backward(
        jnp.where(section == 1, cotangent, middle), saved, (layer_output, firsts[0]), tuple(attended[:1])
    )
    grad_y = jnp.stack(grad_y)
    grad_y = lax.all_gather(grad_y, "dp") if wide else grad_y[None]

    far = run(copy_kernel, [shape(branch.shape, bf16)], (swap(branch, across),), 0, "far", after=(token,))[0]
    total = run(
        attend_grads_kernel,
        [shape((4 * local + EXTRA_ROWS, width), bf16)],
        (*entries, branch, near, far, swap(far, beside), *attended, o_own),
        5.0,
        "attend_grads",
        mib=56,
    )[0]
    local_total = total
    total = lax.psum(total, "dp")
    grad_y = run(copy_kernel, [shape(grad_y.shape, bf16)], (grad_y,), 0, "gathered", after=(local_total,))[0]
    grads_y = [item.reshape(-1, width) for item in (grad_y, swap(grad_y, beside))]
    args = (firsts[0], grads_y[0], firsts[1], grads_y[1], up, down, table)
    outs = [
        shape((width, hidden_local), f32),
        shape((1, hidden_local), f32),
        shape((hidden_local, width), f32),
        shape((1, width), f32),
    ]
    block, tall = 2 * part, firsts[0].shape[0]
    g_up, g_up_b, g_down, g_down_b = run(
        feed_grads_kernel,
        outs,
        args,
        5.0,
        "feed_grads",
        mib=56,
        grid=(tall // block,),
        in_specs=[leading(item, block) for item in args[:4]] + [whole(item) for item in args[4:]],
        out_specs=[whole(item) for item in outs],
    )
    held = run(copy_kernel, [piece_h], (grad_entry,), 0, "held", after=(g_down,))[0]
    input_grad = blocks_of(held)
    if not wide:
        g_up, g_up_b, g_down = [
            lax.psum(item.astype(bf16), "dp").astype(f32) for item in (g_up, g_up_b, g_down)
        ]
        g_down_b = lax.psum(g_down_b, "dp")
    outs = [shape((3, local, width), f32), shape((local, width), f32), shape((EXTRA_ROWS, width), f32)]
    g_w, g_out, small = run(unpack_kernel, outs, (total,), 1.0, "unpack", after=(g_down, input_grad))
    g_b, g_out_b, small = small[:2, :local], small[2:3], small[3:7]
    return (
        layer_output[None],
        input_grad[None],
        jnp.transpose(g_w, (2, 0, 1))[None],
        g_b[None],
        g_out[None],
        g_out_b,
        jnp.stack([small[0], small[2]])[None],
        jnp.stack([small[1], small[3]])[None],
        g_up[None],
        g_up_b,
        g_down[None],
        g_down_b,
    )


def solution(mesh):
    return jax.shard_map(
        shards,
        mesh=mesh,
        in_specs=(
            P("dp", "tensor", None),
            P("dp", None),
            P("dp", "tensor", None),
            P("section", None, None, "tensor"),
            P("section", None, "tensor"),
            P("section", "tensor", None),
            P("section", None),
            P("section", None, None),
            P("section", None, None),
            P("section", None, "tensor"),
            P("section", "tensor"),
            P("section", "tensor", None),
            P("section", None),
        ),
        out_specs=(
            P("section", "dp", "tensor", None),
            P("section", "dp", "tensor", None),
            P("section", None, None, "tensor"),
            P("section", None, "tensor"),
            P("section", "tensor", None),
            P("section", None),
            P("section", None, None),
            P("section", None, None),
            P("section", None, "tensor"),
            P("section", "tensor"),
            P("section", "tensor", None),
            P("section", None),
        ),
        check_vma=False,
    )
```

```python
import functools

import jax
import jax.numpy as jnp
from jax import lax
from jax.experimental import pallas as pl
from jax.experimental.pallas import tpu as pltpu
from jax.sharding import PartitionSpec as P

HEAD_DIM = 64
EPSILON = 1e-06
BIG_NEGATIVE = -1e30
MIB = 1024 * 1024
EXTRA_ROWS = 16
GAIN, SHIFT, OUT_BIAS, UP_BIAS, DOWN_BIAS, QV_OWN, QV_FAR, TABLE_ROWS = 0, 2, 4, 5, 6, 7, 9, 16
SQRT_HALF = 0.7071067811865476
INV_SQRT_TAU = 0.3989422804014327

f32 = jnp.float32
bf16 = jnp.bfloat16


def dot_nn(left, right):
    return lax.dot_general(left, right, (((1,), (0,)), ((), ())), preferred_element_type=f32)


def dot_nt(left, right):
    return lax.dot_general(left, right, (((1,), (1,)), ((), ())), preferred_element_type=f32)


def dot_tn(left, right):
    return lax.dot_general(left, right, (((0,), (0,)), ((), ())), preferred_element_type=f32)


def shape(dims, kind):
    return jax.ShapeDtypeStruct(dims, kind)


def run(kernel, outs, args, us, name, mib=16, after=(), grid=None, in_specs=None, out_specs=None,
        scalars=0, aliases=None):
    count = len(args)
    if in_specs is None:
        in_specs = [pl.BlockSpec(memory_space=pltpu.VMEM)] * count
    if out_specs is None:
        out_specs = [pl.BlockSpec(memory_space=pltpu.VMEM)] * len(outs)
    waits = [pl.BlockSpec(memory_space=pl.ANY)] * len(after)

    def body(*refs):
        kernel(*refs[:count], *refs[count + len(after) :])

    moved = sum(item.size * item.dtype.itemsize for item in (*args, *outs))
    return pl.pallas_call(
        body,
        out_shape=outs,
        grid_spec=pltpu.PrefetchScalarGridSpec(
            num_scalar_prefetch=scalars,
            grid=grid or (),
            in_specs=[*in_specs, *waits],
            out_specs=out_specs,
        ),
        name=name,
        input_output_aliases=aliases or {},
        compiler_params=pltpu.CompilerParams(vmem_limit_bytes=mib * MIB),
        cost_estimate=pl.CostEstimate(
            flops=int(us * 1.15e9), bytes_accessed=moved, transcendentals=0
        ),
    )(*args, *after)


def quarters(ref):
    local = ref.shape[0] // 4
    return [ref[local * number : local * (number + 1)] for number in range(4)]


def heads_forward(entry, w, table, line, same):
    local, length = w[0].shape[0], entry.shape[0] // len(same)
    bias = jnp.transpose(table[line : line + 2, :local])
    query = ((dot_nt(w[0], entry) + bias[:, 0:1]).astype(bf16) * HEAD_DIM**-0.5).astype(bf16)
    key = dot_nt(w[1], entry).astype(bf16)
    value = (dot_nt(w[2], entry) + bias[:, 1:2]).astype(bf16)
    probs, columns = [], []
    for seq, visible in enumerate(same):
        span = slice(length * seq, length * (seq + 1))
        mixed = []
        for start in range(0, local, HEAD_DIM):
            head = slice(start, start + HEAD_DIM)
            scores = jnp.where(visible, dot_tn(key[head, span], query[head, span]), BIG_NEGATIVE)
            weights = jnp.exp(scores - jnp.max(scores, 0, keepdims=True))
            weights = weights * (1.0 / jnp.sum(weights, 0, keepdims=True))
            probs.append(weights.astype(bf16))
            mixed.append(dot_nn(value[head, span], probs[-1]).astype(bf16))
        columns.append(jnp.concatenate(mixed, 0))
    return query, key, value, probs, jnp.concatenate(columns, 1)


def heads_backward(query, key, value, probs, grad_mixed):
    heads = query.shape[0] // HEAD_DIM
    length = probs[0].shape[0]
    columns = []
    for seq in range(len(probs) // heads):
        span = slice(length * seq, length * (seq + 1))
        rows = [], [], []
        for number in range(heads):
            head = slice(HEAD_DIM * number, HEAD_DIM * (number + 1))
            low = probs[heads * seq + number]
            q, k, v, upstream = (item[head, span] for item in (query, key, value, grad_mixed))
            wide = low.astype(f32)
            grads = wide * dot_tn(v, upstream)
            grads = (grads - wide * jnp.sum(grads, 0, keepdims=True)).astype(bf16)
            rows[0].append((dot_nn(k, grads) * HEAD_DIM**-0.5).astype(bf16))
            rows[1].append(dot_nt(q, grads).astype(bf16))
            rows[2].append(dot_nt(upstream, low).astype(bf16))
        columns.append([jnp.concatenate(item, 0) for item in rows])
    return [jnp.concatenate(pair, 1) for pair in zip(*columns)]


def attend_kernel(own, other, w_own, w_far, table, seg_row, seg_col, *outs):
    keep, send = outs[:2]
    rows = jnp.concatenate([own[...], other[...]], 0)
    same = seg_col[...] == seg_row[...]
    total = None
    for group, ref in enumerate((w_own, w_far)):
        *w, out = quarters(ref)
        *parts, probs, mixed = heads_forward(rows, w, table, QV_OWN + 2 * group, [same])
        if len(outs) > 2:
            for number, item in enumerate(parts):
                outs[2][group, number, : out.shape[0]] = item
            for number, item in enumerate(probs):
                outs[2][group, number, out.shape[0] :] = item
        term = dot_tn(mixed, out)
        total = term if total is None else total + term
    half = own.shape[0]
    keep[...] = own[...].astype(f32) + (total[:half] + table[OUT_BIAS : OUT_BIAS + 1])
    send[...] = total[half:].astype(bf16)


def attend_back_kernel(own, other, w_own, w_far, kept, residual, keep, send):
    half = own.shape[0] - EXTRA_ROWS
    rows = jnp.concatenate([own[:half], other[:half]], 0)
    total = None
    for group, ref in enumerate((w_own, w_far)):
        *w, out = quarters(ref)
        local = out.shape[0]
        grad_mixed = dot_nt(out, rows).astype(bf16)
        lines = [kept[group, number, :local] for number in range(3)]
        probs = [kept[group, number, local:] for number in range(3)]
        parts = heads_backward(*lines, probs, grad_mixed)
        for number, part in enumerate(parts):
            term = dot_tn(part, w[number])
            total = term if total is None else total + term
    keep[...] = total[:half] + residual[...]
    send[...] = total[half:].astype(bf16)


def standard(values):
    centred = values - jnp.mean(values, -1, keepdims=True)
    spread = lax.rsqrt(jnp.mean(centred * centred, -1, keepdims=True) + EPSILON)
    return centred * spread, spread


def norm_kernel(which, arrived, kept, table, *outs):
    summed = arrived[...].astype(f32) + kept[...]
    gain, shift = table[GAIN + which : GAIN + which + 1], table[SHIFT + which : SHIFT + which + 1]
    outs[0][...] = (standard(summed)[0] * gain + shift).astype(bf16)
    if len(outs) > 1:
        outs[1][...] = summed


def norm_grads(values, gain, upstream):
    normal, spread = standard(values)
    scaled = upstream * gain
    along = jnp.mean(scaled * normal, -1, keepdims=True)
    grad = (scaled - jnp.mean(scaled, -1, keepdims=True) - normal * along) * spread
    return grad, jnp.sum(upstream * normal, 0, keepdims=True), jnp.sum(upstream, 0, keepdims=True)


def norm_back_kernel(upstream, values, table, grad, low, gain_bias):
    result, grad_gain, grad_shift = norm_grads(
        values[...], table[GAIN + 1 : GAIN + 2], upstream[...].astype(f32)
    )
    grad[...] = result
    low[...] = result.astype(bf16)
    gain_bias[0:1] = grad_gain
    gain_bias[1:2] = grad_shift


def norm_back_sum_kernel(arrived, kept, values, table, others, grad, low):
    upstream = arrived[...].astype(f32) + kept[...]
    result, grad_gain, grad_shift = norm_grads(values[...], table[GAIN : GAIN + 1], upstream)
    rows = result.shape[0]
    grad[...] = result
    low[0:rows] = result.astype(bf16)
    small = jnp.concatenate([grad_gain, grad_shift, others[0:2]], 0)
    high = small.astype(bf16)
    rest = (small - high.astype(f32)).astype(bf16)
    blank = jnp.zeros((EXTRA_ROWS - 8, result.shape[1]), bf16)
    low[rows : rows + EXTRA_ROWS] = jnp.concatenate([high, rest, blank], 0)


def feed_kernel(one, two, three, four, weights, table, keep, send, *saved):
    part = one.shape[0]
    rows = jnp.concatenate([one[...], two[...], three[...], four[...]], 0)
    hidden = dot_nn(rows, weights[0]) + table[UP_BIAS : UP_BIAS + 1]
    phi = 0.5 * (1.0 + lax.erf(hidden * SQRT_HALF))
    if saved:
        slope = phi + hidden * (jnp.exp(-0.5 * hidden * hidden) * INV_SQRT_TAU)
        saved[0][...] = slope.astype(bf16)
    total = dot_nn((hidden * phi).astype(bf16), weights[1])
    keep[:part] = one[...].astype(f32) + (total[:part] + table[DOWN_BIAS : DOWN_BIAS + 1])
    keep[part:] = total[part : 2 * part]
    send[...] = total[2 * part :].astype(bf16)


def feed_back_kernel(one, two, three, four, slope, weights, residual, keep, send):
    part = one.shape[0]
    rows = jnp.concatenate([one[...], two[...], three[...], four[...]], 0)
    hidden = (dot_nt(rows, weights[1]) * slope[...].astype(f32)).astype(bf16)
    total = dot_nt(hidden, weights[0])
    keep[:part] = total[:part] + residual[...]
    keep[part:] = total[part : 2 * part]
    send[...] = total[2 * part :].astype(bf16)


def halves_kernel(arrived, kept, keep, send):
    part = keep.shape[0]
    total = arrived[...].astype(f32) + kept[...]
    keep[...] = total[:part]
    send[...] = total[part:].astype(bf16)


def entry_grad_kernel(arrived, kept, low):
    low[...] = (arrived[...].astype(f32) + kept[...]).astype(bf16)


def copy_kernel(source, target):
    target[...] = source[...]


def pair_kernel(*refs):
    for number, ref in enumerate(refs[:-1]):
        refs[-1][number] = ref[...]


def attend_group_kernel(one, two, three, four, w_own, table, seg_row, seg_col, lines, kept):
    entry = jnp.concatenate([one[...], two[...], three[...], four[...]], 0)
    same = [seg_col[seq] == seg_row[seq] for seq in range(2)]
    *parts, probs, mixed = heads_forward(entry, quarters(w_own)[:3], table, QV_OWN, same)
    for number, item in enumerate((*parts, mixed)):
        lines[number] = item
    for number, item in enumerate(probs):
        kept[number] = item


def unpack_kernel(total, g_w, g_out, small):
    local = g_out.shape[0]
    for number in range(3):
        g_w[number] = total[local * number : local * (number + 1)].astype(f32)
    g_out[...] = total[3 * local : 4 * local].astype(f32)
    rest = total[4 * local :].astype(f32)
    small[...] = rest + jnp.concatenate([rest[7:], rest[:7]], 0)


def attend_grads_kernel(*refs):
    lines, kept, w_own, total = refs[8:]
    out = quarters(w_own)[3]
    entry = jnp.concatenate([item[...] for item in refs[:4]], 0)
    pieces = [item[...] for item in refs[4:8]]
    part = refs[0].shape[0]
    local = out.shape[0]
    query, key, value, mixed = (lines[number] for number in range(4))
    probs = [kept[number] for number in range(kept.shape[0])]
    branch = jnp.concatenate([item[:part] for item in pieces], 0)
    grad_mixed = dot_nt(out, branch).astype(bf16)
    parts = heads_backward(query, key, value, probs, grad_mixed)
    for number, item in enumerate(parts):
        total[local * number : local * (number + 1)] = dot_nn(item, entry).astype(bf16)
    total[3 * local : 4 * local] = dot_nn(mixed, branch).astype(bf16)
    ones = jnp.ones((8, entry.shape[0]), bf16)
    blank = jnp.zeros((2, entry.shape[1] - local), f32)
    sums = jnp.concatenate([dot_nt(ones, parts[0])[:1], dot_nt(ones, parts[2])[:1]], 0)
    small = sum(item[part:].astype(f32) for item in pieces)
    sums = [jnp.concatenate([sums, blank], 1), dot_nn(ones, branch)[:1], small[:4] + small[4:8]]
    sums = jnp.concatenate(sums, 0)
    high = sums.astype(bf16)
    rest = (sums - high.astype(f32)).astype(bf16)
    blank = jnp.zeros((EXTRA_ROWS - 14, sums.shape[1]), bf16)
    total[4 * local : 4 * local + EXTRA_ROWS] = jnp.concatenate([high, rest, blank], 0)


def feed_grads_kernel(*refs):
    weights, table, g_up, g_up_b, g_down, g_down_b = refs[4:]

    @pl.when(pl.program_id(0) == 0)
    def _():
        g_up[...] = jnp.zeros_like(g_up)
        g_up_b[...] = jnp.zeros_like(g_up_b)
        g_down[...] = jnp.zeros_like(g_down)
        g_down_b[...] = jnp.zeros_like(g_down_b)

    first, grad = (jnp.concatenate([refs[i][...], refs[i + 2][...]], 0) for i in range(2))
    hidden = dot_nn(first, weights[0]) + table[UP_BIAS : UP_BIAS + 1]
    phi = 0.5 * (1.0 + lax.erf(hidden * SQRT_HALF))
    slope = phi + hidden * (jnp.exp(-0.5 * hidden * hidden) * INV_SQRT_TAU)
    act = (hidden * phi).astype(bf16)
    grad_hidden = (dot_nt(grad, weights[1]) * slope).astype(bf16)
    g_down[...] += dot_tn(act, grad)
    g_up[...] += dot_tn(first, grad_hidden)
    g_up_b[...] += jnp.sum(grad_hidden.astype(f32), 0, keepdims=True)
    g_down_b[...] += jnp.sum(grad.astype(f32), 0, keepdims=True)


def whole(item):
    return pl.BlockSpec(item.shape, lambda step: (0,) * len(item.shape))


def leading(item, count):
    rest = len(item.shape) - 1
    return pl.BlockSpec((count,) + item.shape[1:], lambda step: (step,) + (0,) * rest)


def shards(
    block_input,
    segments,
    out_grad,
    query_key_value_weight,
    b_qv,
    attention_output_weight,
    attention_out_bias,
    ln_gain,
    ln_bias,
    up_projection_weight,
    up_proj_bias,
    down_projection_weight,
    down_proj_bias,
):
    assert lax.axis_size("tensor") == 4 and block_input.shape[0] == 2
    groups = lax.axis_size("dp")
    section = lax.axis_index("section")
    place = lax.axis_index("tensor")
    a, b = place // 2, place % 2
    seqs, quarter, width = block_input.shape
    length = segments.shape[1]
    part = length // 2
    local = query_key_value_weight.shape[3]
    hidden_local = up_projection_weight.shape[2]
    heads = local // HEAD_DIM

    beside = [(i, i ^ 1) for i in range(4)]
    across = [(i, i ^ 2) for i in range(4)]
    turn = [(2 * s + c, 2 * c + s) for s in range(2) for c in range(2)]
    twist = [(2 * s + c, 2 * c + 1 - s) for s in range(2) for c in range(2)]
    untwist = [(target, source) for source, target in twist]

    def swap(value, pairs):
        return lax.ppermute(value, "tensor", pairs)

    def pieces_of(block):
        one = swap(jnp.where(b == 0, block[0], block[1]), turn)
        two = swap(jnp.where(b == 0, block[1], block[0]), untwist)
        return jnp.where(a == 0, jnp.concatenate([one, two]), jnp.concatenate([two, one]))

    def blocks_of(piece):
        one = swap(jnp.where(a == 0, piece[:quarter], piece[quarter:]), turn)
        two = swap(jnp.where(a == 0, piece[quarter:], piece[:quarter]), twist)
        return jnp.where(b == 0, jnp.stack([one, two]), jnp.stack([two, one]))

    w_own = jnp.transpose(query_key_value_weight[0], (1, 2, 0)).reshape(3 * local, width)
    w_own = jnp.concatenate([w_own, attention_output_weight[0]])
    entry_input = pieces_of(block_input)
    w_far = swap(w_own, across)
    cotangent = pieces_of(out_grad)
    weights = jnp.concatenate([up_projection_weight, down_projection_weight])

    def lines(item):
        return jnp.pad(item, ((0, 0), (0, width - item.shape[1])))

    b_own = lines(b_qv[0])
    table = [ln_gain[0], ln_bias[0], attention_out_bias, lines(up_proj_bias), down_proj_bias]
    table += [b_own, swap(b_own, across)]
    table = jnp.concatenate(table).astype(f32)
    table = jnp.pad(table, ((0, TABLE_ROWS - table.shape[0]), (0, 0)))

    seg_own = segments[0] if seqs == 1 else jnp.where(a == 0, segments[0], segments[1])
    seg_own = seg_own.astype(f32)
    seg_turned = jnp.where(b == 0, seg_own, jnp.roll(seg_own, part))
    seg_row, seg_col = seg_turned[None, :], seg_turned[:, None]
    seg_far = jnp.where(a == 0, segments[1], segments[0]).astype(f32)
    seg_far = jnp.where(b == 0, seg_far, jnp.roll(seg_far, part))
    seg_both = jnp.stack([seg_turned, seg_far])

    piece_f, piece_h = shape((part, width), f32), shape((part, width), bf16)
    pair_f, pair_h = shape((2 * part, width), f32), shape((2 * part, width), bf16)

    def forward(entry, save, before=(), after=()):
        outs = [piece_f, piece_h]
        if save:
            outs.append(shape((2, 3, local + length, length), bf16))
        args = (entry, swap(entry, beside), w_own, w_far, table, seg_row, seg_col)
        keep, branch, *kept = run(attend_kernel, outs, args, 3.0, "attend", after=before)
        args = (swap(branch, beside), keep, table)
        first, *first_res = run(
            functools.partial(norm_kernel, 0),
            [piece_h] + [piece_f] * save,
            args,
            0,
            "first_norm",
            after=after,
        )
        far = swap(first, across)
        near, far_near = swap(first, beside), swap(far, beside)
        outs = [pair_f, pair_h] + [shape((4 * part, hidden_local), bf16)] * save
        args = (first, far, near, far_near, weights, table)
        keep, send, *slope = run(feed_kernel, outs, args, 1.6, "feed")
        keep, send = run(halves_kernel, [piece_f, piece_h], (swap(send, beside), keep), 0, "halves")
        args = (swap(send, across), keep, table)
        output, *second_res = run(
            functools.partial(norm_kernel, 1),
            [piece_h] + [piece_f] * save,
            args,
            0,
            "second_norm",
        )
        if not save:
            return output
        return output, (kept, first_res[0], slope[0], second_res[0]), (first, far), branch

    def backward(upstream, saved, after=(), later=()):
        kept, first_res, slope, second_res = saved
        grad_second, grad_y, gain_bias = run(
            norm_back_kernel,
            [piece_f, piece_h, shape((2, width), f32)],
            (upstream, second_res, table),
            0,
            "second_norm_back",
            after=after,
        )
        far = swap(grad_y, across)
        near, far_near = swap(grad_y, beside), swap(far, beside)
        args = (grad_y, far, near, far_near, slope, weights, grad_second)
        keep, gate = run(feed_back_kernel, [pair_f, pair_h], args, 1.5, "feed_back")
        keep, send = run(halves_kernel, [piece_f, piece_h], (swap(gate, beside), keep), 0, "halves")
        args = (swap(send, across), keep, first_res, table, gain_bias)
        outs = [piece_f, shape((part + EXTRA_ROWS, width), bf16)]
        grad_first, branch = run(norm_back_sum_kernel, outs, args, 0, "first_norm_back")
        near = swap(branch, beside)

        args = (branch, near, w_own, w_far, *kept, grad_first)
        keep, send = run(attend_back_kernel, [piece_f, piece_h], args, 3.2, "attend_back", after=later)
        args = (swap(send, beside), keep)
        grad_entry = run(entry_grad_kernel, [piece_h], args, 0, "entry_grad")[0]
        return grad_entry, (grad_y, far), branch, near, send

    wide = groups in (2, 4)
    count = groups if wide else 1

    def gather(pair):
        mine = lax.all_gather(pair, "dp") if wide else pair[None]
        return mine, swap(mine, beside)

    sections = [(0, 1), (1, 0)]
    middle = lax.ppermute(forward(entry_input, False), "section", sections)
    entry = jnp.where(section == 0, entry_input, middle)
    entry_far = swap(entry, across)
    output, saved, first_pair, _ = forward(entry, True, (cotangent,), (entry_far,))

    entries = (entry, swap(entry, beside), entry_far, swap(entry_far, beside))

    firsts = [item.reshape(-1, width) for item in gather(jnp.stack(first_pair))]
    grad = backward(cotangent, saved, later=(firsts[0],))[0]
    layer_output = blocks_of(output)
    args = (*entries, w_own, table, seg_both[:, None, :], seg_both[:, :, None])
    outs = [shape((4, local, 2 * length), bf16), shape((2 * heads, length, length), bf16)]
    attended = run(attend_group_kernel, outs, args, 4.0, "attend_group", mib=24)
    middle = lax.ppermute(grad, "section", sections)
    grad_entry, grad_y, branch, near, token = backward(
        jnp.where(section == 1, cotangent, middle), saved, (layer_output, attended[0])
    )
    outs = [shape((2, part, width), bf16)]
    grad_y = run(pair_kernel, outs, grad_y, 0, "grad_y_pair")[0]
    grad_y = lax.all_gather(grad_y, "dp") if wide else grad_y[None]

    far = run(copy_kernel, [shape(branch.shape, bf16)], (swap(branch, across),), 0, "far", after=(token,))[0]
    total = run(
        attend_grads_kernel,
        [shape((4 * local + EXTRA_ROWS, width), bf16)],
        (*entries, branch, near, far, swap(far, beside), *attended, w_own),
        5.0,
        "attend_grads",
        mib=24,
    )[0]
    local_total = total
    total = lax.psum(total, "dp")
    grad_y = run(copy_kernel, [shape(grad_y.shape, bf16)], (grad_y,), 0, "gathered", after=(local_total,))[0]
    grads_y = [item.reshape(-1, width) for item in (grad_y, swap(grad_y, beside))]
    args = (firsts[0], grads_y[0], firsts[1], grads_y[1], weights, table)
    outs = [
        shape((width, hidden_local), f32),
        shape((1, hidden_local), f32),
        shape((hidden_local, width), f32),
        shape((1, width), f32),
    ]
    block, tall = 2 * part, firsts[0].shape[0]
    g_up, g_up_b, g_down, g_down_b = run(
        feed_grads_kernel,
        outs,
        args,
        5.0,
        "feed_grads",
        mib=56,
        grid=(tall // block,),
        in_specs=[leading(item, block) for item in args[:4]] + [whole(item) for item in args[4:]],
        out_specs=[whole(item) for item in outs],
    )
    held = run(copy_kernel, [piece_h], (grad_entry,), 0, "held", after=(g_down,))[0]
    input_grad = blocks_of(held)
    if not wide:
        g_up, g_up_b, g_down = [
            lax.psum(item.astype(bf16), "dp").astype(f32) for item in (g_up, g_up_b, g_down)
        ]
        g_down_b = lax.psum(g_down_b, "dp")
    outs = [shape((3, local, width), f32), shape((local, width), f32), shape((EXTRA_ROWS, width), f32)]
    g_w, g_out, small = run(unpack_kernel, outs, (total,), 1.0, "unpack", after=(g_down, input_grad))
    g_b, g_out_b, small = small[:2, :local], small[2:3], small[3:7]
    return (
        layer_output[None],
        input_grad[None],
        jnp.transpose(g_w, (2, 0, 1))[None],
        g_b[None],
        g_out[None],
        g_out_b,
        jnp.stack([small[0], small[2]])[None],
        jnp.stack([small[1], small[3]])[None],
        g_up[None],
        g_up_b,
        g_down[None],
        g_down_b,
    )


def solution(mesh):
    return jax.shard_map(
        shards,
        mesh=mesh,
        in_specs=(
            P("dp", "tensor", None),
            P("dp", None),
            P("dp", "tensor", None),
            P("section", None, None, "tensor"),
            P("section", None, "tensor"),
            P("section", "tensor", None),
            P("section", None),
            P("section", None, None),
            P("section", None, None),
            P("section", None, "tensor"),
            P("section", "tensor"),
            P("section", "tensor", None),
            P("section", None),
        ),
        out_specs=(
            P("section", "dp", "tensor", None),
            P("section", "dp", "tensor", None),
            P("section", None, None, "tensor"),
            P("section", None, "tensor"),
            P("section", "tensor", None),
            P("section", None),
            P("section", None, None),
            P("section", None, None),
            P("section", None, "tensor"),
            P("section", "tensor"),
            P("section", "tensor", None),
            P("section", None),
        ),
        check_vma=False,
    )
```

```python
import functools

import jax
import jax.numpy as jnp
from jax import lax
from jax.experimental import pallas as pl
from jax.experimental.pallas import tpu as pltpu
from jax.sharding import PartitionSpec as P

HEAD_DIM = 64
EPSILON = 1e-06
BIG_NEGATIVE = -1e30
MIB = 1024 * 1024
EXTRA_ROWS = 16
GAIN, SHIFT, OUT_BIAS, UP_BIAS, DOWN_BIAS, QV_OWN, QV_FAR, TABLE_ROWS = 0, 2, 4, 5, 6, 7, 9, 16
SQRT_HALF = 0.7071067811865476
INV_SQRT_TAU = 0.3989422804014327

f32 = jnp.float32
bf16 = jnp.bfloat16


def dot_nn(left, right):
    return lax.dot_general(left, right, (((1,), (0,)), ((), ())), preferred_element_type=f32)


def dot_nt(left, right):
    return lax.dot_general(left, right, (((1,), (1,)), ((), ())), preferred_element_type=f32)


def dot_tn(left, right):
    return lax.dot_general(left, right, (((0,), (0,)), ((), ())), preferred_element_type=f32)


def shape(dims, kind):
    return jax.ShapeDtypeStruct(dims, kind)


def run(kernel, outs, args, us, name, mib=16, after=(), grid=None, in_specs=None, out_specs=None,
        scalars=0, aliases=None):
    count = len(args)
    if in_specs is None:
        in_specs = [pl.BlockSpec(memory_space=pltpu.VMEM)] * count
    if out_specs is None:
        out_specs = [pl.BlockSpec(memory_space=pltpu.VMEM)] * len(outs)
    waits = [pl.BlockSpec(memory_space=pl.ANY)] * len(after)

    def body(*refs):
        kernel(*refs[:count], *refs[count + len(after) :])

    moved = sum(item.size * item.dtype.itemsize for item in (*args, *outs))
    return pl.pallas_call(
        body,
        out_shape=outs,
        grid_spec=pltpu.PrefetchScalarGridSpec(
            num_scalar_prefetch=scalars,
            grid=grid or (),
            in_specs=[*in_specs, *waits],
            out_specs=out_specs,
        ),
        name=name,
        input_output_aliases=aliases or {},
        compiler_params=pltpu.CompilerParams(vmem_limit_bytes=mib * MIB),
        cost_estimate=pl.CostEstimate(
            flops=int(us * 1.15e9), bytes_accessed=moved, transcendentals=0
        ),
    )(*args, *after)


def quarters(ref):
    local = ref.shape[0] // 4
    return [ref[local * number : local * (number + 1)] for number in range(4)]


def heads_forward(entry, w, table, line, same):
    local, length = w[0].shape[0], entry.shape[0] // len(same)
    bias = jnp.transpose(table[line : line + 2, :local])
    query = ((dot_nt(w[0], entry) + bias[:, 0:1]).astype(bf16) * HEAD_DIM**-0.5).astype(bf16)
    key = dot_nt(w[1], entry).astype(bf16)
    value = (dot_nt(w[2], entry) + bias[:, 1:2]).astype(bf16)
    probs, columns = [], []
    for seq, visible in enumerate(same):
        span = slice(length * seq, length * (seq + 1))
        mixed = []
        for start in range(0, local, HEAD_DIM):
            head = slice(start, start + HEAD_DIM)
            scores = jnp.where(visible, dot_tn(key[head, span], query[head, span]), BIG_NEGATIVE)
            weights = jnp.exp(scores - jnp.max(scores, 0, keepdims=True))
            weights = weights * (1.0 / jnp.sum(weights, 0, keepdims=True))
            probs.append(weights.astype(bf16))
            mixed.append(dot_nn(value[head, span], probs[-1]).astype(bf16))
        columns.append(jnp.concatenate(mixed, 0))
    return query, key, value, probs, jnp.concatenate(columns, 1)


def heads_backward(query, key, value, probs, grad_mixed):
    heads = query.shape[0] // HEAD_DIM
    length = probs[0].shape[0]
    columns = []
    for seq in range(len(probs) // heads):
        span = slice(length * seq, length * (seq + 1))
        rows = [], [], []
        for number in range(heads):
            head = slice(HEAD_DIM * number, HEAD_DIM * (number + 1))
            low = probs[heads * seq + number]
            q, k, v, upstream = (item[head, span] for item in (query, key, value, grad_mixed))
            wide = low.astype(f32)
            grads = wide * dot_tn(v, upstream)
            grads = (grads - wide * jnp.sum(grads, 0, keepdims=True)).astype(bf16)
            rows[0].append((dot_nn(k, grads) * HEAD_DIM**-0.5).astype(bf16))
            rows[1].append(dot_nt(q, grads).astype(bf16))
            rows[2].append(dot_nt(upstream, low).astype(bf16))
        columns.append([jnp.concatenate(item, 0) for item in rows])
    return [jnp.concatenate(pair, 1) for pair in zip(*columns)]


def attend_own_kernel(own, other, w_own, table, seg_row, seg_col, total):
    rows = jnp.concatenate([own[...], other[...]], 0)
    *w, out = quarters(w_own)
    mixed = heads_forward(rows, w, table, QV_OWN, [seg_col[...] == seg_row[...]])[-1]
    total[...] = dot_tn(mixed, out)


def attend_kernel(early, own, other, w_own, w_far, table, seg_row, seg_col, *outs):
    keep, send = outs[:2]
    rows = jnp.concatenate([own[...], other[...]], 0)
    same = seg_col[...] == seg_row[...]
    total = w_own[...] if early else None
    for group, ref in enumerate((w_own, w_far)):
        if early and group == 0:
            continue
        *w, out = quarters(ref)
        *parts, probs, mixed = heads_forward(rows, w, table, QV_OWN + 2 * group, [same])
        if len(outs) > 2:
            for number, item in enumerate(parts):
                outs[2][group, number, : out.shape[0]] = item
            for number, item in enumerate(probs):
                outs[2][group, number, out.shape[0] :] = item
        term = dot_tn(mixed, out)
        total = term if total is None else total + term
    half = own.shape[0]
    keep[...] = own[...].astype(f32) + (total[:half] + table[OUT_BIAS : OUT_BIAS + 1])
    send[...] = total[half:].astype(bf16)


def attend_back_kernel(own, other, w_own, w_far, kept, residual, keep, send):
    half = own.shape[0] - EXTRA_ROWS
    rows = jnp.concatenate([own[:half], other[:half]], 0)
    total = None
    for group, ref in enumerate((w_own, w_far)):
        *w, out = quarters(ref)
        local = out.shape[0]
        grad_mixed = dot_nt(out, rows).astype(bf16)
        lines = [kept[group, number, :local] for number in range(3)]
        probs = [kept[group, number, local:] for number in range(3)]
        parts = heads_backward(*lines, probs, grad_mixed)
        for number, part in enumerate(parts):
            term = dot_tn(part, w[number])
            total = term if total is None else total + term
    keep[...] = total[:half] + residual[...]
    send[...] = total[half:].astype(bf16)


def standard(values):
    centred = values - jnp.mean(values, -1, keepdims=True)
    spread = lax.rsqrt(jnp.mean(centred * centred, -1, keepdims=True) + EPSILON)
    return centred * spread, spread


def norm_kernel(which, arrived, kept, table, *outs):
    summed = arrived[...].astype(f32) + kept[...]
    gain, shift = table[GAIN + which : GAIN + which + 1], table[SHIFT + which : SHIFT + which + 1]
    outs[0][...] = (standard(summed)[0] * gain + shift).astype(bf16)
    if len(outs) > 1:
        outs[1][...] = summed


def norm_grads(values, gain, upstream):
    normal, spread = standard(values)
    scaled = upstream * gain
    along = jnp.mean(scaled * normal, -1, keepdims=True)
    grad = (scaled - jnp.mean(scaled, -1, keepdims=True) - normal * along) * spread
    return grad, jnp.sum(upstream * normal, 0, keepdims=True), jnp.sum(upstream, 0, keepdims=True)


def norm_back_kernel(upstream, values, table, grad, low, gain_bias):
    result, grad_gain, grad_shift = norm_grads(
        values[...], table[GAIN + 1 : GAIN + 2], upstream[...].astype(f32)
    )
    grad[...] = result
    low[...] = result.astype(bf16)
    gain_bias[0:1] = grad_gain
    gain_bias[1:2] = grad_shift


def norm_back_sum_kernel(arrived, kept, values, table, others, grad, low):
    upstream = arrived[...].astype(f32) + kept[...]
    result, grad_gain, grad_shift = norm_grads(values[...], table[GAIN : GAIN + 1], upstream)
    rows = result.shape[0]
    grad[...] = result
    low[0:rows] = result.astype(bf16)
    small = jnp.concatenate([grad_gain, grad_shift, others[0:2]], 0)
    high = small.astype(bf16)
    rest = (small - high.astype(f32)).astype(bf16)
    blank = jnp.zeros((EXTRA_ROWS - 8, result.shape[1]), bf16)
    low[rows : rows + EXTRA_ROWS] = jnp.concatenate([high, rest, blank], 0)


def feed_kernel(one, two, three, four, weights, table, keep, send, *saved):
    part = one.shape[0]
    rows = jnp.concatenate([one[...], two[...], three[...], four[...]], 0)
    hidden = dot_nn(rows, weights[0]) + table[UP_BIAS : UP_BIAS + 1]
    phi = 0.5 * (1.0 + lax.erf(hidden * SQRT_HALF))
    if saved:
        slope = phi + hidden * (jnp.exp(-0.5 * hidden * hidden) * INV_SQRT_TAU)
        saved[0][...] = slope.astype(bf16)
    total = dot_nn((hidden * phi).astype(bf16), weights[1])
    keep[:part] = one[...].astype(f32) + (total[:part] + table[DOWN_BIAS : DOWN_BIAS + 1])
    keep[part:] = total[part : 2 * part]
    send[...] = total[2 * part :].astype(bf16)


def feed_back_kernel(one, two, three, four, slope, weights, residual, keep, send):
    part = one.shape[0]
    rows = jnp.concatenate([one[...], two[...], three[...], four[...]], 0)
    hidden = (dot_nt(rows, weights[1]) * slope[...].astype(f32)).astype(bf16)
    total = dot_nt(hidden, weights[0])
    keep[:part] = total[:part] + residual[...]
    keep[part:] = total[part : 2 * part]
    send[...] = total[2 * part :].astype(bf16)


def halves_kernel(arrived, kept, keep, send):
    part = keep.shape[0]
    total = arrived[...].astype(f32) + kept[...]
    keep[...] = total[:part]
    send[...] = total[part:].astype(bf16)


def entry_grad_kernel(arrived, kept, low):
    low[...] = (arrived[...].astype(f32) + kept[...]).astype(bf16)


def copy_kernel(source, target):
    target[...] = source[...]


def pair_kernel(*refs):
    for number, ref in enumerate(refs[:-1]):
        refs[-1][number] = ref[...]


def attend_group_kernel(one, two, three, four, w_own, table, seg_row, seg_col, lines, kept):
    entry = jnp.concatenate([one[...], two[...], three[...], four[...]], 0)
    same = [seg_col[seq] == seg_row[seq] for seq in range(2)]
    *parts, probs, mixed = heads_forward(entry, quarters(w_own)[:3], table, QV_OWN, same)
    for number, item in enumerate((*parts, mixed)):
        lines[number] = item
    for number, item in enumerate(probs):
        kept[number] = item


def unpack_kernel(total, g_w, g_out, g_b, g_out_b, g_gain, g_shift):
    local = g_out.shape[0]
    for number in range(3):
        g_w[number] = total[local * number : local * (number + 1)].astype(f32)
    g_out[...] = total[3 * local : 4 * local].astype(f32)
    rest = total[4 * local :].astype(f32)
    rest = rest[:7] + rest[7:14]
    g_b[...] = rest[:2, :local]
    g_out_b[...] = rest[2:3]
    g_gain[...] = jnp.concatenate([rest[3:4], rest[5:6]], 0)
    g_shift[...] = jnp.concatenate([rest[4:5], rest[6:7]], 0)


def attend_grads_kernel(*refs):
    lines, kept, w_own, total = refs[8:]
    out = quarters(w_own)[3]
    entry = jnp.concatenate([item[...] for item in refs[:4]], 0)
    pieces = [item[...] for item in refs[4:8]]
    part = refs[0].shape[0]
    local = out.shape[0]
    query, key, value, mixed = (lines[number] for number in range(4))
    probs = [kept[number] for number in range(kept.shape[0])]
    branch = jnp.concatenate([item[:part] for item in pieces], 0)
    grad_mixed = dot_nt(out, branch).astype(bf16)
    parts = heads_backward(query, key, value, probs, grad_mixed)
    for number, item in enumerate(parts):
        total[local * number : local * (number + 1)] = dot_nn(item, entry).astype(bf16)
    total[3 * local : 4 * local] = dot_nn(mixed, branch).astype(bf16)
    ones = jnp.ones((8, entry.shape[0]), bf16)
    blank = jnp.zeros((2, entry.shape[1] - local), f32)
    sums = jnp.concatenate([dot_nt(ones, parts[0])[:1], dot_nt(ones, parts[2])[:1]], 0)
    small = sum(item[part:].astype(f32) for item in pieces)
    sums = [jnp.concatenate([sums, blank], 1), dot_nn(ones, branch)[:1], small[:4] + small[4:8]]
    sums = jnp.concatenate(sums, 0)
    high = sums.astype(bf16)
    rest = (sums - high.astype(f32)).astype(bf16)
    blank = jnp.zeros((EXTRA_ROWS - 14, sums.shape[1]), bf16)
    total[4 * local : 4 * local + EXTRA_ROWS] = jnp.concatenate([high, rest, blank], 0)


def feed_grads_kernel(*refs):
    weights, table, g_up, g_up_b, g_down, g_down_b = refs[4:]

    @pl.when(pl.program_id(0) == 0)
    def _():
        g_up[...] = jnp.zeros_like(g_up)
        g_up_b[...] = jnp.zeros_like(g_up_b)
        g_down[...] = jnp.zeros_like(g_down)
        g_down_b[...] = jnp.zeros_like(g_down_b)

    first, grad = (jnp.concatenate([refs[i][...], refs[i + 2][...]], 0) for i in range(2))
    hidden = dot_nn(first, weights[0]) + table[UP_BIAS : UP_BIAS + 1]
    phi = 0.5 * (1.0 + lax.erf(hidden * SQRT_HALF))
    slope = phi + hidden * (jnp.exp(-0.5 * hidden * hidden) * INV_SQRT_TAU)
    act = (hidden * phi).astype(bf16)
    grad_hidden = (dot_nt(grad, weights[1]) * slope).astype(bf16)
    g_down[...] += dot_tn(act, grad)
    g_up[...] += dot_tn(first, grad_hidden)
    g_up_b[...] += jnp.sum(grad_hidden.astype(f32), 0, keepdims=True)
    g_down_b[...] += jnp.sum(grad.astype(f32), 0, keepdims=True)


def whole(item):
    return pl.BlockSpec(item.shape, lambda step: (0,) * len(item.shape))


def leading(item, count):
    rest = len(item.shape) - 1
    return pl.BlockSpec((count,) + item.shape[1:], lambda step: (step,) + (0,) * rest)


def shards(
    block_input,
    segments,
    out_grad,
    query_key_value_weight,
    b_qv,
    attention_output_weight,
    attention_out_bias,
    ln_gain,
    ln_bias,
    up_projection_weight,
    up_proj_bias,
    down_projection_weight,
    down_proj_bias,
):
    assert lax.axis_size("tensor") == 4 and block_input.shape[0] == 2
    groups = lax.axis_size("dp")
    section = lax.axis_index("section")
    place = lax.axis_index("tensor")
    a, b = place // 2, place % 2
    seqs, quarter, width = block_input.shape
    length = segments.shape[1]
    part = length // 2
    local = query_key_value_weight.shape[3]
    hidden_local = up_projection_weight.shape[2]
    heads = local // HEAD_DIM

    beside = [(i, i ^ 1) for i in range(4)]
    across = [(i, i ^ 2) for i in range(4)]
    turn = [(2 * s + c, 2 * c + s) for s in range(2) for c in range(2)]
    twist = [(2 * s + c, 2 * c + 1 - s) for s in range(2) for c in range(2)]
    untwist = [(target, source) for source, target in twist]

    def swap(value, pairs):
        return lax.ppermute(value, "tensor", pairs)

    def pieces_of(block):
        one = swap(jnp.where(b == 0, block[0], block[1]), turn)
        two = swap(jnp.where(b == 0, block[1], block[0]), untwist)
        return jnp.where(a == 0, jnp.concatenate([one, two]), jnp.concatenate([two, one]))

    def blocks_of(piece):
        one = swap(jnp.where(a == 0, piece[:quarter], piece[quarter:]), turn)
        two = swap(jnp.where(a == 0, piece[quarter:], piece[:quarter]), twist)
        return jnp.where(b == 0, jnp.stack([one, two]), jnp.stack([two, one]))

    w_own = jnp.transpose(query_key_value_weight[0], (1, 2, 0)).reshape(3 * local, width)
    w_own = jnp.concatenate([w_own, attention_output_weight[0]])
    entry_input = pieces_of(block_input)
    w_far = swap(w_own, across)
    cotangent = pieces_of(out_grad)
    weights = jnp.concatenate([up_projection_weight, down_projection_weight])

    def lines(item):
        return jnp.pad(item, ((0, 0), (0, width - item.shape[1])))

    b_own = lines(b_qv[0])
    table = [ln_gain[0], ln_bias[0], attention_out_bias, lines(up_proj_bias), down_proj_bias]
    table += [b_own, swap(b_own, across)]
    table = jnp.concatenate(table).astype(f32)
    table = jnp.pad(table, ((0, TABLE_ROWS - table.shape[0]), (0, 0)))

    seg_own = segments[0] if seqs == 1 else jnp.where(a == 0, segments[0], segments[1])
    seg_own = seg_own.astype(f32)
    seg_turned = jnp.where(b == 0, seg_own, jnp.roll(seg_own, part))
    seg_row, seg_col = seg_turned[None, :], seg_turned[:, None]
    seg_far = jnp.where(a == 0, segments[1], segments[0]).astype(f32)
    seg_far = jnp.where(b == 0, seg_far, jnp.roll(seg_far, part))
    seg_both = jnp.stack([seg_turned, seg_far])

    piece_f, piece_h = shape((part, width), f32), shape((part, width), bf16)
    pair_f, pair_h = shape((2 * part, width), f32), shape((2 * part, width), bf16)

    def forward(entry, save, before=(), after=()):
        outs = [piece_f, piece_h]
        if save:
            outs.append(shape((2, 3, local + length, length), bf16))
        near, first_part = swap(entry, beside), w_own
        if not save:
            args = (entry, near, w_own, table, seg_row, seg_col)
            first_part = run(attend_own_kernel, [pair_f], args, 2.0, "attend_own")[0]
        args = (entry, near, first_part, w_far, table, seg_row, seg_col)
        keep, branch, *kept = run(
            functools.partial(attend_kernel, not save), outs, args, 3.0, "attend", after=before
        )
        args = (swap(branch, beside), keep, table)
        first, *first_res = run(
            functools.partial(norm_kernel, 0),
            [piece_h] + [piece_f] * save,
            args,
            0,
            "first_norm",
            after=after,
        )
        far = swap(first, across)
        near, far_near = swap(first, beside), swap(far, beside)
        outs = [pair_f, pair_h] + [shape((4 * part, hidden_local), bf16)] * save
        args = (first, far, near, far_near, weights, table)
        keep, send, *slope = run(feed_kernel, outs, args, 1.6, "feed")
        keep, send = run(halves_kernel, [piece_f, piece_h], (swap(send, beside), keep), 0, "halves")
        args = (swap(send, across), keep, table)
        output, *second_res = run(
            functools.partial(norm_kernel, 1),
            [piece_h] + [piece_f] * save,
            args,
            0,
            "second_norm",
        )
        if not save:
            return output
        return output, (kept, first_res[0], slope[0], second_res[0]), (first, far), branch

    def backward(upstream, saved, after=(), later=()):
        kept, first_res, slope, second_res = saved
        grad_second, grad_y, gain_bias = run(
            norm_back_kernel,
            [piece_f, piece_h, shape((2, width), f32)],
            (upstream, second_res, table),
            0,
            "second_norm_back",
            after=after,
        )
        far = swap(grad_y, across)
        near, far_near = swap(grad_y, beside), swap(far, beside)
        args = (grad_y, far, near, far_near, slope, weights, grad_second)
        keep, gate = run(feed_back_kernel, [pair_f, pair_h], args, 1.5, "feed_back")
        keep, send = run(halves_kernel, [piece_f, piece_h], (swap(gate, beside), keep), 0, "halves")
        args = (swap(send, across), keep, first_res, table, gain_bias)
        outs = [piece_f, shape((part + EXTRA_ROWS, width), bf16)]
        grad_first, branch = run(norm_back_sum_kernel, outs, args, 0, "first_norm_back")
        near = swap(branch, beside)

        args = (branch, near, w_own, w_far, *kept, grad_first)
        keep, send = run(attend_back_kernel, [piece_f, piece_h], args, 3.2, "attend_back", after=later)
        args = (swap(send, beside), keep)
        grad_entry = run(entry_grad_kernel, [piece_h], args, 0, "entry_grad")[0]
        return grad_entry, (grad_y, far), branch, near, send

    wide = groups in (2, 4)
    count = groups if wide else 1

    def gather(pair):
        mine = lax.all_gather(pair, "dp") if wide else pair[None]
        return mine, swap(mine, beside)

    sections = [(0, 1), (1, 0)]
    middle = lax.ppermute(forward(entry_input, False), "section", sections)
    entry = jnp.where(section == 0, entry_input, middle)
    entry_far = swap(entry, across)
    output, saved, first_pair, _ = forward(entry, True, (cotangent,), (entry_far,))

    entries = (entry, swap(entry, beside), entry_far, swap(entry_far, beside))

    firsts = [item.reshape(-1, width) for item in gather(jnp.stack(first_pair))]
    grad = backward(cotangent, saved, later=(firsts[0],))[0]
    layer_output = blocks_of(output)
    args = (*entries, w_own, table, seg_both[:, None, :], seg_both[:, :, None])
    outs = [shape((4, local, 2 * length), bf16), shape((2 * heads, length, length), bf16)]
    attended = run(attend_group_kernel, outs, args, 4.0, "attend_group", mib=24)
    middle = lax.ppermute(grad, "section", sections)
    grad_entry, grad_y, branch, near, token = backward(
        jnp.where(section == 1, cotangent, middle), saved, (layer_output, attended[0])
    )
    outs = [shape((2, part, width), bf16)]
    grad_y = run(pair_kernel, outs, grad_y, 0, "grad_y_pair")[0]
    grad_y = lax.all_gather(grad_y, "dp") if wide else grad_y[None]

    far = run(copy_kernel, [shape(branch.shape, bf16)], (swap(branch, across),), 0, "far", after=(token,))[0]
    total = run(
        attend_grads_kernel,
        [shape((4 * local + EXTRA_ROWS, width), bf16)],
        (*entries, branch, near, far, swap(far, beside), *attended, w_own),
        5.0,
        "attend_grads",
        mib=24,
    )[0]
    local_total = total
    total = lax.psum(total, "dp")
    grad_y = run(copy_kernel, [shape(grad_y.shape, bf16)], (grad_y,), 0, "gathered", after=(local_total,))[0]
    grads_y = [item.reshape(-1, width) for item in (grad_y, swap(grad_y, beside))]
    args = (firsts[0], grads_y[0], firsts[1], grads_y[1], weights, table)
    outs = [
        shape((width, hidden_local), f32),
        shape((1, hidden_local), f32),
        shape((hidden_local, width), f32),
        shape((1, width), f32),
    ]
    block, tall = 2 * part, firsts[0].shape[0]
    g_up, g_up_b, g_down, g_down_b = run(
        feed_grads_kernel,
        outs,
        args,
        5.0,
        "feed_grads",
        mib=56,
        grid=(tall // block,),
        in_specs=[leading(item, block) for item in args[:4]] + [whole(item) for item in args[4:]],
        out_specs=[whole(item) for item in outs],
    )
    held = run(copy_kernel, [piece_h], (grad_entry,), 0, "held", after=(g_down,))[0]
    input_grad = blocks_of(held)
    if not wide:
        g_up, g_up_b, g_down = [
            lax.psum(item.astype(bf16), "dp").astype(f32) for item in (g_up, g_up_b, g_down)
        ]
        g_down_b = lax.psum(g_down_b, "dp")
    outs = [shape((3, local, width), f32), shape((local, width), f32), shape((2, local), f32)]
    outs += [shape((1, width), f32), shape((2, width), f32), shape((2, width), f32)]
    after = (g_down, input_grad)
    g_w, g_out, g_b, g_out_b, g_gain, g_shift = run(
        unpack_kernel, outs, (total,), 1.0, "unpack", after=after
    )
    return (
        layer_output[None],
        input_grad[None],
        jnp.transpose(g_w, (2, 0, 1))[None],
        g_b[None],
        g_out[None],
        g_out_b,
        g_gain[None],
        g_shift[None],
        g_up[None],
        g_up_b,
        g_down[None],
        g_down_b,
    )


def solution(mesh):
    return jax.shard_map(
        shards,
        mesh=mesh,
        in_specs=(
            P("dp", "tensor", None),
            P("dp", None),
            P("dp", "tensor", None),
            P("section", None, None, "tensor"),
            P("section", None, "tensor"),
            P("section", "tensor", None),
            P("section", None),
            P("section", None, None),
            P("section", None, None),
            P("section", None, "tensor"),
            P("section", "tensor"),
            P("section", "tensor", None),
            P("section", None),
        ),
        out_specs=(
            P("section", "dp", "tensor", None),
            P("section", "dp", "tensor", None),
            P("section", None, None, "tensor"),
            P("section", None, "tensor"),
            P("section", "tensor", None),
            P("section", None),
            P("section", None, None),
            P("section", None, None),
            P("section", None, "tensor"),
            P("section", "tensor"),
            P("section", "tensor", None),
            P("section", None),
        ),
        check_vma=False,
    )
```

```python
import functools

import jax
import jax.numpy as jnp
from jax import lax
from jax.experimental import pallas as pl
from jax.experimental.pallas import tpu as pltpu
from jax.sharding import PartitionSpec as P

HEAD_DIM = 64
EPSILON = 1e-06
BIG_NEGATIVE = -1e30
MIB = 1024 * 1024
EXTRA_ROWS = 16
GAIN, SHIFT, OUT_BIAS, UP_BIAS, DOWN_BIAS, QV_OWN, QV_FAR, TABLE_ROWS = 0, 2, 4, 5, 6, 7, 9, 16
SQRT_HALF = 0.7071067811865476
INV_SQRT_TAU = 0.3989422804014327

f32 = jnp.float32
bf16 = jnp.bfloat16


def dot_nn(left, right):
    return lax.dot_general(left, right, (((1,), (0,)), ((), ())), preferred_element_type=f32)


def dot_nt(left, right):
    return lax.dot_general(left, right, (((1,), (1,)), ((), ())), preferred_element_type=f32)


def dot_tn(left, right):
    return lax.dot_general(left, right, (((0,), (0,)), ((), ())), preferred_element_type=f32)


def shape(dims, kind):
    return jax.ShapeDtypeStruct(dims, kind)


def run(kernel, outs, args, us, name, mib=16, after=(), grid=None, in_specs=None, out_specs=None,
        scalars=0, aliases=None):
    count = len(args)
    if in_specs is None:
        in_specs = [pl.BlockSpec(memory_space=pltpu.VMEM)] * count
    if out_specs is None:
        out_specs = [pl.BlockSpec(memory_space=pltpu.VMEM)] * len(outs)
    waits = [pl.BlockSpec(memory_space=pl.ANY)] * len(after)

    def body(*refs):
        kernel(*refs[:count], *refs[count + len(after) :])

    moved = sum(item.size * item.dtype.itemsize for item in (*args, *outs))
    return pl.pallas_call(
        body,
        out_shape=outs,
        grid_spec=pltpu.PrefetchScalarGridSpec(
            num_scalar_prefetch=scalars,
            grid=grid or (),
            in_specs=[*in_specs, *waits],
            out_specs=out_specs,
        ),
        name=name,
        input_output_aliases=aliases or {},
        compiler_params=pltpu.CompilerParams(vmem_limit_bytes=mib * MIB),
        cost_estimate=pl.CostEstimate(
            flops=int(us * 1.15e9), bytes_accessed=moved, transcendentals=0
        ),
    )(*args, *after)


def quarters(ref):
    local = ref.shape[0] // 4
    return [ref[local * number : local * (number + 1)] for number in range(4)]


def heads_forward(entry, w, table, line, same):
    local, length = w[0].shape[0], entry.shape[0] // len(same)
    bias = jnp.transpose(table[line : line + 2, :local])
    query = ((dot_nt(w[0], entry) + bias[:, 0:1]).astype(bf16) * HEAD_DIM**-0.5).astype(bf16)
    key = dot_nt(w[1], entry).astype(bf16)
    value = (dot_nt(w[2], entry) + bias[:, 1:2]).astype(bf16)
    probs, columns = [], []
    for seq, visible in enumerate(same):
        span = slice(length * seq, length * (seq + 1))
        mixed = []
        for start in range(0, local, HEAD_DIM):
            head = slice(start, start + HEAD_DIM)
            scores = jnp.where(visible, dot_tn(key[head, span], query[head, span]), BIG_NEGATIVE)
            weights = jnp.exp(scores - jnp.max(scores, 0, keepdims=True))
            weights = weights * (1.0 / jnp.sum(weights, 0, keepdims=True))
            probs.append(weights.astype(bf16))
            mixed.append(dot_nn(value[head, span], probs[-1]).astype(bf16))
        columns.append(jnp.concatenate(mixed, 0))
    return query, key, value, probs, jnp.concatenate(columns, 1)


def heads_backward(query, key, value, probs, grad_mixed):
    heads = query.shape[0] // HEAD_DIM
    length = probs[0].shape[0]
    columns = []
    for seq in range(len(probs) // heads):
        span = slice(length * seq, length * (seq + 1))
        rows = [], [], []
        for number in range(heads):
            head = slice(HEAD_DIM * number, HEAD_DIM * (number + 1))
            low = probs[heads * seq + number]
            q, k, v, upstream = (item[head, span] for item in (query, key, value, grad_mixed))
            wide = low.astype(f32)
            grads = wide * dot_tn(v, upstream)
            grads = (grads - wide * jnp.sum(grads, 0, keepdims=True)).astype(bf16)
            rows[0].append((dot_nn(k, grads) * HEAD_DIM**-0.5).astype(bf16))
            rows[1].append(dot_nt(q, grads).astype(bf16))
            rows[2].append(dot_nt(upstream, low).astype(bf16))
        columns.append([jnp.concatenate(item, 0) for item in rows])
    return [jnp.concatenate(pair, 1) for pair in zip(*columns)]


def attend_own_kernel(own, other, w_own, table, seg_row, seg_col, total):
    rows = jnp.concatenate([own[...], other[...]], 0)
    *w, out = quarters(w_own)
    mixed = heads_forward(rows, w, table, QV_OWN, [seg_col[...] == seg_row[...]])[-1]
    total[...] = dot_tn(mixed, out)


def attend_kernel(early, own, other, w_own, w_far, table, seg_row, seg_col, *outs):
    keep, send = outs[:2]
    rows = jnp.concatenate([own[...], other[...]], 0)
    same = seg_col[...] == seg_row[...]
    total = w_own[...] if early else None
    for group, ref in enumerate((w_own, w_far)):
        if early and group == 0:
            continue
        *w, out = quarters(ref)
        *parts, probs, mixed = heads_forward(rows, w, table, QV_OWN + 2 * group, [same])
        if len(outs) > 2:
            for number, item in enumerate(parts):
                outs[2][group, number, : out.shape[0]] = item
            for number, item in enumerate(probs):
                outs[2][group, number, out.shape[0] :] = item
        term = dot_tn(mixed, out)
        total = term if total is None else total + term
    half = own.shape[0]
    keep[...] = own[...].astype(f32) + (total[:half] + table[OUT_BIAS : OUT_BIAS + 1])
    send[...] = total[half:].astype(bf16)


def attend_back_kernel(own, other, w_own, w_far, kept, residual, keep, send):
    half = own.shape[0] - EXTRA_ROWS
    rows = jnp.concatenate([own[:half], other[:half]], 0)
    total = None
    for group, ref in enumerate((w_own, w_far)):
        *w, out = quarters(ref)
        local = out.shape[0]
        grad_mixed = dot_nt(out, rows).astype(bf16)
        lines = [kept[group, number, :local] for number in range(3)]
        probs = [kept[group, number, local:] for number in range(3)]
        parts = heads_backward(*lines, probs, grad_mixed)
        for number, part in enumerate(parts):
            term = dot_tn(part, w[number])
            total = term if total is None else total + term
    keep[...] = total[:half] + residual[...]
    send[...] = total[half:].astype(bf16)


def standard(values):
    centred = values - jnp.mean(values, -1, keepdims=True)
    spread = lax.rsqrt(jnp.mean(centred * centred, -1, keepdims=True) + EPSILON)
    return centred * spread, spread


def norm_kernel(which, arrived, kept, table, *outs):
    summed = arrived[...].astype(f32) + kept[...]
    gain, shift = table[GAIN + which : GAIN + which + 1], table[SHIFT + which : SHIFT + which + 1]
    outs[0][...] = (standard(summed)[0] * gain + shift).astype(bf16)
    if len(outs) > 1:
        outs[1][...] = summed


def norm_grads(values, gain, upstream):
    normal, spread = standard(values)
    scaled = upstream * gain
    along = jnp.mean(scaled * normal, -1, keepdims=True)
    grad = (scaled - jnp.mean(scaled, -1, keepdims=True) - normal * along) * spread
    return grad, jnp.sum(upstream * normal, 0, keepdims=True), jnp.sum(upstream, 0, keepdims=True)


def norm_back_kernel(upstream, values, table, grad, low, gain_bias):
    result, grad_gain, grad_shift = norm_grads(
        values[...], table[GAIN + 1 : GAIN + 2], upstream[...].astype(f32)
    )
    grad[...] = result
    low[...] = result.astype(bf16)
    gain_bias[0:1] = grad_gain
    gain_bias[1:2] = grad_shift


def norm_back_sum_kernel(arrived, kept, values, table, others, grad, low):
    upstream = arrived[...].astype(f32) + kept[...]
    result, grad_gain, grad_shift = norm_grads(values[...], table[GAIN : GAIN + 1], upstream)
    rows = result.shape[0]
    grad[...] = result
    low[0:rows] = result.astype(bf16)
    small = jnp.concatenate([grad_gain, grad_shift, others[0:2]], 0)
    high = small.astype(bf16)
    rest = (small - high.astype(f32)).astype(bf16)
    blank = jnp.zeros((EXTRA_ROWS - 8, result.shape[1]), bf16)
    low[rows : rows + EXTRA_ROWS] = jnp.concatenate([high, rest, blank], 0)


def feed_kernel(one, two, three, four, weights, table, keep, send, *saved):
    part = one.shape[0]
    rows = jnp.concatenate([one[...], two[...], three[...], four[...]], 0)
    hidden = dot_nn(rows, weights[0]) + table[UP_BIAS : UP_BIAS + 1]
    phi = 0.5 * (1.0 + lax.erf(hidden * SQRT_HALF))
    if saved:
        slope = phi + hidden * (jnp.exp(-0.5 * hidden * hidden) * INV_SQRT_TAU)
        saved[0][...] = slope.astype(bf16)
    total = dot_nn((hidden * phi).astype(bf16), weights[1])
    keep[:part] = one[...].astype(f32) + (total[:part] + table[DOWN_BIAS : DOWN_BIAS + 1])
    keep[part:] = total[part : 2 * part]
    send[...] = total[2 * part :].astype(bf16)


def feed_back_kernel(one, two, three, four, slope, weights, residual, keep, send):
    part = one.shape[0]
    rows = jnp.concatenate([one[...], two[...], three[...], four[...]], 0)
    hidden = (dot_nt(rows, weights[1]) * slope[...].astype(f32)).astype(bf16)
    total = dot_nt(hidden, weights[0])
    keep[:part] = total[:part] + residual[...]
    keep[part:] = total[part : 2 * part]
    send[...] = total[2 * part :].astype(bf16)


def halves_kernel(arrived, kept, keep, send):
    part = keep.shape[0]
    total = arrived[...].astype(f32) + kept[...]
    keep[...] = total[:part]
    send[...] = total[part:].astype(bf16)


def entry_grad_kernel(arrived, kept, low):
    low[...] = (arrived[...].astype(f32) + kept[...]).astype(bf16)


def copy_kernel(source, target):
    target[...] = source[...]


def pair_kernel(*refs):
    for number, ref in enumerate(refs[:-1]):
        refs[-1][number] = ref[...]


def attend_group_kernel(one, two, three, four, w_own, table, seg_row, seg_col, lines, kept):
    entry = jnp.concatenate([one[...], two[...], three[...], four[...]], 0)
    same = [seg_col[seq] == seg_row[seq] for seq in range(2)]
    *parts, probs, mixed = heads_forward(entry, quarters(w_own)[:3], table, QV_OWN, same)
    for number, item in enumerate((*parts, mixed)):
        lines[number] = item
    for number, item in enumerate(probs):
        kept[number] = item


def unpack_kernel(total, g_w, g_out, g_b, g_out_b, g_gain, g_shift):
    local = g_out.shape[0]
    for number in range(3):
        g_w[number] = total[local * number : local * (number + 1)].astype(f32)
    g_out[...] = total[3 * local : 4 * local].astype(f32)
    rest = total[4 * local :].astype(f32)
    rest = rest[:7] + rest[7:14]
    g_b[...] = rest[:2, :local]
    g_out_b[...] = rest[2:3]
    g_gain[...] = jnp.concatenate([rest[3:4], rest[5:6]], 0)
    g_shift[...] = jnp.concatenate([rest[4:5], rest[6:7]], 0)


def attend_grads_kernel(*refs):
    lines, kept, w_own, total = refs[8:]
    out = quarters(w_own)[3]
    entry = jnp.concatenate([item[...] for item in refs[:4]], 0)
    pieces = [item[...] for item in refs[4:8]]
    part = refs[0].shape[0]
    local = out.shape[0]
    query, key, value, mixed = (lines[number] for number in range(4))
    probs = [kept[number] for number in range(kept.shape[0])]
    branch = jnp.concatenate([item[:part] for item in pieces], 0)
    grad_mixed = dot_nt(out, branch).astype(bf16)
    parts = heads_backward(query, key, value, probs, grad_mixed)
    for number, item in enumerate(parts):
        total[local * number : local * (number + 1)] = dot_nn(item, entry).astype(bf16)
    total[3 * local : 4 * local] = dot_nn(mixed, branch).astype(bf16)
    ones = jnp.ones((8, entry.shape[0]), bf16)
    blank = jnp.zeros((2, entry.shape[1] - local), f32)
    sums = jnp.concatenate([dot_nt(ones, parts[0])[:1], dot_nt(ones, parts[2])[:1]], 0)
    small = sum(item[part:].astype(f32) for item in pieces)
    sums = [jnp.concatenate([sums, blank], 1), dot_nn(ones, branch)[:1], small[:4] + small[4:8]]
    sums = jnp.concatenate(sums, 0)
    high = sums.astype(bf16)
    rest = (sums - high.astype(f32)).astype(bf16)
    blank = jnp.zeros((EXTRA_ROWS - 14, sums.shape[1]), bf16)
    total[4 * local : 4 * local + EXTRA_ROWS] = jnp.concatenate([high, rest, blank], 0)


def feed_grads_kernel(*refs):
    weights, table, g_up, g_up_b, g_down, g_down_b = refs[4:]

    @pl.when(pl.program_id(0) == 0)
    def _():
        g_up[...] = jnp.zeros_like(g_up)
        g_up_b[...] = jnp.zeros_like(g_up_b)
        g_down[...] = jnp.zeros_like(g_down)
        g_down_b[...] = jnp.zeros_like(g_down_b)

    first, grad = (jnp.concatenate([refs[i][...], refs[i + 2][...]], 0) for i in range(2))
    hidden = dot_nn(first, weights[0]) + table[UP_BIAS : UP_BIAS + 1]
    phi = 0.5 * (1.0 + lax.erf(hidden * SQRT_HALF))
    slope = phi + hidden * (jnp.exp(-0.5 * hidden * hidden) * INV_SQRT_TAU)
    act = (hidden * phi).astype(bf16)
    grad_hidden = (dot_nt(grad, weights[1]) * slope).astype(bf16)
    g_down[...] += dot_tn(act, grad)
    g_up[...] += dot_tn(first, grad_hidden)
    g_up_b[...] += jnp.sum(grad_hidden.astype(f32), 0, keepdims=True)
    g_down_b[...] += jnp.sum(grad.astype(f32), 0, keepdims=True)


def whole(item):
    return pl.BlockSpec(item.shape, lambda step: (0,) * len(item.shape))


def leading(item, count):
    rest = len(item.shape) - 1
    return pl.BlockSpec((count,) + item.shape[1:], lambda step: (step,) + (0,) * rest)


def shards(
    block_input,
    segments,
    out_grad,
    query_key_value_weight,
    b_qv,
    attention_output_weight,
    attention_out_bias,
    ln_gain,
    ln_bias,
    up_projection_weight,
    up_proj_bias,
    down_projection_weight,
    down_proj_bias,
):
    assert lax.axis_size("tensor") == 4 and block_input.shape[0] == 2
    groups = lax.axis_size("dp")
    section = lax.axis_index("section")
    place = lax.axis_index("tensor")
    a, b = place // 2, place % 2
    seqs, quarter, width = block_input.shape
    length = segments.shape[1]
    part = length // 2
    local = query_key_value_weight.shape[3]
    hidden_local = up_projection_weight.shape[2]
    heads = local // HEAD_DIM

    beside = [(i, i ^ 1) for i in range(4)]
    across = [(i, i ^ 2) for i in range(4)]
    turn = [(2 * s + c, 2 * c + s) for s in range(2) for c in range(2)]
    twist = [(2 * s + c, 2 * c + 1 - s) for s in range(2) for c in range(2)]
    untwist = [(target, source) for source, target in twist]

    def swap(value, pairs):
        return lax.ppermute(value, "tensor", pairs)

    def pieces_of(block):
        one = swap(jnp.where(b == 0, block[0], block[1]), turn)
        two = swap(jnp.where(b == 0, block[1], block[0]), untwist)
        return jnp.where(a == 0, jnp.concatenate([one, two]), jnp.concatenate([two, one]))

    def blocks_of(piece):
        one = swap(jnp.where(a == 0, piece[:quarter], piece[quarter:]), turn)
        two = swap(jnp.where(a == 0, piece[quarter:], piece[:quarter]), twist)
        return jnp.where(b == 0, jnp.stack([one, two]), jnp.stack([two, one]))

    w_own = jnp.transpose(query_key_value_weight[0], (1, 2, 0)).reshape(3 * local, width)
    w_own = jnp.concatenate([w_own, attention_output_weight[0]])
    entry_input = pieces_of(block_input)
    w_far = swap(w_own, across)
    cotangent = pieces_of(out_grad)
    weights = jnp.concatenate([up_projection_weight, down_projection_weight])

    def lines(item):
        return jnp.pad(item, ((0, 0), (0, width - item.shape[1])))

    b_own = lines(b_qv[0])
    table = [ln_gain[0], ln_bias[0], attention_out_bias, lines(up_proj_bias), down_proj_bias]
    table += [b_own, swap(b_own, across)]
    table = jnp.concatenate(table).astype(f32)
    table = jnp.pad(table, ((0, TABLE_ROWS - table.shape[0]), (0, 0)))

    seg_own = segments[0] if seqs == 1 else jnp.where(a == 0, segments[0], segments[1])
    seg_own = seg_own.astype(f32)
    seg_turned = jnp.where(b == 0, seg_own, jnp.roll(seg_own, part))
    seg_row, seg_col = seg_turned[None, :], seg_turned[:, None]
    seg_far = jnp.where(a == 0, segments[1], segments[0]).astype(f32)
    seg_far = jnp.where(b == 0, seg_far, jnp.roll(seg_far, part))
    seg_both = jnp.stack([seg_turned, seg_far])

    piece_f, piece_h = shape((part, width), f32), shape((part, width), bf16)
    pair_f, pair_h = shape((2 * part, width), f32), shape((2 * part, width), bf16)

    def forward(entry, save, before=(), after=()):
        outs = [piece_f, piece_h]
        if save:
            outs.append(shape((2, 3, local + length, length), bf16))
        near, first_part = swap(entry, beside), w_own
        if not save:
            args = (entry, near, w_own, table, seg_row, seg_col)
            first_part = run(attend_own_kernel, [pair_f], args, 2.0, "attend_own")[0]
        args = (entry, near, first_part, w_far, table, seg_row, seg_col)
        keep, branch, *kept = run(
            functools.partial(attend_kernel, not save), outs, args, 3.0, "attend", after=before
        )
        args = (swap(branch, beside), keep, table)
        first, *first_res = run(
            functools.partial(norm_kernel, 0),
            [piece_h] + [piece_f] * save,
            args,
            0,
            "first_norm",
            after=after,
        )
        far = swap(first, across)
        near, far_near = swap(first, beside), swap(far, beside)
        outs = [pair_f, pair_h] + [shape((4 * part, hidden_local), bf16)] * save
        args = (first, far, near, far_near, weights, table)
        keep, send, *slope = run(feed_kernel, outs, args, 1.6, "feed")
        keep, send = run(halves_kernel, [piece_f, piece_h], (swap(send, beside), keep), 0, "halves")
        args = (swap(send, across), keep, table)
        output, *second_res = run(
            functools.partial(norm_kernel, 1),
            [piece_h] + [piece_f] * save,
            args,
            0,
            "second_norm",
        )
        if not save:
            return output
        return output, (kept, first_res[0], slope[0], second_res[0]), (first, far), branch

    def backward(upstream, saved, after=(), later=()):
        kept, first_res, slope, second_res = saved
        grad_second, grad_y, gain_bias = run(
            norm_back_kernel,
            [piece_f, piece_h, shape((2, width), f32)],
            (upstream, second_res, table),
            0,
            "second_norm_back",
            after=after,
        )
        far = swap(grad_y, across)
        near, far_near = swap(grad_y, beside), swap(far, beside)
        args = (grad_y, far, near, far_near, slope, weights, grad_second)
        keep, gate = run(feed_back_kernel, [pair_f, pair_h], args, 1.5, "feed_back")
        keep, send = run(halves_kernel, [piece_f, piece_h], (swap(gate, beside), keep), 0, "halves")
        args = (swap(send, across), keep, first_res, table, gain_bias)
        outs = [piece_f, shape((part + EXTRA_ROWS, width), bf16)]
        grad_first, branch = run(norm_back_sum_kernel, outs, args, 0, "first_norm_back")
        near = swap(branch, beside)

        args = (branch, near, w_own, w_far, *kept, grad_first)
        keep, send = run(attend_back_kernel, [piece_f, piece_h], args, 3.2, "attend_back", after=later)
        args = (swap(send, beside), keep)
        grad_entry = run(entry_grad_kernel, [piece_h], args, 0, "entry_grad")[0]
        return grad_entry, (grad_y, far), branch, near, send

    wide = groups in (2, 4)
    count = groups if wide else 1

    def gather(pair):
        mine = lax.all_gather(pair, "dp") if wide else pair[None]
        return mine, swap(mine, beside)

    sections = [(0, 1), (1, 0)]
    middle = lax.ppermute(forward(entry_input, False), "section", sections)
    entry = jnp.where(section == 0, entry_input, middle)
    entry_far = swap(entry, across)
    output, saved, first_pair, _ = forward(entry, True, (cotangent,), (entry_far,))

    entries = (entry, swap(entry, beside), entry_far, swap(entry_far, beside))

    firsts = [item.reshape(-1, width) for item in gather(jnp.stack(first_pair))]
    grad = backward(cotangent, saved, later=(firsts[0],))[0]
    layer_output = blocks_of(output)
    args = (*entries, w_own, table, seg_both[:, None, :], seg_both[:, :, None])
    outs = [shape((4, local, 2 * length), bf16), shape((2 * heads, length, length), bf16)]
    attended = run(attend_group_kernel, outs, args, 4.0, "attend_group", mib=24)
    middle = lax.ppermute(grad, "section", sections)
    grad_entry, grad_y, branch, near, token = backward(
        jnp.where(section == 1, cotangent, middle), saved, (layer_output, attended[0])
    )
    outs = [shape((2, part, width), bf16)]
    grad_y = run(pair_kernel, outs, grad_y, 0, "grad_y_pair")[0]
    grad_y = lax.all_gather(grad_y, "dp") if wide else grad_y[None]

    far = run(copy_kernel, [shape(branch.shape, bf16)], (swap(branch, across),), 0, "far", after=(token,))[0]
    total = run(
        attend_grads_kernel,
        [shape((4 * local + EXTRA_ROWS, width), bf16)],
        (*entries, branch, near, far, swap(far, beside), *attended, w_own),
        5.0,
        "attend_grads",
        mib=24,
    )[0]
    local_total = total
    grad_y, local_total = lax.optimization_barrier((grad_y, local_total))
    total = lax.psum(local_total, "dp")
    grads_y = [item.reshape(-1, width) for item in (grad_y, swap(grad_y, beside))]
    args = (firsts[0], grads_y[0], firsts[1], grads_y[1], weights, table)
    outs = [
        shape((width, hidden_local), f32),
        shape((1, hidden_local), f32),
        shape((hidden_local, width), f32),
        shape((1, width), f32),
    ]
    block, tall = 2 * part, firsts[0].shape[0]
    g_up, g_up_b, g_down, g_down_b = run(
        feed_grads_kernel,
        outs,
        args,
        5.0,
        "feed_grads",
        mib=56,
        grid=(tall // block,),
        in_specs=[leading(item, block) for item in args[:4]] + [whole(item) for item in args[4:]],
        out_specs=[whole(item) for item in outs],
    )
    held = run(copy_kernel, [piece_h], (grad_entry,), 0, "held", after=(g_down,))[0]
    input_grad = blocks_of(held)
    if not wide:
        g_up, g_up_b, g_down = [
            lax.psum(item.astype(bf16), "dp").astype(f32) for item in (g_up, g_up_b, g_down)
        ]
        g_down_b = lax.psum(g_down_b, "dp")
    outs = [shape((3, local, width), f32), shape((local, width), f32), shape((2, local), f32)]
    outs += [shape((1, width), f32), shape((2, width), f32), shape((2, width), f32)]
    after = (g_down, input_grad)
    g_w, g_out, g_b, g_out_b, g_gain, g_shift = run(
        unpack_kernel, outs, (total,), 1.0, "unpack", after=after
    )
    return (
        layer_output[None],
        input_grad[None],
        jnp.transpose(g_w, (2, 0, 1))[None],
        g_b[None],
        g_out[None],
        g_out_b,
        g_gain[None],
        g_shift[None],
        g_up[None],
        g_up_b,
        g_down[None],
        g_down_b,
    )


def solution(mesh):
    return jax.shard_map(
        shards,
        mesh=mesh,
        in_specs=(
            P("dp", "tensor", None),
            P("dp", None),
            P("dp", "tensor", None),
            P("section", None, None, "tensor"),
            P("section", None, "tensor"),
            P("section", "tensor", None),
            P("section", None),
            P("section", None, None),
            P("section", None, None),
            P("section", None, "tensor"),
            P("section", "tensor"),
            P("section", "tensor", None),
            P("section", None),
        ),
        out_specs=(
            P("section", "dp", "tensor", None),
            P("section", "dp", "tensor", None),
            P("section", None, None, "tensor"),
            P("section", None, "tensor"),
            P("section", "tensor", None),
            P("section", None),
            P("section", None, None),
            P("section", None, None),
            P("section", None, "tensor"),
            P("section", "tensor"),
            P("section", "tensor", None),
            P("section", None),
        ),
        check_vma=False,
    )
```

```python
import functools

import jax
import jax.numpy as jnp
from jax import lax
from jax.experimental import pallas as pl
from jax.experimental.pallas import tpu as pltpu
from jax.sharding import PartitionSpec as P

HEAD_DIM = 64
EPSILON = 1e-06
BIG_NEGATIVE = -1e30
MIB = 1024 * 1024
EXTRA_ROWS = 16
GAIN, SHIFT, OUT_BIAS, UP_BIAS, DOWN_BIAS, QV_OWN, QV_FAR, TABLE_ROWS = 0, 2, 4, 5, 6, 7, 9, 16
SQRT_HALF = 0.7071067811865476
INV_SQRT_TAU = 0.3989422804014327

f32 = jnp.float32
bf16 = jnp.bfloat16


def dot_nn(left, right):
    return lax.dot_general(left, right, (((1,), (0,)), ((), ())), preferred_element_type=f32)


def dot_nt(left, right):
    return lax.dot_general(left, right, (((1,), (1,)), ((), ())), preferred_element_type=f32)


def dot_tn(left, right):
    return lax.dot_general(left, right, (((0,), (0,)), ((), ())), preferred_element_type=f32)


def shape(dims, kind):
    return jax.ShapeDtypeStruct(dims, kind)


def run(kernel, outs, args, us, name, mib=16, after=(), grid=None, in_specs=None, out_specs=None,
        scalars=0, aliases=None):
    count = len(args)
    if in_specs is None:
        in_specs = [pl.BlockSpec(memory_space=pltpu.VMEM)] * count
    if out_specs is None:
        out_specs = [pl.BlockSpec(memory_space=pltpu.VMEM)] * len(outs)
    waits = [pl.BlockSpec(memory_space=pl.ANY)] * len(after)

    def body(*refs):
        kernel(*refs[:count], *refs[count + len(after) :])

    moved = sum(item.size * item.dtype.itemsize for item in (*args, *outs))
    return pl.pallas_call(
        body,
        out_shape=outs,
        grid_spec=pltpu.PrefetchScalarGridSpec(
            num_scalar_prefetch=scalars,
            grid=grid or (),
            in_specs=[*in_specs, *waits],
            out_specs=out_specs,
        ),
        name=name,
        input_output_aliases=aliases or {},
        compiler_params=pltpu.CompilerParams(vmem_limit_bytes=mib * MIB),
        cost_estimate=pl.CostEstimate(
            flops=int(us * 1.15e9), bytes_accessed=moved, transcendentals=0
        ),
    )(*args, *after)


def quarters(ref):
    local = ref.shape[0] // 4
    return [ref[local * number : local * (number + 1)] for number in range(4)]


def heads_forward(entry, w, table, line, same):
    local, length = w[0].shape[0], entry.shape[0] // len(same)
    bias = jnp.transpose(table[line : line + 2, :local])
    query = ((dot_nt(w[0], entry) + bias[:, 0:1]).astype(bf16) * HEAD_DIM**-0.5).astype(bf16)
    key = dot_nt(w[1], entry).astype(bf16)
    value = (dot_nt(w[2], entry) + bias[:, 1:2]).astype(bf16)
    probs, columns = [], []
    for seq, visible in enumerate(same):
        span = slice(length * seq, length * (seq + 1))
        mixed = []
        for start in range(0, local, HEAD_DIM):
            head = slice(start, start + HEAD_DIM)
            scores = jnp.where(visible, dot_tn(key[head, span], query[head, span]), BIG_NEGATIVE)
            weights = jnp.exp(scores - jnp.max(scores, 0, keepdims=True))
            weights = weights * (1.0 / jnp.sum(weights, 0, keepdims=True))
            probs.append(weights.astype(bf16))
            mixed.append(dot_nn(value[head, span], probs[-1]).astype(bf16))
        columns.append(jnp.concatenate(mixed, 0))
    return query, key, value, probs, jnp.concatenate(columns, 1)


def heads_backward(query, key, value, probs, grad_mixed):
    heads = query.shape[0] // HEAD_DIM
    length = probs[0].shape[0]
    columns = []
    for seq in range(len(probs) // heads):
        span = slice(length * seq, length * (seq + 1))
        rows = [], [], []
        for number in range(heads):
            head = slice(HEAD_DIM * number, HEAD_DIM * (number + 1))
            low = probs[heads * seq + number]
            q, k, v, upstream = (item[head, span] for item in (query, key, value, grad_mixed))
            wide = low.astype(f32)
            grads = wide * dot_tn(v, upstream)
            grads = (grads - wide * jnp.sum(grads, 0, keepdims=True)).astype(bf16)
            rows[0].append((dot_nn(k, grads) * HEAD_DIM**-0.5).astype(bf16))
            rows[1].append(dot_nt(q, grads).astype(bf16))
            rows[2].append(dot_nt(upstream, low).astype(bf16))
        columns.append([jnp.concatenate(item, 0) for item in rows])
    return [jnp.concatenate(pair, 1) for pair in zip(*columns)]


def attend_own_kernel(own, other, w_own, table, seg_row, seg_col, total):
    rows = jnp.concatenate([own[...], other[...]], 0)
    *w, out = quarters(w_own)
    mixed = heads_forward(rows, w, table, QV_OWN, [seg_col[...] == seg_row[...]])[-1]
    total[...] = dot_tn(mixed, out)


def attend_kernel(early, own, other, w_own, w_far, table, seg_row, seg_col, *outs):
    keep, send = outs[:2]
    rows = jnp.concatenate([own[...], other[...]], 0)
    same = seg_col[...] == seg_row[...]
    total = w_own[...] if early else None
    for group, ref in enumerate((w_own, w_far)):
        if early and group == 0:
            continue
        *w, out = quarters(ref)
        *parts, probs, mixed = heads_forward(rows, w, table, QV_OWN + 2 * group, [same])
        if len(outs) > 2:
            for number, item in enumerate(parts):
                outs[2][group, number, : out.shape[0]] = item
            for number, item in enumerate(probs):
                outs[2][group, number, out.shape[0] :] = item
        term = dot_tn(mixed, out)
        total = term if total is None else total + term
    half = own.shape[0]
    keep[...] = own[...].astype(f32) + (total[:half] + table[OUT_BIAS : OUT_BIAS + 1])
    send[...] = total[half:].astype(bf16)


def attend_back_kernel(own, other, w_own, w_far, kept, residual, keep, send):
    half = own.shape[0] - EXTRA_ROWS
    rows = jnp.concatenate([own[:half], other[:half]], 0)
    total = None
    for group, ref in enumerate((w_own, w_far)):
        *w, out = quarters(ref)
        local = out.shape[0]
        grad_mixed = dot_nt(out, rows).astype(bf16)
        lines = [kept[group, number, :local] for number in range(3)]
        probs = [kept[group, number, local:] for number in range(3)]
        parts = heads_backward(*lines, probs, grad_mixed)
        for number, part in enumerate(parts):
            term = dot_tn(part, w[number])
            total = term if total is None else total + term
    keep[...] = total[:half] + residual[...]
    send[...] = total[half:].astype(bf16)


def standard(values):
    centred = values - jnp.mean(values, -1, keepdims=True)
    spread = lax.rsqrt(jnp.mean(centred * centred, -1, keepdims=True) + EPSILON)
    return centred * spread, spread


def norm_kernel(which, arrived, kept, table, *outs):
    summed = arrived[...].astype(f32) + kept[...]
    gain, shift = table[GAIN + which : GAIN + which + 1], table[SHIFT + which : SHIFT + which + 1]
    outs[0][...] = (standard(summed)[0] * gain + shift).astype(bf16)
    if len(outs) > 1:
        outs[1][...] = summed


def norm_grads(values, gain, upstream):
    normal, spread = standard(values)
    scaled = upstream * gain
    along = jnp.mean(scaled * normal, -1, keepdims=True)
    grad = (scaled - jnp.mean(scaled, -1, keepdims=True) - normal * along) * spread
    return grad, jnp.sum(upstream * normal, 0, keepdims=True), jnp.sum(upstream, 0, keepdims=True)


def norm_back_kernel(upstream, values, table, grad, low, gain_bias):
    result, grad_gain, grad_shift = norm_grads(
        values[...], table[GAIN + 1 : GAIN + 2], upstream[...].astype(f32)
    )
    grad[...] = result
    low[...] = result.astype(bf16)
    gain_bias[0:1] = grad_gain
    gain_bias[1:2] = grad_shift


def norm_back_sum_kernel(arrived, kept, values, table, others, grad, low):
    upstream = arrived[...].astype(f32) + kept[...]
    result, grad_gain, grad_shift = norm_grads(values[...], table[GAIN : GAIN + 1], upstream)
    rows = result.shape[0]
    grad[...] = result
    low[0:rows] = result.astype(bf16)
    small = jnp.concatenate([grad_gain, grad_shift, others[0:2]], 0)
    high = small.astype(bf16)
    rest = (small - high.astype(f32)).astype(bf16)
    blank = jnp.zeros((EXTRA_ROWS - 8, result.shape[1]), bf16)
    low[rows : rows + EXTRA_ROWS] = jnp.concatenate([high, rest, blank], 0)


def feed_kernel(one, two, three, four, weights, table, keep, send, *saved):
    part = one.shape[0]
    rows = jnp.concatenate([one[...], two[...], three[...], four[...]], 0)
    hidden = dot_nn(rows, weights[0]) + table[UP_BIAS : UP_BIAS + 1]
    phi = 0.5 * (1.0 + lax.erf(hidden * SQRT_HALF))
    if saved:
        slope = phi + hidden * (jnp.exp(-0.5 * hidden * hidden) * INV_SQRT_TAU)
        saved[0][...] = slope.astype(bf16)
    total = dot_nn((hidden * phi).astype(bf16), weights[1])
    keep[:part] = one[...].astype(f32) + (total[:part] + table[DOWN_BIAS : DOWN_BIAS + 1])
    keep[part:] = total[part : 2 * part]
    send[...] = total[2 * part :].astype(bf16)


def feed_back_kernel(one, two, three, four, slope, weights, residual, keep, send):
    part = one.shape[0]
    rows = jnp.concatenate([one[...], two[...], three[...], four[...]], 0)
    hidden = (dot_nt(rows, weights[1]) * slope[...].astype(f32)).astype(bf16)
    total = dot_nt(hidden, weights[0])
    keep[:part] = total[:part] + residual[...]
    keep[part:] = total[part : 2 * part]
    send[...] = total[2 * part :].astype(bf16)


def halves_kernel(arrived, kept, keep, send):
    part = keep.shape[0]
    total = arrived[...].astype(f32) + kept[...]
    keep[...] = total[:part]
    send[...] = total[part:].astype(bf16)


def entry_grad_kernel(arrived, kept, low):
    low[...] = (arrived[...].astype(f32) + kept[...]).astype(bf16)


def copy_kernel(source, target):
    target[...] = source[...]


def pair_kernel(*refs):
    for number, ref in enumerate(refs[:-1]):
        refs[-1][number] = ref[...]


def attend_group_kernel(one, two, three, four, w_own, table, seg_row, seg_col, lines, kept):
    entry = jnp.concatenate([one[...], two[...], three[...], four[...]], 0)
    same = [seg_col[seq] == seg_row[seq] for seq in range(2)]
    *parts, probs, mixed = heads_forward(entry, quarters(w_own)[:3], table, QV_OWN, same)
    for number, item in enumerate((*parts, mixed)):
        lines[number] = item
    for number, item in enumerate(probs):
        kept[number] = item


def unpack_kernel(total, g_w, g_out, g_b, g_out_b, g_gain, g_shift):
    local = g_out.shape[0]
    for number in range(3):
        g_w[number] = total[local * number : local * (number + 1)].astype(f32)
    g_out[...] = total[3 * local : 4 * local].astype(f32)
    rest = total[4 * local :].astype(f32)
    rest = rest[:7] + rest[7:14]
    g_b[...] = rest[:2, :local]
    g_out_b[...] = rest[2:3]
    g_gain[...] = jnp.concatenate([rest[3:4], rest[5:6]], 0)
    g_shift[...] = jnp.concatenate([rest[4:5], rest[6:7]], 0)


def attend_grads_kernel(*refs):
    lines, kept, w_own, total = refs[8:]
    out = quarters(w_own)[3]
    entry = jnp.concatenate([item[...] for item in refs[:4]], 0)
    pieces = [item[...] for item in refs[4:8]]
    part = refs[0].shape[0]
    local = out.shape[0]
    query, key, value, mixed = (lines[number] for number in range(4))
    probs = [kept[number] for number in range(kept.shape[0])]
    branch = jnp.concatenate([item[:part] for item in pieces], 0)
    grad_mixed = dot_nt(out, branch).astype(bf16)
    parts = heads_backward(query, key, value, probs, grad_mixed)
    for number, item in enumerate(parts):
        total[local * number : local * (number + 1)] = dot_nn(item, entry).astype(bf16)
    total[3 * local : 4 * local] = dot_nn(mixed, branch).astype(bf16)
    ones = jnp.ones((8, entry.shape[0]), bf16)
    blank = jnp.zeros((2, entry.shape[1] - local), f32)
    sums = jnp.concatenate([dot_nt(ones, parts[0])[:1], dot_nt(ones, parts[2])[:1]], 0)
    small = sum(item[part:].astype(f32) for item in pieces)
    sums = [jnp.concatenate([sums, blank], 1), dot_nn(ones, branch)[:1], small[:4] + small[4:8]]
    sums = jnp.concatenate(sums, 0)
    high = sums.astype(bf16)
    rest = (sums - high.astype(f32)).astype(bf16)
    blank = jnp.zeros((EXTRA_ROWS - 14, sums.shape[1]), bf16)
    total[4 * local : 4 * local + EXTRA_ROWS] = jnp.concatenate([high, rest, blank], 0)


def feed_grads_kernel(*refs):
    weights, table, g_up, g_up_b, g_down, g_down_b = refs[4:]

    @pl.when(pl.program_id(0) == 0)
    def _():
        g_up[...] = jnp.zeros_like(g_up)
        g_up_b[...] = jnp.zeros_like(g_up_b)
        g_down[...] = jnp.zeros_like(g_down)
        g_down_b[...] = jnp.zeros_like(g_down_b)

    first, grad = (jnp.concatenate([refs[i][...], refs[i + 2][...]], 0) for i in range(2))
    hidden = dot_nn(first, weights[0]) + table[UP_BIAS : UP_BIAS + 1]
    phi = 0.5 * (1.0 + lax.erf(hidden * SQRT_HALF))
    slope = phi + hidden * (jnp.exp(-0.5 * hidden * hidden) * INV_SQRT_TAU)
    act = (hidden * phi).astype(bf16)
    grad_hidden = (dot_nt(grad, weights[1]) * slope).astype(bf16)
    g_down[...] += dot_tn(act, grad)
    g_up[...] += dot_tn(first, grad_hidden)
    g_up_b[...] += jnp.sum(grad_hidden.astype(f32), 0, keepdims=True)
    g_down_b[...] += jnp.sum(grad.astype(f32), 0, keepdims=True)


def whole(item):
    return pl.BlockSpec(item.shape, lambda step: (0,) * len(item.shape))


def leading(item, count):
    rest = len(item.shape) - 1
    return pl.BlockSpec((count,) + item.shape[1:], lambda step: (step,) + (0,) * rest)


def shards(
    block_input,
    segments,
    out_grad,
    query_key_value_weight,
    b_qv,
    attention_output_weight,
    attention_out_bias,
    ln_gain,
    ln_bias,
    up_projection_weight,
    up_proj_bias,
    down_projection_weight,
    down_proj_bias,
):
    assert lax.axis_size("tensor") == 4 and block_input.shape[0] == 2
    groups = lax.axis_size("dp")
    section = lax.axis_index("section")
    place = lax.axis_index("tensor")
    a, b = place // 2, place % 2
    seqs, quarter, width = block_input.shape
    length = segments.shape[1]
    part = length // 2
    local = query_key_value_weight.shape[3]
    hidden_local = up_projection_weight.shape[2]
    heads = local // HEAD_DIM

    beside = [(i, i ^ 1) for i in range(4)]
    across = [(i, i ^ 2) for i in range(4)]
    turn = [(2 * s + c, 2 * c + s) for s in range(2) for c in range(2)]
    twist = [(2 * s + c, 2 * c + 1 - s) for s in range(2) for c in range(2)]
    untwist = [(target, source) for source, target in twist]

    def swap(value, pairs):
        return lax.ppermute(value, "tensor", pairs)

    def pieces_of(block):
        one = swap(jnp.where(b == 0, block[0], block[1]), turn)
        two = swap(jnp.where(b == 0, block[1], block[0]), untwist)
        return jnp.where(a == 0, jnp.concatenate([one, two]), jnp.concatenate([two, one]))

    def blocks_of(piece):
        one = swap(jnp.where(a == 0, piece[:quarter], piece[quarter:]), turn)
        two = swap(jnp.where(a == 0, piece[quarter:], piece[:quarter]), twist)
        return jnp.where(b == 0, jnp.stack([one, two]), jnp.stack([two, one]))

    w_own = jnp.transpose(query_key_value_weight[0], (1, 2, 0)).reshape(3 * local, width)
    w_own = jnp.concatenate([w_own, attention_output_weight[0]])
    entry_input = pieces_of(block_input)
    w_far = swap(w_own, across)
    cotangent = pieces_of(out_grad)
    weights = jnp.concatenate([up_projection_weight, down_projection_weight])

    def lines(item):
        return jnp.pad(item, ((0, 0), (0, width - item.shape[1])))

    b_own = lines(b_qv[0])
    table = [ln_gain[0], ln_bias[0], attention_out_bias, lines(up_proj_bias), down_proj_bias]
    table += [b_own, swap(b_own, across)]
    table = jnp.concatenate(table).astype(f32)
    table = jnp.pad(table, ((0, TABLE_ROWS - table.shape[0]), (0, 0)))

    seg_own = segments[0] if seqs == 1 else jnp.where(a == 0, segments[0], segments[1])
    seg_own = seg_own.astype(f32)
    seg_turned = jnp.where(b == 0, seg_own, jnp.roll(seg_own, part))
    seg_row, seg_col = seg_turned[None, :], seg_turned[:, None]
    seg_far = jnp.where(a == 0, segments[1], segments[0]).astype(f32)
    seg_far = jnp.where(b == 0, seg_far, jnp.roll(seg_far, part))
    seg_both = jnp.stack([seg_turned, seg_far])

    piece_f, piece_h = shape((part, width), f32), shape((part, width), bf16)
    pair_f, pair_h = shape((2 * part, width), f32), shape((2 * part, width), bf16)

    def forward(entry, save, before=(), after=()):
        outs = [piece_f, piece_h]
        if save:
            outs.append(shape((2, 3, local + length, length), bf16))
        near, first_part = swap(entry, beside), w_own
        if not save:
            args = (entry, near, w_own, table, seg_row, seg_col)
            first_part = run(attend_own_kernel, [pair_f], args, 2.0, "attend_own")[0]
        args = (entry, near, first_part, w_far, table, seg_row, seg_col)
        keep, branch, *kept = run(
            functools.partial(attend_kernel, not save), outs, args, 3.0, "attend", after=before
        )
        args = (swap(branch, beside), keep, table)
        first, *first_res = run(
            functools.partial(norm_kernel, 0),
            [piece_h] + [piece_f] * save,
            args,
            0,
            "first_norm",
            after=after,
        )
        far = swap(first, across)
        near, far_near = swap(first, beside), swap(far, beside)
        outs = [pair_f, pair_h] + [shape((4 * part, hidden_local), bf16)] * save
        args = (first, far, near, far_near, weights, table)
        keep, send, *slope = run(feed_kernel, outs, args, 1.6, "feed")
        keep, send = run(halves_kernel, [piece_f, piece_h], (swap(send, beside), keep), 0, "halves")
        args = (swap(send, across), keep, table)
        output, *second_res = run(
            functools.partial(norm_kernel, 1),
            [piece_h] + [piece_f] * save,
            args,
            0,
            "second_norm",
        )
        if not save:
            return output
        return output, (kept, first_res[0], slope[0], second_res[0]), (first, far), branch

    def backward(upstream, saved, after=(), later=()):
        kept, first_res, slope, second_res = saved
        grad_second, grad_y, gain_bias = run(
            norm_back_kernel,
            [piece_f, piece_h, shape((2, width), f32)],
            (upstream, second_res, table),
            0,
            "second_norm_back",
            after=after,
        )
        far = swap(grad_y, across)
        near, far_near = swap(grad_y, beside), swap(far, beside)
        args = (grad_y, far, near, far_near, slope, weights, grad_second)
        keep, gate = run(feed_back_kernel, [pair_f, pair_h], args, 1.5, "feed_back")
        keep, send = run(halves_kernel, [piece_f, piece_h], (swap(gate, beside), keep), 0, "halves")
        args = (swap(send, across), keep, first_res, table, gain_bias)
        outs = [piece_f, shape((part + EXTRA_ROWS, width), bf16)]
        grad_first, branch = run(norm_back_sum_kernel, outs, args, 0, "first_norm_back")
        near = swap(branch, beside)

        args = (branch, near, w_own, w_far, *kept, grad_first)
        keep, send = run(attend_back_kernel, [piece_f, piece_h], args, 3.2, "attend_back", after=later)
        args = (swap(send, beside), keep)
        grad_entry = run(entry_grad_kernel, [piece_h], args, 0, "entry_grad")[0]
        return grad_entry, (grad_y, far), branch, near, send

    wide = groups in (2, 4)
    count = groups if wide else 1

    def gather(pair):
        mine = lax.all_gather(pair, "dp") if wide else pair[None]
        return mine, swap(mine, beside)

    sections = [(0, 1), (1, 0)]
    middle = lax.ppermute(forward(entry_input, False), "section", sections)
    entry = jnp.where(section == 0, entry_input, middle)
    entry_far = swap(entry, across)
    output, saved, first_pair, _ = forward(entry, True, (cotangent,), (entry_far,))

    entries = (entry, swap(entry, beside), entry_far, swap(entry_far, beside))

    firsts = [item.reshape(-1, width) for item in gather(jnp.stack(first_pair))]
    grad = backward(cotangent, saved)[0]
    layer_output = blocks_of(output)
    args = (*entries, w_own, table, seg_both[:, None, :], seg_both[:, :, None])
    outs = [shape((4, local, 2 * length), bf16), shape((2 * heads, length, length), bf16)]
    attended = run(attend_group_kernel, outs, args, 4.0, "attend_group", mib=24, after=(firsts[0],))
    middle = lax.ppermute(grad, "section", sections)
    grad_entry, grad_y, branch, near, token = backward(
        jnp.where(section == 1, cotangent, middle), saved, (layer_output, attended[0])
    )
    outs = [shape((2, part, width), bf16)]
    grad_y = run(pair_kernel, outs, grad_y, 0, "grad_y_pair")[0]
    grad_y = lax.all_gather(grad_y, "dp") if wide else grad_y[None]

    far = run(copy_kernel, [shape(branch.shape, bf16)], (swap(branch, across),), 0, "far", after=(token,))[0]
    total = run(
        attend_grads_kernel,
        [shape((4 * local + EXTRA_ROWS, width), bf16)],
        (*entries, branch, near, far, swap(far, beside), *attended, w_own),
        5.0,
        "attend_grads",
        mib=24,
    )[0]
    local_total = total
    grad_y, local_total = lax.optimization_barrier((grad_y, local_total))
    total = lax.psum(local_total, "dp")
    grads_y = [item.reshape(-1, width) for item in (grad_y, swap(grad_y, beside))]
    args = (firsts[0], grads_y[0], firsts[1], grads_y[1], weights, table)
    outs = [
        shape((width, hidden_local), f32),
        shape((1, hidden_local), f32),
        shape((hidden_local, width), f32),
        shape((1, width), f32),
    ]
    block, tall = 2 * part, firsts[0].shape[0]
    g_up, g_up_b, g_down, g_down_b = run(
        feed_grads_kernel,
        outs,
        args,
        5.0,
        "feed_grads",
        mib=56,
        grid=(tall // block,),
        in_specs=[leading(item, block) for item in args[:4]] + [whole(item) for item in args[4:]],
        out_specs=[whole(item) for item in outs],
    )
    held = run(copy_kernel, [piece_h], (grad_entry,), 0, "held", after=(g_down,))[0]
    input_grad = blocks_of(held)
    if not wide:
        g_up, g_up_b, g_down = [
            lax.psum(item.astype(bf16), "dp").astype(f32) for item in (g_up, g_up_b, g_down)
        ]
        g_down_b = lax.psum(g_down_b, "dp")
    outs = [shape((3, local, width), f32), shape((local, width), f32), shape((2, local), f32)]
    outs += [shape((1, width), f32), shape((2, width), f32), shape((2, width), f32)]
    after = (g_down, input_grad)
    g_w, g_out, g_b, g_out_b, g_gain, g_shift = run(
        unpack_kernel, outs, (total,), 1.0, "unpack", after=after
    )
    return (
        layer_output[None],
        input_grad[None],
        jnp.transpose(g_w, (2, 0, 1))[None],
        g_b[None],
        g_out[None],
        g_out_b,
        g_gain[None],
        g_shift[None],
        g_up[None],
        g_up_b,
        g_down[None],
        g_down_b,
    )


def solution(mesh):
    return jax.shard_map(
        shards,
        mesh=mesh,
        in_specs=(
            P("dp", "tensor", None),
            P("dp", None),
            P("dp", "tensor", None),
            P("section", None, None, "tensor"),
            P("section", None, "tensor"),
            P("section", "tensor", None),
            P("section", None),
            P("section", None, None),
            P("section", None, None),
            P("section", None, "tensor"),
            P("section", "tensor"),
            P("section", "tensor", None),
            P("section", None),
        ),
        out_specs=(
            P("section", "dp", "tensor", None),
            P("section", "dp", "tensor", None),
            P("section", None, None, "tensor"),
            P("section", None, "tensor"),
            P("section", "tensor", None),
            P("section", None),
            P("section", None, None),
            P("section", None, None),
            P("section", None, "tensor"),
            P("section", "tensor"),
            P("section", "tensor", None),
            P("section", None),
        ),
        check_vma=False,
    )
```

```python
import functools

import jax
import jax.numpy as jnp
from jax import lax
from jax.experimental import pallas as pl
from jax.experimental.pallas import tpu as pltpu
from jax.sharding import PartitionSpec as P

HEAD_DIM = 64
EPSILON = 1e-06
BIG_NEGATIVE = -1e30
MIB = 1024 * 1024
EXTRA_ROWS = 16
GAIN, SHIFT, OUT_BIAS, UP_BIAS, DOWN_BIAS, QV_OWN, QV_FAR, TABLE_ROWS = 0, 2, 4, 5, 6, 7, 9, 16
SQRT_HALF = 0.7071067811865476
INV_SQRT_TAU = 0.3989422804014327

f32 = jnp.float32
bf16 = jnp.bfloat16


def dot_nn(left, right):
    return lax.dot_general(left, right, (((1,), (0,)), ((), ())), preferred_element_type=f32)


def dot_nt(left, right):
    return lax.dot_general(left, right, (((1,), (1,)), ((), ())), preferred_element_type=f32)


def dot_tn(left, right):
    return lax.dot_general(left, right, (((0,), (0,)), ((), ())), preferred_element_type=f32)


def shape(dims, kind):
    return jax.ShapeDtypeStruct(dims, kind)


def run(kernel, outs, args, us, name, mib=16, after=(), grid=None, in_specs=None, out_specs=None,
        scalars=0, aliases=None):
    count = len(args)
    if in_specs is None:
        in_specs = [pl.BlockSpec(memory_space=pltpu.VMEM)] * count
    if out_specs is None:
        out_specs = [pl.BlockSpec(memory_space=pltpu.VMEM)] * len(outs)
    waits = [pl.BlockSpec(memory_space=pl.ANY)] * len(after)

    def body(*refs):
        kernel(*refs[:count], *refs[count + len(after) :])

    moved = sum(item.size * item.dtype.itemsize for item in (*args, *outs))
    return pl.pallas_call(
        body,
        out_shape=outs,
        grid_spec=pltpu.PrefetchScalarGridSpec(
            num_scalar_prefetch=scalars,
            grid=grid or (),
            in_specs=[*in_specs, *waits],
            out_specs=out_specs,
        ),
        name=name,
        input_output_aliases=aliases or {},
        compiler_params=pltpu.CompilerParams(vmem_limit_bytes=mib * MIB),
        cost_estimate=pl.CostEstimate(
            flops=int(us * 1.15e9), bytes_accessed=moved, transcendentals=0
        ),
    )(*args, *after)


def quarters(ref):
    local = ref.shape[0] // 4
    return [ref[local * number : local * (number + 1)] for number in range(4)]


def heads_forward(entry, w, table, line, same):
    local, length = w[0].shape[0], entry.shape[0] // len(same)
    bias = jnp.transpose(table[line : line + 2, :local])
    query = ((dot_nt(w[0], entry) + bias[:, 0:1]).astype(bf16) * HEAD_DIM**-0.5).astype(bf16)
    key = dot_nt(w[1], entry).astype(bf16)
    value = (dot_nt(w[2], entry) + bias[:, 1:2]).astype(bf16)
    probs, columns = [], []
    for seq, visible in enumerate(same):
        span = slice(length * seq, length * (seq + 1))
        mixed = []
        for start in range(0, local, HEAD_DIM):
            head = slice(start, start + HEAD_DIM)
            scores = jnp.where(visible, dot_tn(key[head, span], query[head, span]), BIG_NEGATIVE)
            weights = jnp.exp(scores - jnp.max(scores, 0, keepdims=True))
            weights = weights * (1.0 / jnp.sum(weights, 0, keepdims=True))
            probs.append(weights.astype(bf16))
            mixed.append(dot_nn(value[head, span], probs[-1]).astype(bf16))
        columns.append(jnp.concatenate(mixed, 0))
    return query, key, value, probs, jnp.concatenate(columns, 1)


def heads_backward(query, key, value, probs, grad_mixed):
    heads = query.shape[0] // HEAD_DIM
    length = probs[0].shape[0]
    columns = []
    for seq in range(len(probs) // heads):
        span = slice(length * seq, length * (seq + 1))
        rows = [], [], []
        for number in range(heads):
            head = slice(HEAD_DIM * number, HEAD_DIM * (number + 1))
            low = probs[heads * seq + number]
            q, k, v, upstream = (item[head, span] for item in (query, key, value, grad_mixed))
            wide = low.astype(f32)
            grads = wide * dot_tn(v, upstream)
            grads = (grads - wide * jnp.sum(grads, 0, keepdims=True)).astype(bf16)
            rows[0].append((dot_nn(k, grads) * HEAD_DIM**-0.5).astype(bf16))
            rows[1].append(dot_nt(q, grads).astype(bf16))
            rows[2].append(dot_nt(upstream, low).astype(bf16))
        columns.append([jnp.concatenate(item, 0) for item in rows])
    return [jnp.concatenate(pair, 1) for pair in zip(*columns)]


def attend_own_kernel(own, other, w_own, table, seg_row, seg_col, total):
    rows = jnp.concatenate([own[...], other[...]], 0)
    *w, out = quarters(w_own)
    mixed = heads_forward(rows, w, table, QV_OWN, [seg_col[...] == seg_row[...]])[-1]
    total[...] = dot_tn(mixed, out)


def attend_kernel(early, own, other, w_own, w_far, table, seg_row, seg_col, *outs):
    keep, send = outs[:2]
    rows = jnp.concatenate([own[...], other[...]], 0)
    same = seg_col[...] == seg_row[...]
    total = w_own[...] if early else None
    for group, ref in enumerate((w_own, w_far)):
        if early and group == 0:
            continue
        *w, out = quarters(ref)
        *parts, probs, mixed = heads_forward(rows, w, table, QV_OWN + 2 * group, [same])
        if len(outs) > 2:
            for number, item in enumerate(parts):
                outs[2][group, number, : out.shape[0]] = item
            for number, item in enumerate(probs):
                outs[2][group, number, out.shape[0] :] = item
        term = dot_tn(mixed, out)
        total = term if total is None else total + term
    half = own.shape[0]
    keep[...] = own[...].astype(f32) + (total[:half] + table[OUT_BIAS : OUT_BIAS + 1])
    send[...] = total[half:].astype(bf16)


def attend_back_kernel(own, other, w_own, w_far, kept, residual, keep, send):
    half = own.shape[0] - EXTRA_ROWS
    rows = jnp.concatenate([own[:half], other[:half]], 0)
    total = None
    for group, ref in enumerate((w_own, w_far)):
        *w, out = quarters(ref)
        local = out.shape[0]
        grad_mixed = dot_nt(out, rows).astype(bf16)
        lines = [kept[group, number, :local] for number in range(3)]
        probs = [kept[group, number, local:] for number in range(3)]
        parts = heads_backward(*lines, probs, grad_mixed)
        for number, part in enumerate(parts):
            term = dot_tn(part, w[number])
            total = term if total is None else total + term
    keep[...] = total[:half] + residual[...]
    send[...] = total[half:].astype(bf16)


def standard(values):
    centred = values - jnp.mean(values, -1, keepdims=True)
    spread = lax.rsqrt(jnp.mean(centred * centred, -1, keepdims=True) + EPSILON)
    return centred * spread, spread


def norm_kernel(which, arrived, kept, table, *outs):
    summed = arrived[...].astype(f32) + kept[...]
    gain, shift = table[GAIN + which : GAIN + which + 1], table[SHIFT + which : SHIFT + which + 1]
    outs[0][...] = (standard(summed)[0] * gain + shift).astype(bf16)
    if len(outs) > 1:
        outs[1][...] = summed


def norm_grads(values, gain, upstream):
    normal, spread = standard(values)
    scaled = upstream * gain
    along = jnp.mean(scaled * normal, -1, keepdims=True)
    grad = (scaled - jnp.mean(scaled, -1, keepdims=True) - normal * along) * spread
    return grad, jnp.sum(upstream * normal, 0, keepdims=True), jnp.sum(upstream, 0, keepdims=True)


def norm_back_kernel(upstream, values, table, grad, low, gain_bias):
    result, grad_gain, grad_shift = norm_grads(
        values[...], table[GAIN + 1 : GAIN + 2], upstream[...].astype(f32)
    )
    grad[...] = result
    low[...] = result.astype(bf16)
    gain_bias[0:1] = grad_gain
    gain_bias[1:2] = grad_shift


def norm_back_sum_kernel(arrived, kept, values, table, others, grad, low):
    upstream = arrived[...].astype(f32) + kept[...]
    result, grad_gain, grad_shift = norm_grads(values[...], table[GAIN : GAIN + 1], upstream)
    rows = result.shape[0]
    grad[...] = result
    low[0:rows] = result.astype(bf16)
    small = jnp.concatenate([grad_gain, grad_shift, others[0:2]], 0)
    high = small.astype(bf16)
    rest = (small - high.astype(f32)).astype(bf16)
    blank = jnp.zeros((EXTRA_ROWS - 8, result.shape[1]), bf16)
    low[rows : rows + EXTRA_ROWS] = jnp.concatenate([high, rest, blank], 0)


def feed_kernel(one, two, three, four, weights, table, keep, send, *saved):
    part = one.shape[0]
    rows = jnp.concatenate([one[...], two[...], three[...], four[...]], 0)
    hidden = dot_nn(rows, weights[0]) + table[UP_BIAS : UP_BIAS + 1]
    phi = 0.5 * (1.0 + lax.erf(hidden * SQRT_HALF))
    if saved:
        slope = phi + hidden * (jnp.exp(-0.5 * hidden * hidden) * INV_SQRT_TAU)
        saved[0][...] = slope.astype(bf16)
    total = dot_nn((hidden * phi).astype(bf16), weights[1])
    keep[:part] = one[...].astype(f32) + (total[:part] + table[DOWN_BIAS : DOWN_BIAS + 1])
    keep[part:] = total[part : 2 * part]
    send[...] = total[2 * part :].astype(bf16)


def feed_back_kernel(one, two, three, four, slope, weights, residual, keep, send):
    part = one.shape[0]
    rows = jnp.concatenate([one[...], two[...], three[...], four[...]], 0)
    hidden = (dot_nt(rows, weights[1]) * slope[...].astype(f32)).astype(bf16)
    total = dot_nt(hidden, weights[0])
    keep[:part] = total[:part] + residual[...]
    keep[part:] = total[part : 2 * part]
    send[...] = total[2 * part :].astype(bf16)


def halves_kernel(arrived, kept, keep, send):
    part = keep.shape[0]
    total = arrived[...].astype(f32) + kept[...]
    keep[...] = total[:part]
    send[...] = total[part:].astype(bf16)


def entry_grad_kernel(arrived, kept, low):
    low[...] = (arrived[...].astype(f32) + kept[...]).astype(bf16)


def copy_kernel(source, target):
    target[...] = source[...]


def pair_kernel(*refs):
    for number, ref in enumerate(refs[:-1]):
        refs[-1][number] = ref[...]


def attend_group_kernel(one, two, three, four, w_own, table, seg_row, seg_col, lines, kept):
    entry = jnp.concatenate([one[...], two[...], three[...], four[...]], 0)
    same = [seg_col[seq] == seg_row[seq] for seq in range(2)]
    *parts, probs, mixed = heads_forward(entry, quarters(w_own)[:3], table, QV_OWN, same)
    for number, item in enumerate((*parts, mixed)):
        lines[number] = item
    for number, item in enumerate(probs):
        kept[number] = item


def unpack_kernel(total, tail, g_w, g_out, g_b, g_out_b, g_gain, g_shift):
    step = pl.program_id(0)

    @pl.when(step < 3)
    def _():
        g_w[0] = total[...].astype(f32)

    @pl.when(step == 3)
    def _():
        g_out[...] = total[...].astype(f32)
        rest = tail[...].astype(f32)
        rest = rest[:7] + rest[7:14]
        g_b[...] = rest[:2, : g_b.shape[1]]
        g_out_b[...] = rest[2:3]
        g_gain[...] = jnp.concatenate([rest[3:4], rest[5:6]], 0)
        g_shift[...] = jnp.concatenate([rest[4:5], rest[6:7]], 0)


def attend_grads_kernel(*refs):
    lines, kept, w_own, total = refs[8:]
    out = quarters(w_own)[3]
    entry = jnp.concatenate([item[...] for item in refs[:4]], 0)
    pieces = [item[...] for item in refs[4:8]]
    part = refs[0].shape[0]
    local = out.shape[0]
    query, key, value, mixed = (lines[number] for number in range(4))
    probs = [kept[number] for number in range(kept.shape[0])]
    branch = jnp.concatenate([item[:part] for item in pieces], 0)
    grad_mixed = dot_nt(out, branch).astype(bf16)
    parts = heads_backward(query, key, value, probs, grad_mixed)
    for number, item in enumerate(parts):
        total[local * number : local * (number + 1)] = dot_nn(item, entry).astype(bf16)
    total[3 * local : 4 * local] = dot_nn(mixed, branch).astype(bf16)
    ones = jnp.ones((8, entry.shape[0]), bf16)
    blank = jnp.zeros((2, entry.shape[1] - local), f32)
    sums = jnp.concatenate([dot_nt(ones, parts[0])[:1], dot_nt(ones, parts[2])[:1]], 0)
    small = sum(item[part:].astype(f32) for item in pieces)
    sums = [jnp.concatenate([sums, blank], 1), dot_nn(ones, branch)[:1], small[:4] + small[4:8]]
    sums = jnp.concatenate(sums, 0)
    high = sums.astype(bf16)
    rest = (sums - high.astype(f32)).astype(bf16)
    blank = jnp.zeros((EXTRA_ROWS - 14, sums.shape[1]), bf16)
    total[4 * local : 4 * local + EXTRA_ROWS] = jnp.concatenate([high, rest, blank], 0)


def feed_grads_kernel(*refs):
    weights, table, g_up, g_up_b, g_down, g_down_b = refs[4:]

    @pl.when(pl.program_id(0) == 0)
    def _():
        g_up[...] = jnp.zeros_like(g_up)
        g_up_b[...] = jnp.zeros_like(g_up_b)
        g_down[...] = jnp.zeros_like(g_down)
        g_down_b[...] = jnp.zeros_like(g_down_b)

    first, grad = (jnp.concatenate([refs[i][...], refs[i + 2][...]], 0) for i in range(2))
    hidden = dot_nn(first, weights[0]) + table[UP_BIAS : UP_BIAS + 1]
    phi = 0.5 * (1.0 + lax.erf(hidden * SQRT_HALF))
    slope = phi + hidden * (jnp.exp(-0.5 * hidden * hidden) * INV_SQRT_TAU)
    act = (hidden * phi).astype(bf16)
    grad_hidden = (dot_nt(grad, weights[1]) * slope).astype(bf16)
    g_down[...] += dot_tn(act, grad)
    g_up[...] += dot_tn(first, grad_hidden)
    g_up_b[...] += jnp.sum(grad_hidden.astype(f32), 0, keepdims=True)
    g_down_b[...] += jnp.sum(grad.astype(f32), 0, keepdims=True)


def whole(item):
    return pl.BlockSpec(item.shape, lambda step: (0,) * len(item.shape))


def leading(item, count):
    rest = len(item.shape) - 1
    return pl.BlockSpec((count,) + item.shape[1:], lambda step: (step,) + (0,) * rest)


def shards(
    block_input,
    segments,
    out_grad,
    query_key_value_weight,
    b_qv,
    attention_output_weight,
    attention_out_bias,
    ln_gain,
    ln_bias,
    up_projection_weight,
    up_proj_bias,
    down_projection_weight,
    down_proj_bias,
):
    assert lax.axis_size("tensor") == 4 and block_input.shape[0] == 2
    groups = lax.axis_size("dp")
    section = lax.axis_index("section")
    place = lax.axis_index("tensor")
    a, b = place // 2, place % 2
    seqs, quarter, width = block_input.shape
    length = segments.shape[1]
    part = length // 2
    local = query_key_value_weight.shape[3]
    hidden_local = up_projection_weight.shape[2]
    heads = local // HEAD_DIM

    beside = [(i, i ^ 1) for i in range(4)]
    across = [(i, i ^ 2) for i in range(4)]
    turn = [(2 * s + c, 2 * c + s) for s in range(2) for c in range(2)]
    twist = [(2 * s + c, 2 * c + 1 - s) for s in range(2) for c in range(2)]
    untwist = [(target, source) for source, target in twist]

    def swap(value, pairs):
        return lax.ppermute(value, "tensor", pairs)

    def pieces_of(block):
        one = swap(jnp.where(b == 0, block[0], block[1]), turn)
        two = swap(jnp.where(b == 0, block[1], block[0]), untwist)
        return jnp.where(a == 0, jnp.concatenate([one, two]), jnp.concatenate([two, one]))

    def blocks_of(piece):
        one = swap(jnp.where(a == 0, piece[:quarter], piece[quarter:]), turn)
        two = swap(jnp.where(a == 0, piece[quarter:], piece[:quarter]), twist)
        return jnp.where(b == 0, jnp.stack([one, two]), jnp.stack([two, one]))

    w_own = jnp.transpose(query_key_value_weight[0], (1, 2, 0)).reshape(3 * local, width)
    w_own = jnp.concatenate([w_own, attention_output_weight[0]])
    entry_input = pieces_of(block_input)
    w_far = swap(w_own, across)
    cotangent = pieces_of(out_grad)
    weights = jnp.concatenate([up_projection_weight, down_projection_weight])

    def lines(item):
        return jnp.pad(item, ((0, 0), (0, width - item.shape[1])))

    b_own = lines(b_qv[0])
    table = [ln_gain[0], ln_bias[0], attention_out_bias, lines(up_proj_bias), down_proj_bias]
    table += [b_own, swap(b_own, across)]
    table = jnp.concatenate(table).astype(f32)
    table = jnp.pad(table, ((0, TABLE_ROWS - table.shape[0]), (0, 0)))

    seg_own = segments[0] if seqs == 1 else jnp.where(a == 0, segments[0], segments[1])
    seg_own = seg_own.astype(f32)
    seg_turned = jnp.where(b == 0, seg_own, jnp.roll(seg_own, part))
    seg_row, seg_col = seg_turned[None, :], seg_turned[:, None]
    seg_far = jnp.where(a == 0, segments[1], segments[0]).astype(f32)
    seg_far = jnp.where(b == 0, seg_far, jnp.roll(seg_far, part))
    seg_both = jnp.stack([seg_turned, seg_far])

    piece_f, piece_h = shape((part, width), f32), shape((part, width), bf16)
    pair_f, pair_h = shape((2 * part, width), f32), shape((2 * part, width), bf16)

    def forward(entry, save, before=(), after=()):
        outs = [piece_f, piece_h]
        if save:
            outs.append(shape((2, 3, local + length, length), bf16))
        near, first_part = swap(entry, beside), w_own
        if not save:
            args = (entry, near, w_own, table, seg_row, seg_col)
            first_part = run(attend_own_kernel, [pair_f], args, 2.0, "attend_own")[0]
        args = (entry, near, first_part, w_far, table, seg_row, seg_col)
        keep, branch, *kept = run(
            functools.partial(attend_kernel, not save), outs, args, 3.0, "attend", after=before
        )
        args = (swap(branch, beside), keep, table)
        first, *first_res = run(
            functools.partial(norm_kernel, 0),
            [piece_h] + [piece_f] * save,
            args,
            0,
            "first_norm",
            after=after,
        )
        far = swap(first, across)
        near, far_near = swap(first, beside), swap(far, beside)
        outs = [pair_f, pair_h] + [shape((4 * part, hidden_local), bf16)] * save
        args = (first, far, near, far_near, weights, table)
        keep, send, *slope = run(feed_kernel, outs, args, 1.6, "feed")
        keep, send = run(halves_kernel, [piece_f, piece_h], (swap(send, beside), keep), 0, "halves")
        args = (swap(send, across), keep, table)
        output, *second_res = run(
            functools.partial(norm_kernel, 1),
            [piece_h] + [piece_f] * save,
            args,
            0,
            "second_norm",
        )
        if not save:
            return output
        return output, (kept, first_res[0], slope[0], second_res[0]), (first, far), branch

    def backward(upstream, saved, after=(), later=()):
        kept, first_res, slope, second_res = saved
        grad_second, grad_y, gain_bias = run(
            norm_back_kernel,
            [piece_f, piece_h, shape((2, width), f32)],
            (upstream, second_res, table),
            0,
            "second_norm_back",
            after=after,
        )
        far = swap(grad_y, across)
        near, far_near = swap(grad_y, beside), swap(far, beside)
        args = (grad_y, far, near, far_near, slope, weights, grad_second)
        keep, gate = run(feed_back_kernel, [pair_f, pair_h], args, 1.5, "feed_back")
        keep, send = run(halves_kernel, [piece_f, piece_h], (swap(gate, beside), keep), 0, "halves")
        args = (swap(send, across), keep, first_res, table, gain_bias)
        outs = [piece_f, shape((part + EXTRA_ROWS, width), bf16)]
        grad_first, branch = run(norm_back_sum_kernel, outs, args, 0, "first_norm_back")
        near = swap(branch, beside)

        args = (branch, near, w_own, w_far, *kept, grad_first)
        keep, send = run(attend_back_kernel, [piece_f, piece_h], args, 3.2, "attend_back", after=later)
        args = (swap(send, beside), keep)
        grad_entry = run(entry_grad_kernel, [piece_h], args, 0, "entry_grad")[0]
        return grad_entry, (grad_y, far), branch, near, send

    wide = groups in (2, 4)
    count = groups if wide else 1

    def gather(pair):
        mine = lax.all_gather(pair, "dp") if wide else pair[None]
        return mine, swap(mine, beside)

    sections = [(0, 1), (1, 0)]
    middle = lax.ppermute(forward(entry_input, False), "section", sections)
    entry = jnp.where(section == 0, entry_input, middle)
    entry_far = swap(entry, across)
    output, saved, first_pair, _ = forward(entry, True, (cotangent,), (entry_far,))

    entries = (entry, swap(entry, beside), entry_far, swap(entry_far, beside))

    firsts = [item.reshape(-1, width) for item in gather(jnp.stack(first_pair))]
    grad = backward(cotangent, saved)[0]
    layer_output = blocks_of(output)
    args = (*entries, w_own, table, seg_both[:, None, :], seg_both[:, :, None])
    outs = [shape((4, local, 2 * length), bf16), shape((2 * heads, length, length), bf16)]
    attended = run(attend_group_kernel, outs, args, 4.0, "attend_group", mib=24, after=(firsts[0],))
    middle = lax.ppermute(grad, "section", sections)
    grad_entry, grad_y, branch, near, token = backward(
        jnp.where(section == 1, cotangent, middle), saved, (layer_output, attended[0])
    )
    outs = [shape((2, part, width), bf16)]
    grad_y = run(pair_kernel, outs, grad_y, 0, "grad_y_pair")[0]
    grad_y = lax.all_gather(grad_y, "dp") if wide else grad_y[None]

    far = run(copy_kernel, [shape(branch.shape, bf16)], (swap(branch, across),), 0, "far", after=(token,))[0]
    total = run(
        attend_grads_kernel,
        [shape((4 * local + EXTRA_ROWS, width), bf16)],
        (*entries, branch, near, far, swap(far, beside), *attended, w_own),
        5.0,
        "attend_grads",
        mib=24,
    )[0]
    local_total = total
    grad_y, local_total = lax.optimization_barrier((grad_y, local_total))
    total = lax.psum(local_total, "dp")
    grads_y = [item.reshape(-1, width) for item in (grad_y, swap(grad_y, beside))]
    args = (firsts[0], grads_y[0], firsts[1], grads_y[1], weights, table)
    outs = [
        shape((width, hidden_local), f32),
        shape((1, hidden_local), f32),
        shape((hidden_local, width), f32),
        shape((1, width), f32),
    ]
    block, tall = 2 * part, firsts[0].shape[0]
    g_up, g_up_b, g_down, g_down_b = run(
        feed_grads_kernel,
        outs,
        args,
        5.0,
        "feed_grads",
        mib=56,
        grid=(tall // block,),
        in_specs=[leading(item, block) for item in args[:4]] + [whole(item) for item in args[4:]],
        out_specs=[whole(item) for item in outs],
    )
    held = run(copy_kernel, [piece_h], (grad_entry,), 0, "held", after=(g_down,))[0]
    input_grad = blocks_of(held)
    if not wide:
        g_up, g_up_b, g_down = [
            lax.psum(item.astype(bf16), "dp").astype(f32) for item in (g_up, g_up_b, g_down)
        ]
        g_down_b = lax.psum(g_down_b, "dp")
    outs = [shape((3, local, width), f32), shape((local, width), f32), shape((2, local), f32)]
    outs += [shape((1, width), f32), shape((2, width), f32), shape((2, width), f32)]
    after = (g_down, input_grad)
    g_w, g_out, g_b, g_out_b, g_gain, g_shift = run(
        unpack_kernel,
        outs,
        (total, total),
        1.0,
        "unpack",
        mib=56,
        after=after,
        grid=(4,),
        in_specs=[
            pl.BlockSpec((local, width), lambda i: (i, 0)),
            pl.BlockSpec((EXTRA_ROWS, width), lambda i: (4 * local // EXTRA_ROWS, 0)),
        ],
        out_specs=[pl.BlockSpec((1, local, width), lambda i: (jnp.minimum(i, 2), 0, 0))]
        + [whole(item) for item in outs[1:]],
    )
    return (
        layer_output[None],
        input_grad[None],
        jnp.transpose(g_w, (2, 0, 1))[None],
        g_b[None],
        g_out[None],
        g_out_b,
        g_gain[None],
        g_shift[None],
        g_up[None],
        g_up_b,
        g_down[None],
        g_down_b,
    )


def solution(mesh):
    return jax.shard_map(
        shards,
        mesh=mesh,
        in_specs=(
            P("dp", "tensor", None),
            P("dp", None),
            P("dp", "tensor", None),
            P("section", None, None, "tensor"),
            P("section", None, "tensor"),
            P("section", "tensor", None),
            P("section", None),
            P("section", None, None),
            P("section", None, None),
            P("section", None, "tensor"),
            P("section", "tensor"),
            P("section", "tensor", None),
            P("section", None),
        ),
        out_specs=(
            P("section", "dp", "tensor", None),
            P("section", "dp", "tensor", None),
            P("section", None, None, "tensor"),
            P("section", None, "tensor"),
            P("section", "tensor", None),
            P("section", None),
            P("section", None, None),
            P("section", None, None),
            P("section", None, "tensor"),
            P("section", "tensor"),
            P("section", "tensor", None),
            P("section", None),
        ),
        check_vma=False,
    )
```
